32 devices in a mesh: parts: 2 (over y), tile: 4 (over z), tm: 2 (over x), layer: 2 (over core).
Axes of the slice: x: 2, y: 2, z: 4, core: 2. Of those that a mesh axis runs over, the one named last changes fastest.
Arguments:
- u_start: float32 [4, 8, 64, 256], P(('parts', 'tm'), 'layer', 'tile'), parts along dimension 0, may hold values from -4 to 4
- flux: float32 [4, 64, 256], P(('parts', 'tm'), 'tile'), parts along dimension 0, may hold values from 0.003 to 0.03
- zone_of_cell: int32 [8, 64, 256], P('layer', 'tile'), may hold values from 0 to 15
- zone_row: int32 [16], replicated, may hold values from 0 to 7
- plane_rate: float32 [8], replicated, may hold values from 0.015 to 0.07
- thick_rate: float32 [8], replicated, may hold values from 0.02 to 0.1
- soften: float32 [8], replicated, may hold values from 0.05 to 0.15
Outputs:
- u_next: float32 [4, 8, 64, 256], P(('parts', 'tm'), 'layer', 'tile'), parts along dimension 0
The draws below stay inside these ranges and needn't reach their ends.
There are 2 independent parts, one for each index of `parts`. The reference program is written for one: setup_inputs(seed, part) draws one part's arguments, and reference() takes and returns one part's arrays. A program takes and returns all parts, laid end to end along the dimension named above; an argument that names none is the same for every part. Nothing has to cross between parts.
All inputs are finite; a program needn't handle non-finite values.
Results may differ from the reference program's by a relative error of at most 0.0001.
Values sent between devices are 32-bit elements; how exact they have to be, the bound alone decides.
No kernel may reach another device: no remote copies, remote signals or barrier semaphores. Data moves between devices by JAX's collectives and lax.ppermute only.
A program may use at most 64 MiB of HBM per device.

```python
import math
import jax
import jax.numpy as jnp

NY = 256
ZONES = 16
ROWS = 8
FINE_STEPS = 8
COARSE_STEPS = 2
NX = 64
NZ = 8
SLICES = 2


def with_ends(entries, key, low, high):
    spot = [jax.random.randint(jax.random.fold_in(key, axis), (), 0, length) for axis, length in enumerate(entries.shape)]
    longest = entries.shape.index(max(entries.shape))
    neighbour = spot[:longest] + [(spot[longest] + 1) % entries.shape[longest]] + spot[longest + 1:]
    return entries.at[tuple(spot)].set(low).at[tuple(neighbour)].set(high)


def shard_levels(own_key, extent, split, least, top_value):
    loudness, own = 1.0, jax.random.fold_in(own_key, 6)
    for axis_at, parts in split:
        draws = jnp.exp(jax.random.uniform(jax.random.fold_in(own, axis_at), (parts,), jnp.float32, least / len(split), top_value / len(split)))
        loudness = loudness * jnp.repeat(draws, extent[axis_at] // parts).reshape([-1 if axis == axis_at else 1 for axis in range(len(extent))])
    return loudness


def gaussian(stream_key, dims, spread, reach, split=(), kind=jnp.bfloat16):
    values = spread * jax.random.normal(stream_key, dims, jnp.float32)
    if split:
        values = values * shard_levels(stream_key, dims, split, -0.22, 0.18)
    return jnp.clip(values, -reach, reach).astype(kind)


def setup_inputs(seed: int = 0, part: int = 0) -> dict:
    splits = jax.random.split(jax.random.key(seed), 8)
    part_keys = jax.random.split(jax.random.fold_in(splits[7], part), 8)
    return {
        "u_start": gaussian(part_keys[0], (SLICES, NZ, NX, NY), 1.0, 4.0, ((0, 2), (1, 2), (2, 4)), jnp.float32),
        "flux": jnp.clip(jnp.exp(math.log(0.03) - 2.3025851 * jax.random.uniform(part_keys[1], (SLICES, NX, NY), jnp.float32) ** shard_levels(part_keys[1], (SLICES, NX, NY), ((0, 2), (1, 4)), -0.2, 0.2)), 0.003, 0.03),
        "zone_of_cell": with_ends(jax.random.randint(splits[2], (NZ, NX, NY), 0, ZONES), jax.random.fold_in(splits[2], 1), 0, ZONES - 1).astype(jnp.int32),
        "zone_row": with_ends(jax.random.randint(splits[3], (ZONES,), 0, ROWS), jax.random.fold_in(splits[3], 1), 0, ROWS - 1).astype(jnp.int32),
        "plane_rate": jnp.clip(jnp.exp(jax.random.uniform(splits[4], (ROWS,), jnp.float32, math.log(0.015), math.log(0.07))), 0.015, 0.07),
        "thick_rate": jnp.clip(jnp.exp(jax.random.uniform(splits[5], (ROWS,), jnp.float32, math.log(0.02), math.log(0.1))), 0.02, 0.1),
        "soften": jnp.clip(jax.random.uniform(splits[6], (ROWS,), jnp.float32, 0.05, 0.15), 0.05, 0.15),
    }


def edge_masks(start, count, total):
    positions = start + jnp.arange(count, dtype=jnp.int32)
    return (positions > 0).astype(jnp.float32), (positions < total - 1).astype(jnp.float32)


def restrict_cells(field):
    depth, width, length = field.shape
    return field.reshape(depth // 2, 2, width // 2, 2, length // 2, 2).mean(axis=(1, 3, 5))


def restrict_surface(field):
    width, length = field.shape
    return field.reshape(width // 2, 2, length // 2, 2).mean(axis=(1, 3))


def prolong_cells(field):
    return jnp.repeat(jnp.repeat(jnp.repeat(field, 2, axis=0), 2, axis=1), 2, axis=2)


def pad_block(field):
    return jnp.pad(field, ((1, 1), (1, 1), (0, 0)))


def diffuse(padded, plane_pad, thick_pad, soft_pad, z_low, z_high, x_low, x_high, source):
    k_plane = plane_pad * (1.0 + soft_pad * padded)
    k_thick = thick_pad * (1.0 + soft_pad * padded)
    center = padded[1:-1, 1:-1]
    c_plane = k_plane[1:-1, 1:-1]
    c_thick = k_thick[1:-1, 1:-1]
    gain = 0.5 * (c_thick + k_thick[:-2, 1:-1]) * (padded[:-2, 1:-1] - center) * z_low[:, None, None]
    gain = gain + 0.5 * (c_thick + k_thick[2:, 1:-1]) * (padded[2:, 1:-1] - center) * z_high[:, None, None]
    gain = gain + 0.5 * (c_plane + k_plane[1:-1, :-2]) * (padded[1:-1, :-2] - center) * x_low[None, :, None]
    gain = gain + 0.5 * (c_plane + k_plane[1:-1, 2:]) * (padded[1:-1, 2:] - center) * x_high[None, :, None]
    flow = 0.5 * (c_plane[..., 1:] + c_plane[..., :-1]) * (center[..., 1:] - center[..., :-1])
    zeros_col = jnp.zeros(center.shape[:2] + (1,), jnp.float32)
    gain = gain + jnp.concatenate([flow, zeros_col], axis=-1) - jnp.concatenate([zeros_col, flow], axis=-1)
    return center + gain + source


def reference(u_start, flux, zone_of_cell, zone_row, plane_rate, thick_rate, soften):
    table_row = zone_row[zone_of_cell]
    cell_plane = plane_rate[table_row]
    cell_thick = thick_rate[table_row]
    cell_soft = soften[table_row]
    depth, width, length = zone_of_cell.shape
    z_low, z_high = edge_masks(0, depth, depth)
    x_low, x_high = edge_masks(0, width, width)
    top_layer = (jnp.arange(depth, dtype=jnp.int32) == 0).astype(jnp.float32)[:, None, None]
    plane_pad = pad_block(cell_plane)
    thick_pad = pad_block(cell_thick)
    soft_pad = pad_block(cell_soft)
    coarse_plane = pad_block(restrict_cells(cell_plane))
    coarse_thick = pad_block(restrict_cells(cell_thick))
    coarse_soft = pad_block(restrict_cells(cell_soft))
    cz_low, cz_high = edge_masks(0, depth // 2, depth // 2)
    cx_low, cx_high = edge_masks(0, width // 2, width // 2)
    coarse_top = (jnp.arange(depth // 2, dtype=jnp.int32) == 0).astype(jnp.float32)[:, None, None]

    def fine_prop(state, heat_flux):
        source = top_layer * heat_flux[None]
        for step_index in range(FINE_STEPS):
            state = diffuse(pad_block(state), plane_pad, thick_pad, soft_pad, z_low, z_high, x_low, x_high, source)
        return state

    def coarse_prop(state, heat_flux):
        source = 2.0 * coarse_top * restrict_surface(heat_flux)[None]
        for step_index in range(COARSE_STEPS):
            state = diffuse(pad_block(state), coarse_plane, coarse_thick, coarse_soft, cz_low, cz_high, cx_low, cx_high, source)
        return state

    results = []
    current = u_start[0]
    for slice_index in range(SLICES):
        correction = fine_prop(u_start[slice_index], flux[slice_index]) - prolong_cells(coarse_prop(restrict_cells(u_start[slice_index]), flux[slice_index]))
        advanced = prolong_cells(coarse_prop(restrict_cells(current), flux[slice_index])) + correction
        results.append(advanced)
        current = advanced
    return jnp.stack(results)
```

```python
import functools

import jax
import jax.numpy as jnp
from jax import lax
from jax.experimental import pallas as pl
from jax.experimental.pallas import tpu as pltpu
from jax.sharding import PartitionSpec as P

FINE_STEPS = 8
COARSE_STEPS = 2
LANES = 128
EDGE = 2 * COARSE_STEPS
HALO = FINE_STEPS + EDGE
VMEM_BYTES = 16 * 2**20
VMEM = pl.BlockSpec(memory_space=pltpu.VMEM)


def iota(shape, dim):
    return lax.broadcasted_iota(jnp.int32, shape, dim)


def pick(table, index):
    return jnp.take_along_axis(table, index, axis=1, mode="promise_in_bounds")


def split_lanes(row):
    rows = row.shape[0]
    lane = iota((rows, LANES), 1)
    low = lane < LANES // 2
    even = (2 * lane) % LANES
    first, second = row[:, :LANES], row[:, LANES:]
    return jnp.concatenate(
        [
            jnp.where(low, pick(first, even), pick(second, even)),
            jnp.where(low, pick(first, even + 1), pick(second, even + 1)),
        ],
        axis=1,
    )


def join_lanes(row):
    rows = row.shape[0]
    lane = iota((rows, LANES), 1)
    is_even = lane % 2 == 0
    half = lane // 2
    even, odd = row[:, :LANES], row[:, LANES:]
    return jnp.concatenate(
        [
            jnp.where(is_even, pick(even, half), pick(odd, half)),
            jnp.where(is_even, pick(even, half + LANES // 2), pick(odd, half + LANES // 2)),
        ],
        axis=1,
    )


def prepare_kernel(u_ref, u_other, zone_ref, zone_other, flux_ref, local_ref, send_ref):
    width = u_ref.shape[1]
    core = lax.axis_index("layer")

    def fill(order, mirror):
        for i in range(width):
            row = width - 1 - i if mirror else i
            for at, pair in ((0, (u_ref, u_other)), (width, (zone_ref, zone_other))):
                low, high = (pair[k] for k in order)
                slab = jnp.concatenate([low[:, row, :], high[:, row, :]], axis=0)
                slab = split_lanes(slab.astype(jnp.float32))
                local_ref[at + i] = slab
                if i < HALO:
                    send_ref[(HALO if at else 0) + i] = slab
        flux = split_lanes(flux_ref[...])
        for i in range(width):
            row = width - 1 - i if mirror else i
            local_ref[2 * width + i // 8, i % 8 : i % 8 + 1, :] = flux[row : row + 1]
            send_ref[2 * HALO + i // 8, i % 8 : i % 8 + 1, :] = flux[row : row + 1]

    pl.when(core == 0)(lambda: fill((0, 1), False))
    pl.when(core == 1)(lambda: fill((1, 0), True))


def pair_sum(value):
    layers = value.shape[0]
    even = iota(value.shape, 0) % 2 == 0
    return value + jnp.where(even, pltpu.roll(value, layers - 1, 0), pltpu.roll(value, 1, 0))


def halves(value):
    return value[:, :LANES] + value[:, LANES:]


def step_row(v, low, high, k_plane, k_thick, source, y_flow, layer_gap):
    layers = v.shape[0]
    inside = iota(v.shape, 0) < layers - layer_gap
    shift = layers - layer_gap
    up_v, up_k = pltpu.roll(v, shift, 0), pltpu.roll(k_thick, shift, 0)
    flow = jnp.where(inside, (k_thick + up_k) * (up_v - v), 0.0)
    return v + source + (high - low) + y_flow(v, k_plane) + (flow - pltpu.roll(flow, layer_gap, 0))


def fine_y(v, k):
    va, vb, ka, kb = v[:, :LANES], v[:, LANES:], k[:, :LANES], k[:, LANES:]
    inner = (ka + kb) * (vb - va)
    next_v, next_k = pltpu.roll(va, LANES - 1, 1), pltpu.roll(ka, LANES - 1, 1)
    outer = jnp.where(iota(va.shape, 1) < LANES - 1, (kb + next_k) * (next_v - vb), 0.0)
    return jnp.concatenate([inner - pltpu.roll(outer, 1, 1), outer - inner], axis=1)


def coarse_y(v, k):
    next_v, next_k = pltpu.roll(v, LANES - 1, 1), pltpu.roll(k, LANES - 1, 1)
    flow = jnp.where(iota(v.shape, 1) < LANES - 1, (k + next_k) * (next_v - v), 0.0)
    return flow - pltpu.roll(flow, 1, 1)


def outer_mask(core):
    tile, tiles = lax.axis_index("tile"), lax.axis_size("tile")
    at_edge = jnp.where(core == 0, tile == 0, tile == tiles - 1)
    return jnp.where(at_edge, 0.0, 1.0).astype(jnp.float32)


def propagate_kernel(
    local_ref, recv_ref, table_ref, rest_ref, share_ref, coarse_ref, v_ref, coef_ref, source_ref
):
    rows = v_ref.shape[0]
    width = rows - HALO
    layers = local_ref.shape[1]
    mask = outer_mask(lax.axis_index("layer"))
    tables = [jnp.broadcast_to(table_ref[k : k + 1, :], (layers, LANES)) for k in range(5)]
    top = iota((layers, 2 * LANES), 0) == 0
    top_pair = iota((layers, LANES), 0) < 2

    def flux_row(j):
        ref, at, i = (
            (recv_ref, 2 * HALO, HALO - 1 - j) if j < HALO else (local_ref, 2 * width, j - HALO)
        )
        return ref[at + i // 8, i % 8 : i % 8 + 1, :]

    fields = []
    for j in range(rows):
        if j < HALO:
            v, zone = recv_ref[HALO - 1 - j], recv_ref[2 * HALO - 1 - j]
        else:
            v, zone = local_ref[j - HALO], local_ref[width + j - HALO]
        zone = zone.astype(jnp.int32)
        coefs = [
            jnp.concatenate([pick(t, zone[:, :LANES]), pick(t, zone[:, LANES:])], axis=1)
            for t in tables
        ]
        v_ref[j] = v
        for k in range(4):
            coef_ref[k, j] = coefs[k]
        flux = flux_row(j)
        source_ref[j] = jnp.where(top, flux, 0.0)
        if j >= HALO - EDGE:
            here = [halves(x) for x in (coefs[0], coefs[2], coefs[4], v)] + [halves(flux)]
            if j % 2 == 0:
                fields = here
            else:
                at = (j - (HALO - EDGE)) // 2
                for k in range(4):
                    coarse_ref[k, at] = 0.125 * pair_sum(fields[k] + here[k])
                coarse_ref[4, at] = jnp.where(top_pair, 0.5 * (fields[4] + here[4]), 0.0)

    for step in range(1, FINE_STEPS + 1):
        v_next = v_ref[step - 1]
        k_next = coef_ref[0, step - 1] + coef_ref[1, step - 1] * v_next
        high = None
        for j in range(step - 1, rows - step):
            v, k_plane, low = v_next, k_next, high
            v_next = v_ref[j + 1]
            k_next = coef_ref[0, j + 1] + coef_ref[1, j + 1] * v_next
            high = (k_plane + k_next) * (v_next - v)
            if j == HALO - 1:
                high = high * mask
            if j >= step:
                k_thick = coef_ref[2, j] + coef_ref[3, j] * v
                v_ref[j] = step_row(v, low, high, k_plane, k_thick, source_ref[j], fine_y, 1)

    even = iota((layers, LANES), 0) % 2 == 0
    start = HALO - EDGE
    restricted = []
    for j in range(start, HALO + width // 2, 2):
        restricted.append(0.125 * pair_sum(halves(v_ref[j]) + halves(v_ref[j + 1])))
    for i in range(0, len(restricted), 2):
        rest_ref[i // 2] = jnp.where(even, restricted[i], restricted[i + 1])
    for i in range(width // 2):
        share_ref[2 * i] = v_ref[HALO + i][:, :LANES]
        share_ref[2 * i + 1] = v_ref[HALO + i][:, LANES:]
    for k in range(5):
        for i in range(COARSE_STEPS):
            share_ref[width + k * COARSE_STEPS + i] = coarse_ref[k, i]


def coarse_fields(mine_ref, coarse_ref, other_ref, width):
    def row(k, j):
        known = width // 2 + COARSE_STEPS
        if j < known:
            return coarse_ref[k, j]
        return other_ref[width + k * COARSE_STEPS + width // 2 + 2 * COARSE_STEPS - 1 - j]

    return row


def coarse_propagate(state, field, masks):
    count = len(state)
    flux = {j: field(4, j) for j in range(1, count - 1)}
    plane = [field(0, j) for j in range(count)]
    thick = [field(1, j) for j in range(count)]
    soft = [field(2, j) for j in range(count)]
    for step in range(1, COARSE_STEPS + 1):
        k_plane = {
            j: plane[j] * (1.0 + soft[j] * state[j]) for j in range(step - 1, count - step + 1)
        }
        flows = {}
        for j in range(step - 1, count - step):
            flow = (k_plane[j] + k_plane[j + 1]) * (state[j + 1] - state[j])
            flows[j] = flow * masks[j] if j in masks else flow
        fresh = list(state)
        for j in range(step, count - step):
            k_thick = thick[j] * (1.0 + soft[j] * state[j])
            fresh[j] = step_row(
                state[j], flows[j - 1], flows[j], k_plane[j], k_thick, flux[j], coarse_y, 2
            )
        state = fresh
    return state[COARSE_STEPS : count - COARSE_STEPS]


def edge_factors(rows):
    core = lax.axis_index("layer")
    return {
        COARSE_STEPS - 1: outer_mask(core),
        rows - COARSE_STEPS - 1: outer_mask(1 - core),
    }


def expand(slab):
    layers = slab.shape[0]
    even = iota(slab.shape, 0) % 2 == 0
    return [
        jnp.where(even, slab, pltpu.roll(slab, 1, 0)),
        jnp.where(even, pltpu.roll(slab, layers - 1, 0), slab),
    ]


def read_state(state_ref, rows):
    if state_ref.shape[0] == rows:
        return [state_ref[j] for j in range(rows)]
    half = state_ref.shape[0] // 2
    mine = sum((expand(state_ref[i]) for i in range(half)), [])
    other = sum((expand(state_ref[half + i]) for i in range(half)), [])
    return mine + other[::-1]


def output_kernel(state_ref, coarse_ref, share_ref, other_ref, out_ref):
    depth, width = out_ref.shape[1:3]
    core = lax.axis_index("layer")
    rows = width // 2 + 2 * COARSE_STEPS
    field = coarse_fields(share_ref, coarse_ref, other_ref, width)
    masks = edge_factors(rows)
    own = [field(3, j) for j in range(rows)]
    first = lax.axis_index("tm") == 0
    state = [jnp.where(first, a, b) for a, b in zip(own, read_state(state_ref, rows))]
    moved = coarse_propagate(state, field, masks)
    base = coarse_propagate(own, field, masks)

    def write(mirror):
        for j in range(0, width, 2):
            gain = moved[j // 2] - base[j // 2]
            slabs = []
            for i in (j, j + 1):
                ref, at = (share_ref, i) if i < width // 2 else (other_ref, width - 1 - i)
                slab = jnp.concatenate([ref[2 * at] + gain, ref[2 * at + 1] + gain], axis=1)
                slabs.append(slab[depth:] if mirror else slab[:depth])
            both = join_lanes(jnp.concatenate(slabs, axis=0))
            for i in (0, 1):
                row = width - 1 - (j + i) if mirror else j + i
                out_ref[0, :, row, :] = both[depth * i : depth * (i + 1)]

    pl.when(core == 0)(lambda: write(False))
    pl.when(core == 1)(lambda: write(True))


def advance_kernel(state_ref, coarse_ref, share_ref, other_ref, next_ref):
    width = 2 * next_ref.shape[0]
    rows = width // 2 + 2 * COARSE_STEPS
    field = coarse_fields(share_ref, coarse_ref, other_ref, width)
    masks = edge_factors(rows)
    own = [field(3, j) for j in range(rows)]
    first = lax.axis_index("tm") == 0
    state = [jnp.where(first, a, b) for a, b in zip(own, read_state(state_ref, rows))]
    moved = coarse_propagate(state, field, masks)
    base = coarse_propagate(own, field, masks)
    for j in range(width // 2):
        pair = []
        for i in (2 * j, 2 * j + 1):
            ref, at = (share_ref, i) if i < width // 2 else (other_ref, width - 1 - i)
            pair.append(ref[2 * at] + ref[2 * at + 1])
        next_ref[j] = moved[j] - base[j] + 0.125 * pair_sum(pair[0] + pair[1])


def layer_swap(value):
    return lax.ppermute(value, "layer", [(0, 1), (1, 0)])


def swap_pairs(pairs):
    return [edge for a, b in pairs for edge in ((a, b), (b, a))]


def tile_swap(value):
    tiles, slices = lax.axis_size("tile"), lax.axis_size("tm")
    at = lambda tile, time, core: (tile * slices + time) * 2 + core
    pairs = [
        (at(t, m, 0), at(t - 1, m, 1)) for t in range(1, tiles) for m in range(slices)
    ]
    for m in range(0, slices - 1, 2):
        pairs.append((at(0, m, 0), at(0, m + 1, 0)))
        pairs.append((at(tiles - 1, m, 1), at(tiles - 1, m + 1, 1)))
    return lax.ppermute(value, ("tile", "tm", "layer"), swap_pairs(pairs))


def time_swap(value, parity):
    slices = lax.axis_size("tm")
    at = lambda time, core: time * 2 + core
    pairs = [
        (at(m, c), at(m + 1, c)) for m in range(parity, slices - 1, 2) for c in range(2)
    ]
    used = {d for pair in pairs for d in pair}
    pairs += [(at(m, 0), at(m, 1)) for m in range(slices) if at(m, 0) not in used]
    return lax.ppermute(value, ("tm", "layer"), swap_pairs(pairs))


def zone_tables(zone_row, plane_rate, thick_rate, soften):
    table_rows = plane_rate.shape[0]
    hit = (zone_row[:, None] == jnp.arange(table_rows, dtype=jnp.int32)[None, :]).astype(
        jnp.float32
    )
    plane, thick, soft = (
        jnp.sum(hit * rate[None, :], axis=1) for rate in (plane_rate, thick_rate, soften)
    )
    tables = jnp.stack(
        [0.5 * plane, 0.5 * plane * soft, 0.5 * thick, 0.5 * thick * soft, soft]
    )
    return jnp.pad(tables, ((0, 8 - tables.shape[0]), (0, LANES - tables.shape[1])))


def on_device(u_start, flux, zone_of_cell, zone_row, plane_rate, thick_rate, soften):
    depth, width, length = zone_of_cell.shape
    layers = depth * lax.axis_size("layer")
    f32 = jnp.float32
    slabs = lambda *lead: jax.ShapeDtypeStruct((*lead, layers, LANES), f32)
    wide = lambda *lead: jax.ShapeDtypeStruct((*lead, layers, length), f32)
    call = functools.partial(
        pl.pallas_call, compiler_params=pltpu.CompilerParams(vmem_limit_bytes=VMEM_BYTES)
    )
    specs = lambda count: [VMEM] * count

    own = u_start[0]
    tables = zone_tables(zone_row, plane_rate, thick_rate, soften)
    own_other = layer_swap(own)
    zone_other = layer_swap(zone_of_cell)
    flux_slabs = width // 8
    local, send = call(
        prepare_kernel,
        out_shape=(wide(2 * width + flux_slabs), wide(2 * HALO + flux_slabs)),
        in_specs=specs(5),
        out_specs=(VMEM, VMEM),
        name="prepare",
    )(own, own_other, zone_of_cell, zone_other, flux[0])
    recv = tile_swap(send)

    rows = HALO + width
    edge_rows = width // 2 + EDGE
    rest, share, coarse = call(
        propagate_kernel,
        out_shape=(
            slabs(edge_rows // 4),
            slabs(width + 5 * COARSE_STEPS),
            slabs(5, (width + EDGE) // 2),
        ),
        in_specs=specs(3),
        out_specs=(VMEM, VMEM, VMEM),
        scratch_shapes=[
            pltpu.VMEM((rows, layers, length), f32),
            pltpu.VMEM((4, rows, layers, length), f32),
            pltpu.VMEM((rows, layers, length), f32),
        ],
        name="propagate",
    )(local, recv, tables)

    state = jnp.concatenate([rest, layer_swap(rest)], axis=0)
    other = layer_swap(share)
    slices = lax.axis_size("tm")
    position = lax.axis_index("tm")
    for turn in range(slices - 1):
        if turn == 0:
            state = time_swap(state, 0)
            continue
        ended = call(
            advance_kernel,
            out_shape=slabs(width // 2),
            in_specs=specs(4),
            out_specs=VMEM,
            name="advance",
        )(state, coarse, share, other)
        outer = tile_swap(ended[:COARSE_STEPS])
        inner = layer_swap(outer)
        full = jnp.concatenate([outer[::-1], ended, inner], axis=0)
        arrived = time_swap(full, turn % 2)
        if state.shape != full.shape:
            state = call(
                lambda s, o: [o.__setitem__(j, r) for j, r in enumerate(read_state(s, o.shape[0]))]
                and None,
                out_shape=slabs(full.shape[0]),
                in_specs=specs(1),
                out_specs=VMEM,
                name="unfold",
            )(state)
        state = jnp.where(position == turn + 1, arrived, state)
    return call(
        output_kernel,
        out_shape=jax.ShapeDtypeStruct((1, depth, width, length), f32),
        in_specs=specs(4),
        out_specs=VMEM,
        name="output",
    )(state, coarse, share, other)


def solution(mesh):
    return jax.shard_map(
        on_device,
        mesh=mesh,
        in_specs=(
            P(("parts", "tm"), "layer", "tile", None),
            P(("parts", "tm"), "tile", None),
            P("layer", "tile", None),
            P(),
            P(),
            P(),
            P(),
        ),
        out_specs=P(("parts", "tm"), "layer", "tile", None),
        check_vma=False,
    )
```

```python
import jax
import jax.numpy as jnp
from jax import lax
from jax.experimental import pallas as pl
from jax.experimental.pallas import tpu as pltpu
from jax.sharding import PartitionSpec as P

FINE_STEPS = 8
COARSE_STEPS = 2
LANES = 128
EDGE = 2 * COARSE_STEPS
HALO = FINE_STEPS + EDGE
VMEM_BYTES = 16 * 2**20
VMEM = pl.BlockSpec(memory_space=pltpu.VMEM)


def iota(shape, dim):
    return lax.broadcasted_iota(jnp.int32, shape, dim)


def pick(table, index):
    return jnp.take_along_axis(table, index, axis=1, mode="promise_in_bounds")


def split_lanes(row):
    rows = row.shape[0]
    lane = iota((rows, LANES), 1)
    low = lane < LANES // 2
    even = (2 * lane) % LANES
    first, second = row[:, :LANES], row[:, LANES:]
    return jnp.concatenate(
        [
            jnp.where(low, pick(first, even), pick(second, even)),
            jnp.where(low, pick(first, even + 1), pick(second, even + 1)),
        ],
        axis=1,
    )


def join_lanes(row):
    rows = row.shape[0]
    lane = iota((rows, LANES), 1)
    is_even = lane % 2 == 0
    half = lane // 2
    even, odd = row[:, :LANES], row[:, LANES:]
    return jnp.concatenate(
        [
            jnp.where(is_even, pick(even, half), pick(odd, half)),
            jnp.where(is_even, pick(even, half + LANES // 2), pick(odd, half + LANES // 2)),
        ],
        axis=1,
    )


def pack_rows(core, u_ref, zone_ref, head_ref, tail_ref, flux_ref=None):
    depth, width = u_ref.shape[:2]

    def fill(mirror):
        for i in range(width):
            row = width - 1 - i if mirror else i
            slab = jnp.concatenate(
                [u_ref[:, row, :], zone_ref[:, row, :].astype(jnp.float32)], axis=0
            )
            slab = split_lanes(slab)
            if i < HALO:
                head_ref[i] = slab
            else:
                tail_ref[i - HALO] = slab
        if flux_ref is not None:
            flux = split_lanes(flux_ref[...])
            for i in range(width):
                row = width - 1 - i if mirror else i
                head_ref[HALO + i // 8, i % 8 : i % 8 + 1, :] = flux[row : row + 1]

    pl.when(core == 0)(lambda: fill(False))
    pl.when(core == 1)(lambda: fill(True))


def pack_own_kernel(
    u_hbm,
    zone_hbm,
    flux_hbm,
    row_hbm,
    plane_hbm,
    thick_hbm,
    soft_hbm,
    head_ref,
    tail_ref,
    table_ref,
    u_ref,
    zone_ref,
    flux_ref,
    row_ref,
    plane_ref,
    thick_ref,
    soft_ref,
    sems,
):
    sources = (u_hbm, zone_hbm, flux_hbm, row_hbm, plane_hbm, thick_hbm, soft_hbm)
    targets = (u_ref, zone_ref, flux_ref, row_ref, plane_ref, thick_ref, soft_ref)
    copies = [
        pltpu.make_async_copy(source, target, sems.at[k])
        for k, (source, target) in enumerate(zip(sources, targets))
    ]
    for copy in copies:
        copy.start()
    for copy in copies[3:]:
        copy.wait()
    lane = iota(table_ref.shape, 1)
    plane = thick = soft = jnp.zeros(table_ref.shape, jnp.float32)
    for zone in range(row_ref.shape[0]):
        at, here = row_ref[zone], lane == zone
        plane = jnp.where(here, 0.5 * plane_ref[at], plane)
        thick = jnp.where(here, 0.5 * thick_ref[at], thick)
        soft = jnp.where(here, soft_ref[at], soft)
    table_ref[0:1] = plane[:1]
    table_ref[1:2] = (plane * soft)[:1]
    table_ref[2:3] = thick[:1]
    table_ref[3:4] = (thick * soft)[:1]
    table_ref[4:8] = soft[:4]
    for copy in copies[:3]:
        copy.wait()
    pack_rows(lax.axis_index("layer"), u_ref, zone_ref, head_ref, tail_ref, flux_ref)


def pack_other_kernel(u_ref, zone_ref, head_ref, tail_ref):
    pack_rows(lax.axis_index("layer"), u_ref, zone_ref, head_ref, tail_ref)


def join_layers(low, high):
    depth = low.shape[0] // 2
    return (
        jnp.concatenate([low[:depth], high[:depth]], axis=0),
        jnp.concatenate([low[depth:], high[depth:]], axis=0),
    )


def pair_sum(value):
    layers = value.shape[0]
    even = iota(value.shape, 0) % 2 == 0
    return value + jnp.where(even, pltpu.roll(value, layers - 1, 0), pltpu.roll(value, 1, 0))


def halves(value):
    return value[:, :LANES] + value[:, LANES:]


def step_row(v, low, high, k_plane, k_thick, source, y_flow, layer_gap):
    layers = v.shape[0]
    inside = iota(v.shape, 0) < layers - layer_gap
    shift = layers - layer_gap
    up_v, up_k = pltpu.roll(v, shift, 0), pltpu.roll(k_thick, shift, 0)
    flow = jnp.where(inside, (k_thick + up_k) * (up_v - v), 0.0)
    return v + source + (high - low) + y_flow(v, k_plane) + (flow - pltpu.roll(flow, layer_gap, 0))


def fine_y(v, k):
    va, vb, ka, kb = v[:, :LANES], v[:, LANES:], k[:, :LANES], k[:, LANES:]
    inner = (ka + kb) * (vb - va)
    next_v, next_k = pltpu.roll(va, LANES - 1, 1), pltpu.roll(ka, LANES - 1, 1)
    outer = jnp.where(iota(va.shape, 1) < LANES - 1, (kb + next_k) * (next_v - vb), 0.0)
    return jnp.concatenate([inner - pltpu.roll(outer, 1, 1), outer - inner], axis=1)


def coarse_y(v, k):
    next_v, next_k = pltpu.roll(v, LANES - 1, 1), pltpu.roll(k, LANES - 1, 1)
    flow = jnp.where(iota(v.shape, 1) < LANES - 1, (k + next_k) * (next_v - v), 0.0)
    return flow - pltpu.roll(flow, 1, 1)


def outer_mask(core):
    tile, tiles = lax.axis_index("tile"), lax.axis_size("tile")
    at_edge = jnp.where(core == 0, tile == 0, tile == tiles - 1)
    return jnp.where(at_edge, 0.0, 1.0).astype(jnp.float32)


def look_up(table_ref, zone):
    zone = zone.astype(jnp.int32)
    halves_of = (zone[:, :LANES], zone[:, LANES:])
    tables = [jnp.broadcast_to(table_ref[k : k + 1, :], halves_of[0].shape) for k in range(5)]
    return [jnp.concatenate([pick(t, z) for z in halves_of], axis=1) for t in tables]


def flux_row(head_ref, i):
    return head_ref[HALO + i // 8, i % 8 : i % 8 + 1, :]


def to_source(flux, layers):
    return jnp.where(iota((layers, flux.shape[1]), 0) == 0, flux, 0.0)


def to_coarse(coarse_ref, at, rows):
    sums = []
    for coefs, v, flux in rows:
        sums.append([halves(x) for x in (coefs[0], coefs[2], coefs[4], v, flux)])
    first, second = sums
    for k in range(4):
        coarse_ref[k, at] = 0.125 * pair_sum(first[k] + second[k])
    pair = iota(coarse_ref.shape[2:], 0) < 2
    coarse_ref[4, at] = jnp.where(pair, 0.5 * (first[4] + second[4]), 0.0)


def fine_sweep(step, rows, load_v, store_v, load_coef, source, mask):
    v_next = load_v(rows[0] - 1)
    k_next = load_coef(0, rows[0] - 1) + load_coef(1, rows[0] - 1) * v_next
    high = None
    for j in (rows[0] - 1, *rows):
        v, k_plane, low = v_next, k_next, high
        v_next = load_v(j + 1)
        k_next = load_coef(0, j + 1) + load_coef(1, j + 1) * v_next
        high = (k_plane + k_next) * (v_next - v)
        if j == HALO - 1:
            high = high * mask
        if j >= rows[0]:
            k_thick = load_coef(2, j) + load_coef(3, j) * v
            store_v(j, step_row(v, low, high, k_plane, k_thick, source(j), fine_y, 1))


def interior_kernel(
    own_ref, own_tail, other_ref, other_tail, table_ref, edge_ref, coef_out, coarse_ref, v_ref, coef_ref
):
    width, layers = v_ref.shape[:2]
    core = lax.axis_index("layer")

    def gather(order):
        rows = []
        for i in range(width):
            slabs = [
                ref[i] if i < HALO else tail[i - HALO]
                for ref, tail in ((own_ref, own_tail), (other_ref, other_tail))
            ]
            v, zone = join_layers(*(slabs[k] for k in order))
            coefs = look_up(table_ref, zone)
            v_ref[i] = v
            for k in range(4):
                coef_ref[k, i] = coefs[k]
                if i < coef_out.shape[1]:
                    coef_out[k, i] = coefs[k]
            rows.append((coefs, v, flux_row(own_ref, i)))
            if i % 2:
                to_coarse(coarse_ref, i // 2, rows)
                rows = []

    pl.when(core == 0)(lambda: gather((0, 1)))
    pl.when(core == 1)(lambda: gather((1, 0)))
    for level in range(FINE_STEPS):
        if level:
            fine_sweep(
                level,
                range(HALO + level, HALO + width - level),
                lambda j: v_ref[j - HALO],
                lambda j, value: v_ref.__setitem__(j - HALO, value),
                lambda k, j: coef_ref[k, j - HALO],
                lambda j: to_source(flux_row(own_ref, j - HALO), layers),
                None,
            )
        for i in range(2):
            edge_ref[level, i] = v_ref[level + i]


def edge_kernel(
    recv_ref,
    recv_other,
    own_ref,
    table_ref,
    edge_ref,
    own_coef,
    rest_ref,
    share_ref,
    coarse_ref,
    v_ref,
    coef_ref,
):
    layers = v_ref.shape[1]
    half = v_ref.shape[0] - HALO
    core = lax.axis_index("layer")
    mask = outer_mask(core)

    def gather(order):
        rows = []
        for j in range(HALO):
            i = HALO - 1 - j
            slabs = (recv_ref[i], recv_other[i])
            v, zone = join_layers(*(slabs[k] for k in order))
            coefs = look_up(table_ref, zone)
            v_ref[j] = v
            for k in range(4):
                coef_ref[k, j] = coefs[k]
            rows.append((coefs, v, flux_row(recv_ref, i)))
            if j % 2:
                if j >= HALO - EDGE:
                    to_coarse(coarse_ref, (j - (HALO - EDGE)) // 2, rows)
                rows = []

    pl.when(core == 0)(lambda: gather((1, 0)))
    pl.when(core == 1)(lambda: gather((0, 1)))

    def source(j):
        flux = flux_row(own_ref, j - HALO) if j >= HALO else flux_row(recv_ref, HALO - 1 - j)
        return to_source(flux, layers)

    for step in range(1, FINE_STEPS + 1):
        reach = HALO + step - 1
        fine_sweep(
            step,
            range(step, HALO + step),
            lambda j: edge_ref[step - 1, j - reach] if j >= reach else v_ref[j],
            lambda j, value: v_ref.__setitem__(j, value),
            lambda k, j: own_coef[k, j - HALO] if j >= HALO else coef_ref[k, j],
            source,
            mask,
        )

    even = iota((layers, LANES), 0) % 2 == 0
    restricted = []
    for j in range(HALO - EDGE, HALO + half, 2):
        restricted.append(0.125 * pair_sum(halves(v_ref[j]) + halves(v_ref[j + 1])))
    for i in range(0, len(restricted), 2):
        rest_ref[i // 2] = jnp.where(even, restricted[i], restricted[i + 1])
    for i in range(half):
        share_ref[2 * i] = v_ref[HALO + i][:, :LANES]
        share_ref[2 * i + 1] = v_ref[HALO + i][:, LANES:]
    for k in range(5):
        for i in range(COARSE_STEPS):
            share_ref[2 * half + k * COARSE_STEPS + i] = coarse_ref[k, i]


def coarse_fields(coarse_ref, outer_ref, other_ref):
    own = coarse_ref.shape[1]

    def row(k, j):
        if j < COARSE_STEPS:
            return outer_ref[k, j]
        if j < COARSE_STEPS + own:
            return coarse_ref[k, j - COARSE_STEPS]
        return other_ref[2 * own + k * COARSE_STEPS + own + 2 * COARSE_STEPS - 1 - j]

    return row


def coarse_propagate(state, field, masks):
    count = len(state)
    flux = {j: field(4, j) for j in range(1, count - 1)}
    plane = [field(0, j) for j in range(count)]
    thick = [field(1, j) for j in range(count)]
    soft = [field(2, j) for j in range(count)]
    for step in range(1, COARSE_STEPS + 1):
        k_plane = {
            j: plane[j] * (1.0 + soft[j] * state[j]) for j in range(step - 1, count - step + 1)
        }
        flows = {}
        for j in range(step - 1, count - step):
            flow = (k_plane[j] + k_plane[j + 1]) * (state[j + 1] - state[j])
            flows[j] = flow * masks[j] if j in masks else flow
        fresh = list(state)
        for j in range(step, count - step):
            k_thick = thick[j] * (1.0 + soft[j] * state[j])
            fresh[j] = step_row(
                state[j], flows[j - 1], flows[j], k_plane[j], k_thick, flux[j], coarse_y, 2
            )
        state = fresh
    return state[COARSE_STEPS : count - COARSE_STEPS]


def edge_factors(rows):
    core = lax.axis_index("layer")
    return {
        COARSE_STEPS - 1: outer_mask(core),
        rows - COARSE_STEPS - 1: outer_mask(1 - core),
    }


def expand(slab):
    layers = slab.shape[0]
    even = iota(slab.shape, 0) % 2 == 0
    return [
        jnp.where(even, slab, pltpu.roll(slab, 1, 0)),
        jnp.where(even, pltpu.roll(slab, layers - 1, 0), slab),
    ]


def read_state(refs):
    if len(refs) == 1:
        return [refs[0][j] for j in range(refs[0].shape[0])]
    mine, other = (sum((expand(ref[i]) for i in range(ref.shape[0])), []) for ref in refs)
    return mine + other[::-1]


def unfold_kernel(mine_ref, other_ref, state_ref):
    for j, row in enumerate(read_state((mine_ref, other_ref))):
        state_ref[j] = row


def propagated(refs, state_refs=None):
    field = coarse_fields(*refs)
    rows = refs[0].shape[1] + 2 * COARSE_STEPS
    state = [field(3, j) for j in range(rows)]
    if state_refs:
        first = lax.axis_index("tm") == 0
        state = [jnp.where(first, a, b) for a, b in zip(state, read_state(state_refs))]
    return coarse_propagate(state, field, edge_factors(rows))


def base_kernel(coarse_ref, outer_ref, share_ref, other_ref, base_ref):
    depth, width = base_ref.shape[:2]
    core = lax.axis_index("layer")
    base = propagated((coarse_ref, outer_ref, other_ref))

    def write(mirror):
        for j in range(0, width, 2):
            slabs = []
            for i in (j, j + 1):
                ref, at = (share_ref, i) if i < width // 2 else (other_ref, width - 1 - i)
                slab = jnp.concatenate(
                    [ref[2 * at] - base[j // 2], ref[2 * at + 1] - base[j // 2]], axis=1
                )
                slabs.append(slab[depth:] if mirror else slab[:depth])
            both = join_lanes(jnp.concatenate(slabs, axis=0))
            for i in (0, 1):
                row = width - 1 - (j + i) if mirror else j + i
                base_ref[:, row, :] = both[depth * i : depth * (i + 1)]

    pl.when(core == 0)(lambda: write(False))
    pl.when(core == 1)(lambda: write(True))


def output_kernel(*refs):
    *state_refs, coarse_ref, outer_ref, other_ref, base_ref, out_ref = refs
    depth, width = base_ref.shape[:2]
    core = lax.axis_index("layer")
    moved = propagated((coarse_ref, outer_ref, other_ref), state_refs)
    half = iota(moved[0].shape, 1) // 2

    def write(mirror):
        for j, row in enumerate(moved):
            gain = jnp.concatenate([pick(row, half), pick(row, half + LANES // 2)], axis=1)
            gain = gain[depth:] if mirror else gain[:depth]
            for i in (2 * j, 2 * j + 1):
                at = width - 1 - i if mirror else i
                out_ref[0, :, at, :] = base_ref[:, at, :] + gain

    pl.when(core == 0)(lambda: write(False))
    pl.when(core == 1)(lambda: write(True))


def advance_kernel(state_ref, coarse_ref, outer_ref, share_ref, other_ref, next_ref):
    own = next_ref.shape[0]
    refs = (coarse_ref, outer_ref, other_ref)
    moved, base = propagated(refs, (state_ref,)), propagated(refs)
    for j in range(own):
        pair = []
        for i in (2 * j, 2 * j + 1):
            ref, at = (share_ref, i) if i < own else (other_ref, 2 * own - 1 - i)
            pair.append(ref[2 * at] + ref[2 * at + 1])
        next_ref[j] = moved[j] - base[j] + 0.125 * pair_sum(pair[0] + pair[1])


def layer_swap(value):
    return lax.ppermute(value, "layer", [(0, 1), (1, 0)])


def swap_pairs(pairs):
    return [edge for a, b in pairs for edge in ((a, b), (b, a))]


def tile_swap(value):
    tiles, slices = lax.axis_size("tile"), lax.axis_size("tm")
    at = lambda tile, time, core: (tile * slices + time) * 2 + core
    pairs = [
        (at(t, m, 0), at(t - 1, m, 1)) for t in range(1, tiles) for m in range(slices)
    ]
    for m in range(0, slices - 1, 2):
        pairs.append((at(0, m, 0), at(0, m + 1, 0)))
        pairs.append((at(tiles - 1, m, 1), at(tiles - 1, m + 1, 1)))
    return lax.ppermute(value, ("tile", "tm", "layer"), swap_pairs(pairs))


def time_swap(value, parity):
    slices = lax.axis_size("tm")
    at = lambda time, core: time * 2 + core
    pairs = [
        (at(m, c), at(m + 1, c)) for m in range(parity, slices - 1, 2) for c in range(2)
    ]
    used = {d for pair in pairs for d in pair}
    pairs += [(at(m, 0), at(m, 1)) for m in range(slices) if at(m, 0) not in used]
    return lax.ppermute(value, ("tm", "layer"), swap_pairs(pairs))


def cross_swap(value):
    slices = lax.axis_size("tm")
    pairs = [(m * 2 + c, m * 2 + 3 - c) for m in range(0, slices - 1, 2) for c in range(2)]
    return lax.ppermute(value, ("tm", "layer"), swap_pairs(pairs))


def on_device(u_start, flux, zone_of_cell, zone_row, plane_rate, thick_rate, soften):
    depth, width, length = zone_of_cell.shape
    layers = depth * lax.axis_size("layer")
    half = width // 2
    f32 = jnp.float32
    slabs = lambda *lead: jax.ShapeDtypeStruct((*lead, layers, LANES), f32)
    wide = lambda *lead: jax.ShapeDtypeStruct((*lead, layers, length), f32)

    def call(kernel, out_shape, *operands, name, scratch=(), memory=pltpu.VMEM):
        return pl.pallas_call(
            kernel,
            out_shape=out_shape,
            in_specs=[pl.BlockSpec(memory_space=memory)] * len(operands),
            out_specs=jax.tree.map(lambda _: VMEM, out_shape),
            scratch_shapes=scratch,
            compiler_params=pltpu.CompilerParams(vmem_limit_bytes=VMEM_BYTES),
            name=name,
        )(*operands)

    u_own = u_start[0]
    u_other, zone_other = layer_swap(u_own), layer_swap(zone_of_cell)
    own, own_tail, tables = call(
        pack_own_kernel,
        (wide(HALO + width // 8), wide(width - HALO), jax.ShapeDtypeStruct((8, LANES), f32)),
        *(u_own, zone_of_cell, flux[0], zone_row, plane_rate, thick_rate, soften),
        name="pack_own",
        scratch=[
            pltpu.VMEM(u_own.shape, f32),
            pltpu.VMEM(zone_of_cell.shape, jnp.int32),
            pltpu.VMEM(flux.shape[1:], f32),
            pltpu.SMEM(zone_row.shape, jnp.int32),
            *[pltpu.SMEM(plane_rate.shape, f32)] * 3,
            pltpu.SemaphoreType.DMA((7,)),
        ],
        memory=pltpu.HBM,
    )
    recv = tile_swap(own)
    other, other_tail = call(
        pack_other_kernel,
        (wide(HALO), wide(width - HALO)),
        *(u_other, zone_other),
        name="pack_other",
    )
    recv_other = tile_swap(other)

    levels, own_coef, coarse = call(
        interior_kernel,
        (wide(FINE_STEPS, 2), wide(4, FINE_STEPS + 1), slabs(5, half)),
        *(own, own_tail, other, other_tail, tables),
        name="interior",
        scratch=[
            pltpu.VMEM((width, layers, length), f32),
            pltpu.VMEM((4, width, layers, length), f32),
        ],
    )
    rest, share, outer = call(
        edge_kernel,
        (
            slabs((half + EDGE) // 4),
            slabs(2 * half + 5 * COARSE_STEPS),
            slabs(5, COARSE_STEPS),
        ),
        *(recv, recv_other, own, tables, levels, own_coef),
        name="edge",
        scratch=[
            pltpu.VMEM((HALO + half, layers, length), f32),
            pltpu.VMEM((4, HALO, layers, length), f32),
        ],
    )

    slices = lax.axis_size("tm")
    position = lax.axis_index("tm")
    state = [rest, rest]
    if slices > 1:
        state = [time_swap(rest, 0), cross_swap(rest)]
    other_share = layer_swap(share)
    base = call(
        base_kernel,
        jax.ShapeDtypeStruct((depth, width, length), f32),
        *(coarse, outer, share, other_share),
        name="base",
    )
    if slices > 2:
        full = slabs(half + 2 * COARSE_STEPS)
        state = [call(unfold_kernel, full, *state, name="unfold")]
    for turn in range(1, slices - 1):
        ended = call(
            advance_kernel,
            slabs(half),
            *(*state, coarse, outer, share, other_share),
            name="advance",
        )
        low = tile_swap(ended[:COARSE_STEPS])
        high = layer_swap(low)
        arrived = time_swap(jnp.concatenate([low[::-1], ended, high], axis=0), turn % 2)
        state = [jnp.where(position == turn + 1, arrived, state[0])]
    return call(
        output_kernel,
        jax.ShapeDtypeStruct((1, depth, width, length), f32),
        *(*state, coarse, outer, other_share, base),
        name="output",
    )


def solution(mesh):
    return jax.shard_map(
        on_device,
        mesh=mesh,
        in_specs=(
            P(("parts", "tm"), "layer", "tile", None),
            P(("parts", "tm"), "tile", None),
            P("layer", "tile", None),
            P(),
            P(),
            P(),
            P(),
        ),
        out_specs=P(("parts", "tm"), "layer", "tile", None),
        check_vma=False,
    )
```

```python
import jax
import jax.numpy as jnp
from jax import lax
from jax.experimental import pallas as pl
from jax.experimental.pallas import tpu as pltpu
from jax.sharding import PartitionSpec as P

FINE_STEPS = 8
COARSE_STEPS = 2
LANES = 128
EDGE = 2 * COARSE_STEPS
HALO = FINE_STEPS + EDGE
VMEM_BYTES = 16 * 2**20
VMEM = pl.BlockSpec(memory_space=pltpu.VMEM)


def iota(shape, dim):
    return lax.broadcasted_iota(jnp.int32, shape, dim)


def pick(table, index):
    return jnp.take_along_axis(table, index, axis=1, mode="promise_in_bounds")


def split_lanes(row):
    rows = row.shape[0]
    lane = iota((rows, LANES), 1)
    low = lane < LANES // 2
    even = (2 * lane) % LANES
    first, second = row[:, :LANES], row[:, LANES:]
    return jnp.concatenate(
        [
            jnp.where(low, pick(first, even), pick(second, even)),
            jnp.where(low, pick(first, even + 1), pick(second, even + 1)),
        ],
        axis=1,
    )


def join_lanes(row):
    rows = row.shape[0]
    lane = iota((rows, LANES), 1)
    is_even = lane % 2 == 0
    half = lane // 2
    even, odd = row[:, :LANES], row[:, LANES:]
    return jnp.concatenate(
        [
            jnp.where(is_even, pick(even, half), pick(odd, half)),
            jnp.where(is_even, pick(even, half + LANES // 2), pick(odd, half + LANES // 2)),
        ],
        axis=1,
    )


def pack_kernel(
    u_hbm, zone_hbm, flux_hbm, head_ref, tail_ref, turned_ref, u_ref, zone_ref, flux_ref, sems
):
    copies = start_copies((u_hbm, zone_hbm, flux_hbm), (u_ref, zone_ref, flux_ref), sems)
    width = u_ref.shape[1]

    def fill(mirror):
        for i in range(width):
            row = width - 1 - i if mirror else i
            slab = jnp.concatenate(
                [u_ref[:, row, :], zone_ref[:, row, :].astype(jnp.float32)], axis=0
            )
            slab = split_lanes(slab)
            turned_ref[width - 1 - i] = slab
            if i < HALO:
                head_ref[i] = slab
            else:
                tail_ref[i - HALO] = slab
        flux = split_lanes(flux_ref[...])
        for i in range(width):
            row = width - 1 - i if mirror else i
            head_ref[HALO + i // 8, i % 8 : i % 8 + 1, :] = flux[row : row + 1]

    for copy in copies:
        copy.wait()
    core = lax.axis_index("layer")
    pl.when(core == 0)(lambda: fill(True))
    pl.when(core == 1)(lambda: fill(False))


def start_copies(sources, targets, sems):
    copies = [
        pltpu.make_async_copy(source, target, sems.at[k])
        for k, (source, target) in enumerate(zip(sources, targets))
    ]
    for copy in copies:
        copy.start()
    return copies


def fill_tables(table_ref, row_ref, plane_ref, thick_ref, soft_ref):
    lane = iota((1, LANES), 1)
    tables = [jnp.zeros((1, LANES), jnp.float32)] * 3
    for zone in range(row_ref.shape[0]):
        at = row_ref[zone]
        values = (0.5 * plane_ref[at], 0.5 * thick_ref[at], soft_ref[at])
        tables = [jnp.where(lane == zone, x, t) for x, t in zip(values, tables)]
    for k in range(3):
        table_ref[k : k + 1] = tables[k]


def join_layers(low, high):
    depth = low.shape[0] // 2
    return (
        jnp.concatenate([low[:depth], high[:depth]], axis=0),
        jnp.concatenate([low[depth:], high[depth:]], axis=0),
    )


def pair_sum(value):
    layers = value.shape[0]
    even = iota(value.shape, 0) % 2 == 0
    return value + jnp.where(even, pltpu.roll(value, layers - 1, 0), pltpu.roll(value, 1, 0))


def halves(value):
    return value[:, :LANES] + value[:, LANES:]


def step_row(v, low, high, k_plane, k_thick, source, y_gain, layer_gap):
    layers = v.shape[0]
    layer = iota(v.shape, 0)
    up, down = layers - layer_gap, layer_gap
    from_up = jnp.where(layer < layers - layer_gap, pltpu.roll(v, up, 0) - v, 0.0)
    from_down = jnp.where(layer >= layer_gap, pltpu.roll(v, down, 0) - v, 0.0)
    z_gain = (k_thick + pltpu.roll(k_thick, up, 0)) * from_up
    z_gain = z_gain + (k_thick + pltpu.roll(k_thick, down, 0)) * from_down
    return ((v + source) + (high - low)) + (z_gain + y_gain(v, k_plane))


def fine_y(v, k):
    va, vb, ka, kb = v[:, :LANES], v[:, LANES:], k[:, :LANES], k[:, LANES:]
    lane = iota(va.shape, 1)
    inner = (ka + kb) * (vb - va)
    from_last = jnp.where(lane > 0, pltpu.roll(vb, 1, 1) - va, 0.0)
    from_next = jnp.where(lane < LANES - 1, pltpu.roll(va, LANES - 1, 1) - vb, 0.0)
    even = inner + (ka + pltpu.roll(kb, 1, 1)) * from_last
    odd = (kb + pltpu.roll(ka, LANES - 1, 1)) * from_next - inner
    return jnp.concatenate([even, odd], axis=1)


def coarse_y(v, k):
    lane = iota(v.shape, 1)
    from_last = jnp.where(lane > 0, pltpu.roll(v, 1, 1) - v, 0.0)
    from_next = jnp.where(lane < LANES - 1, pltpu.roll(v, LANES - 1, 1) - v, 0.0)
    last = (k + pltpu.roll(k, 1, 1)) * from_last
    return last + (k + pltpu.roll(k, LANES - 1, 1)) * from_next


def outer_mask(core):
    tile, tiles = lax.axis_index("tile"), lax.axis_size("tile")
    at_edge = jnp.where(core == 1, tile == 0, tile == tiles - 1)
    return jnp.where(at_edge, 0.0, 1.0).astype(jnp.float32)


def look_up(table_ref, zone):
    zone = zone.astype(jnp.int32)
    halves_of = (zone[:, :LANES], zone[:, LANES:])
    tables = [jnp.broadcast_to(table_ref[k : k + 1, :], halves_of[0].shape) for k in range(3)]
    plane, thick, soft = (
        jnp.concatenate([pick(t, z) for z in halves_of], axis=1) for t in tables
    )
    return [plane, plane * soft, thick, thick * soft, soft]


def flux_row(head_ref, i):
    return head_ref[HALO + i // 8, i % 8 : i % 8 + 1, :]


def to_source(flux, layers):
    return jnp.where(iota((layers, flux.shape[1]), 0) == 0, flux, 0.0)


def to_coarse(coarse_ref, at, rows):
    sums = []
    for coefs, v, flux in rows:
        sums.append([halves(x) for x in (coefs[0], coefs[2], coefs[4], v, flux)])
    first, second = sums
    for k in range(4):
        coarse_ref[k, at] = 0.125 * pair_sum(first[k] + second[k])
    pair = iota(coarse_ref.shape[2:], 0) < 2
    coarse_ref[4, at] = jnp.where(pair, 0.5 * (first[4] + second[4]), 0.0)


def fine_step(rows, state, load_coef, source, mask):
    v_next = state[rows[0] - 1]
    k_next = load_coef(0, rows[0] - 1) + load_coef(1, rows[0] - 1) * v_next
    high = None
    fresh = {}
    for j in (rows[0] - 1, *rows):
        v, k_plane, low = v_next, k_next, high
        v_next = state[j + 1]
        k_next = load_coef(0, j + 1) + load_coef(1, j + 1) * v_next
        high = (k_plane + k_next) * (v_next - v)
        if j == HALO - 1:
            high = high * mask
        if j >= rows[0]:
            k_thick = load_coef(2, j) + load_coef(3, j) * v
            fresh[j] = step_row(v, low, high, k_plane, k_thick, source(j), fine_y, 1)
    return fresh


def interior_kernel(
    own_ref,
    own_tail,
    other_ref,
    row_hbm,
    plane_hbm,
    thick_hbm,
    soft_hbm,
    edge_ref,
    coef_out,
    coarse_ref,
    table_ref,
    v_ref,
    coef_ref,
    row_ref,
    plane_ref,
    thick_ref,
    soft_ref,
    sems,
):
    parameters = (row_ref, plane_ref, thick_ref, soft_ref)
    for copy in start_copies((row_hbm, plane_hbm, thick_hbm, soft_hbm), parameters, sems):
        copy.wait()
    fill_tables(table_ref, *parameters)
    width, layers = v_ref.shape[:2]
    core = lax.axis_index("layer")

    def gather(order):
        rows = []
        for i in range(width):
            slabs = (own_ref[i] if i < HALO else own_tail[i - HALO], other_ref[i])
            v, zone = join_layers(*(slabs[k] for k in order))
            coefs = look_up(table_ref, zone)
            v_ref[i] = v
            for k in range(4):
                coef_ref[k, i] = coefs[k]
                if i < coef_out.shape[1]:
                    coef_out[k, i] = coefs[k]
            rows.append((coefs, v, flux_row(own_ref, i)))
            if i % 2:
                to_coarse(coarse_ref, i // 2, rows)
                rows = []

    pl.when(core == 0)(lambda: gather((0, 1)))
    pl.when(core == 1)(lambda: gather((1, 0)))
    state = {HALO + i: v_ref[i] for i in range(width)}
    for level in range(FINE_STEPS):
        if level:
            state = fine_step(
                range(HALO + level, HALO + width - level),
                state,
                lambda k, j: coef_ref[k, j - HALO],
                lambda j: to_source(flux_row(own_ref, j - HALO), layers),
                None,
            )
        for i in range(2):
            edge_ref[level, i] = state[HALO + level + i]


def edge_kernel(
    recv_ref,
    recv_other,
    own_ref,
    table_ref,
    edge_ref,
    own_coef,
    rest_ref,
    share_ref,
    coarse_ref,
    v_ref,
    coef_ref,
    source_ref,
):
    layers = v_ref.shape[1]
    half = v_ref.shape[0] - HALO
    core = lax.axis_index("layer")
    mask = outer_mask(core)

    def gather(order):
        rows = []
        for j in range(HALO):
            i = HALO - 1 - j
            slabs = (recv_ref[i], recv_other[i])
            v, zone = join_layers(*(slabs[k] for k in order))
            coefs = look_up(table_ref, zone)
            v_ref[j] = v
            for k in range(4):
                coef_ref[k, j] = coefs[k]
            rows.append((coefs, v, flux_row(recv_ref, i)))
            if j % 2:
                if j >= HALO - EDGE:
                    to_coarse(coarse_ref, (j - (HALO - EDGE)) // 2, rows)
                rows = []

    pl.when(core == 0)(lambda: gather((1, 0)))
    pl.when(core == 1)(lambda: gather((0, 1)))

    for j in range(HALO + FINE_STEPS):
        flux = flux_row(own_ref, j - HALO) if j >= HALO else flux_row(recv_ref, HALO - 1 - j)
        source_ref[j] = to_source(flux, layers)
    source = lambda j: source_ref[j]

    state = {j: v_ref[j] for j in range(HALO)}
    for step in range(1, FINE_STEPS + 1):
        for i in range(2):
            state[HALO + step - 1 + i] = edge_ref[step - 1, i]
        state = fine_step(
            range(step, HALO + step),
            state,
            lambda k, j: own_coef[k, j - HALO] if j >= HALO else coef_ref[k, j],
            source,
            mask,
        )

    even = iota((layers, LANES), 0) % 2 == 0
    restricted = []
    for j in range(HALO - EDGE, HALO + half, 2):
        restricted.append(0.125 * pair_sum(halves(state[j]) + halves(state[j + 1])))
    for i in range(0, len(restricted), 2):
        rest_ref[i // 2] = jnp.where(even, restricted[i], restricted[i + 1])
    for i in range(half):
        share_ref[2 * i] = state[HALO + i][:, :LANES]
        share_ref[2 * i + 1] = state[HALO + i][:, LANES:]
    for k in range(5):
        for i in range(COARSE_STEPS):
            share_ref[2 * half + k * COARSE_STEPS + i] = coarse_ref[k, i]


def coarse_fields(coarse_ref, outer_ref, other_ref):
    own = coarse_ref.shape[1]

    def row(k, j):
        if j < COARSE_STEPS:
            return outer_ref[k, j]
        if j < COARSE_STEPS + own:
            return coarse_ref[k, j - COARSE_STEPS]
        return other_ref[2 * own + k * COARSE_STEPS + own + 2 * COARSE_STEPS - 1 - j]

    return row


def coarse_propagate(state, field, masks):
    count = len(state)
    flux = {j: field(4, j) for j in range(1, count - 1)}
    plane = [field(0, j) for j in range(count)]
    thick = [field(1, j) for j in range(count)]
    soft = [field(2, j) for j in range(count)]
    for step in range(1, COARSE_STEPS + 1):
        k_plane = {
            j: plane[j] * (1.0 + soft[j] * state[j]) for j in range(step - 1, count - step + 1)
        }
        flows = {}
        for j in range(step - 1, count - step):
            flow = (k_plane[j] + k_plane[j + 1]) * (state[j + 1] - state[j])
            flows[j] = flow * masks[j] if j in masks else flow
        fresh = list(state)
        for j in range(step, count - step):
            k_thick = thick[j] * (1.0 + soft[j] * state[j])
            fresh[j] = step_row(
                state[j], flows[j - 1], flows[j], k_plane[j], k_thick, flux[j], coarse_y, 2
            )
        state = fresh
    return state[COARSE_STEPS : count - COARSE_STEPS]


def edge_factors(rows):
    core = lax.axis_index("layer")
    return {
        COARSE_STEPS - 1: outer_mask(core),
        rows - COARSE_STEPS - 1: outer_mask(1 - core),
    }


def expand(slab):
    layers = slab.shape[0]
    even = iota(slab.shape, 0) % 2 == 0
    return [
        jnp.where(even, slab, pltpu.roll(slab, 1, 0)),
        jnp.where(even, pltpu.roll(slab, layers - 1, 0), slab),
    ]


def read_state(refs):
    if len(refs) == 1:
        return [refs[0][j] for j in range(refs[0].shape[0])]
    mine, other = (sum((expand(ref[i]) for i in range(ref.shape[0])), []) for ref in refs)
    return mine + other[::-1]


def unfold_kernel(mine_ref, other_ref, state_ref):
    for j, row in enumerate(read_state((mine_ref, other_ref))):
        state_ref[j] = row


def propagated(refs, state_refs=None):
    field = coarse_fields(*refs)
    rows = refs[0].shape[1] + 2 * COARSE_STEPS
    state = [field(3, j) for j in range(rows)]
    if state_refs:
        first = lax.axis_index("tm") == 0
        state = [jnp.where(first, a, b) for a, b in zip(state, read_state(state_refs))]
    return coarse_propagate(state, field, edge_factors(rows))


def base_kernel(coarse_ref, outer_ref, share_ref, other_ref, base_ref):
    depth, width = base_ref.shape[:2]
    core = lax.axis_index("layer")
    base = propagated((coarse_ref, outer_ref, other_ref))

    def write(mirror):
        for j in range(0, width, 2):
            slabs = []
            for i in (j, j + 1):
                ref, at = (share_ref, i) if i < width // 2 else (other_ref, width - 1 - i)
                slab = jnp.concatenate(
                    [ref[2 * at] - base[j // 2], ref[2 * at + 1] - base[j // 2]], axis=1
                )
                slabs.append(slab[:depth] if mirror else slab[depth:])
            both = join_lanes(jnp.concatenate(slabs, axis=0))
            for i in (0, 1):
                row = width - 1 - (j + i) if mirror else j + i
                base_ref[:, row, :] = both[depth * i : depth * (i + 1)]

    pl.when(core == 0)(lambda: write(True))
    pl.when(core == 1)(lambda: write(False))


def output_kernel(*refs):
    *state_refs, coarse_ref, outer_ref, other_ref, base_ref, out_ref = refs
    depth, width = base_ref.shape[:2]
    core = lax.axis_index("layer")
    moved = propagated((coarse_ref, outer_ref, other_ref), state_refs)
    half = iota(moved[0].shape, 1) // 2

    def write(mirror):
        for j, row in enumerate(moved):
            gain = jnp.concatenate([pick(row, half), pick(row, half + LANES // 2)], axis=1)
            gain = gain[:depth] if mirror else gain[depth:]
            for i in (2 * j, 2 * j + 1):
                at = width - 1 - i if mirror else i
                out_ref[0, :, at, :] = base_ref[:, at, :] + gain

    pl.when(core == 0)(lambda: write(True))
    pl.when(core == 1)(lambda: write(False))


def advance_kernel(state_ref, coarse_ref, outer_ref, share_ref, other_ref, next_ref):
    own = next_ref.shape[0]
    refs = (coarse_ref, outer_ref, other_ref)
    moved, base = propagated(refs, (state_ref,)), propagated(refs)
    for j in range(own):
        pair = []
        for i in (2 * j, 2 * j + 1):
            ref, at = (share_ref, i) if i < own else (other_ref, 2 * own - 1 - i)
            pair.append(ref[2 * at] + ref[2 * at + 1])
        next_ref[j] = moved[j] - base[j] + 0.125 * pair_sum(pair[0] + pair[1])


def layer_swap(value):
    return lax.ppermute(value, "layer", [(0, 1), (1, 0)])


def swap_pairs(pairs):
    return [edge for a, b in pairs for edge in ((a, b), (b, a))]


def tile_swap(value):
    tiles, slices = lax.axis_size("tile"), lax.axis_size("tm")
    at = lambda tile, time, core: (tile * slices + time) * 2 + core
    pairs = [
        (at(t, m, 1), at(t - 1, m, 0)) for t in range(1, tiles) for m in range(slices)
    ]
    for m in range(0, slices - 1, 2):
        pairs.append((at(0, m, 1), at(0, m + 1, 1)))
        pairs.append((at(tiles - 1, m, 0), at(tiles - 1, m + 1, 0)))
    return lax.ppermute(value, ("tile", "tm", "layer"), swap_pairs(pairs))


def time_swap(value, parity):
    slices = lax.axis_size("tm")
    at = lambda time, core: time * 2 + core
    pairs = [
        (at(m, c), at(m + 1, c)) for m in range(parity, slices - 1, 2) for c in range(2)
    ]
    used = {d for pair in pairs for d in pair}
    pairs += [(at(m, 0), at(m, 1)) for m in range(slices) if at(m, 0) not in used]
    return lax.ppermute(value, ("tm", "layer"), swap_pairs(pairs))


def cross_swap(value):
    slices = lax.axis_size("tm")
    pairs = [(m * 2 + c, m * 2 + 3 - c) for m in range(0, slices - 1, 2) for c in range(2)]
    return lax.ppermute(value, ("tm", "layer"), swap_pairs(pairs))


def on_device(u_start, flux, zone_of_cell, zone_row, plane_rate, thick_rate, soften):
    depth, width, length = zone_of_cell.shape
    layers = depth * lax.axis_size("layer")
    half = width // 2
    f32 = jnp.float32
    slabs = lambda *lead: jax.ShapeDtypeStruct((*lead, layers, LANES), f32)
    wide = lambda *lead: jax.ShapeDtypeStruct((*lead, layers, length), f32)

    def call(kernel, out_shape, *operands, name, scratch=(), in_hbm=()):
        spaces = [pltpu.HBM if k in in_hbm else pltpu.VMEM for k in range(len(operands))]
        operands = [
            pltpu.with_memory_space_constraint(x, space) if space is pltpu.HBM else x
            for x, space in zip(operands, spaces)
        ]
        return pl.pallas_call(
            kernel,
            out_shape=out_shape,
            in_specs=[pl.BlockSpec(memory_space=space) for space in spaces],
            out_specs=jax.tree.map(lambda _: VMEM, out_shape),
            scratch_shapes=scratch,
            compiler_params=pltpu.CompilerParams(vmem_limit_bytes=VMEM_BYTES),
            name=name,
        )(*operands)

    u_own = u_start[0]
    own, own_tail, turned = call(
        pack_kernel,
        (wide(HALO + width // 8), wide(width - HALO), wide(width)),
        *(u_own, zone_of_cell, flux[0]),
        name="pack",
        scratch=[
            pltpu.VMEM(u_own.shape, f32),
            pltpu.VMEM(zone_of_cell.shape, jnp.int32),
            pltpu.VMEM(flux.shape[1:], f32),
            pltpu.SemaphoreType.DMA((3,)),
        ],
        in_hbm=range(3),
    )
    other = layer_swap(turned)
    recv, recv_other = tile_swap(own), tile_swap(other[:HALO])

    levels, own_coef, coarse, tables = call(
        interior_kernel,
        (
            wide(FINE_STEPS, 2),
            wide(4, FINE_STEPS + 1),
            slabs(5, half),
            jax.ShapeDtypeStruct((3, LANES), f32),
        ),
        *(own, own_tail, other, zone_row, plane_rate, thick_rate, soften),
        name="interior",
        scratch=[
            pltpu.VMEM((width, layers, length), f32),
            pltpu.VMEM((4, width, layers, length), f32),
            pltpu.SMEM(zone_row.shape, jnp.int32),
            *[pltpu.SMEM(plane_rate.shape, f32)] * 3,
            pltpu.SemaphoreType.DMA((4,)),
        ],
        in_hbm=range(3, 7),
    )
    rest, share, outer = call(
        edge_kernel,
        (
            slabs((half + EDGE) // 4),
            slabs(2 * half + 5 * COARSE_STEPS),
            slabs(5, COARSE_STEPS),
        ),
        *(recv, recv_other, own, tables, levels, own_coef),
        name="edge",
        scratch=[
            pltpu.VMEM((HALO + half, layers, length), f32),
            pltpu.VMEM((4, HALO, layers, length), f32),
            pltpu.VMEM((HALO + FINE_STEPS, layers, length), f32),
        ],
    )

    slices = lax.axis_size("tm")
    position = lax.axis_index("tm")
    state = [rest, rest]
    if slices > 1:
        state = [time_swap(rest, 0), cross_swap(rest)]
    other_share = layer_swap(share)
    base = call(
        base_kernel,
        jax.ShapeDtypeStruct((depth, width, length), f32),
        *(coarse, outer, share, other_share),
        name="base",
    )
    if slices > 2:
        full = slabs(half + 2 * COARSE_STEPS)
        state = [call(unfold_kernel, full, *state, name="unfold")]
    for turn in range(1, slices - 1):
        ended = call(
            advance_kernel,
            slabs(half),
            *(*state, coarse, outer, share, other_share),
            name="advance",
        )
        low = tile_swap(ended[:COARSE_STEPS])
        high = layer_swap(low)
        arrived = time_swap(jnp.concatenate([low[::-1], ended, high], axis=0), turn % 2)
        state = [jnp.where(position == turn + 1, arrived, state[0])]
    return call(
        output_kernel,
        jax.ShapeDtypeStruct((1, depth, width, length), f32),
        *(*state, coarse, outer, other_share, base),
        name="output",
    )


def solution(mesh):
    return jax.shard_map(
        on_device,
        mesh=mesh,
        in_specs=(
            P(("parts", "tm"), "layer", "tile", None),
            P(("parts", "tm"), "tile", None),
            P("layer", "tile", None),
            P(),
            P(),
            P(),
            P(),
        ),
        out_specs=P(("parts", "tm"), "layer", "tile", None),
        check_vma=False,
    )
```

```python
import jax
import jax.numpy as jnp
from jax import lax
from jax.experimental import pallas as pl
from jax.experimental.pallas import tpu as pltpu
from jax.sharding import PartitionSpec as P

FINE_STEPS = 8
COARSE_STEPS = 2
LANES = 128
EDGE = 2 * COARSE_STEPS
HALO = FINE_STEPS + EDGE
VMEM_BYTES = 16 * 2**20
VMEM = pl.BlockSpec(memory_space=pltpu.VMEM)


def iota(shape, dim):
    return lax.broadcasted_iota(jnp.int32, shape, dim)


def pick(table, index):
    return jnp.take_along_axis(table, index, axis=1, mode="promise_in_bounds")


def split_lanes(row):
    rows = row.shape[0]
    lane = iota((rows, LANES), 1)
    low = lane < LANES // 2
    even = (2 * lane) % LANES
    first, second = row[:, :LANES], row[:, LANES:]
    return jnp.concatenate(
        [
            jnp.where(low, pick(first, even), pick(second, even)),
            jnp.where(low, pick(first, even + 1), pick(second, even + 1)),
        ],
        axis=1,
    )


def join_lanes(row):
    rows = row.shape[0]
    lane = iota((rows, LANES), 1)
    is_even = lane % 2 == 0
    half = lane // 2
    even, odd = row[:, :LANES], row[:, LANES:]
    return jnp.concatenate(
        [
            jnp.where(is_even, pick(even, half), pick(odd, half)),
            jnp.where(is_even, pick(even, half + LANES // 2), pick(odd, half + LANES // 2)),
        ],
        axis=1,
    )


def pack_kernel(
    u_hbm, zone_hbm, flux_hbm, head_ref, tail_ref, turned_ref, u_ref, zone_ref, flux_ref, sems
):
    copies = start_copies((u_hbm, zone_hbm, flux_hbm), (u_ref, zone_ref, flux_ref), sems)
    width = u_ref.shape[1]

    def fill(mirror):
        for i in range(width):
            row = width - 1 - i if mirror else i
            slab = jnp.concatenate(
                [u_ref[:, row, :], zone_ref[:, row, :].astype(jnp.float32)], axis=0
            )
            slab = split_lanes(slab)
            turned_ref[width - 1 - i] = slab
            if i < HALO:
                head_ref[i] = slab
            else:
                tail_ref[i - HALO] = slab
        flux = split_lanes(flux_ref[...])
        for i in range(width):
            row = width - 1 - i if mirror else i
            head_ref[HALO + i // 8, i % 8 : i % 8 + 1, :] = flux[row : row + 1]

    for copy in copies:
        copy.wait()
    core = lax.axis_index("layer")
    pl.when(core == 0)(lambda: fill(True))
    pl.when(core == 1)(lambda: fill(False))


def start_copies(sources, targets, sems):
    copies = [
        pltpu.make_async_copy(source, target, sems.at[k])
        for k, (source, target) in enumerate(zip(sources, targets))
    ]
    for copy in copies:
        copy.start()
    return copies


def fill_tables(table_ref, row_ref, plane_ref, thick_ref, soft_ref):
    lane = iota((1, LANES), 1)
    tables = [jnp.zeros((1, LANES), jnp.float32)] * 3
    for zone in range(row_ref.shape[0]):
        at = row_ref[zone]
        values = (0.5 * plane_ref[at], 0.5 * thick_ref[at], soft_ref[at])
        tables = [jnp.where(lane == zone, x, t) for x, t in zip(values, tables)]
    for k in range(3):
        table_ref[k : k + 1] = tables[k]


def join_layers(low, high):
    depth = low.shape[0] // 2
    return (
        jnp.concatenate([low[:depth], high[:depth]], axis=0),
        jnp.concatenate([low[depth:], high[depth:]], axis=0),
    )


def pair_sum(value):
    layers = value.shape[0]
    even = iota(value.shape, 0) % 2 == 0
    return value + jnp.where(even, pltpu.roll(value, layers - 1, 0), pltpu.roll(value, 1, 0))


def halves(value):
    return value[:, :LANES] + value[:, LANES:]


def step_row(v, low, high, k_plane, k_thick, source, y_gain, layer_gap, coefs_beside=None):
    layers = v.shape[0]
    layer = iota(v.shape, 0)
    up, down = layers - layer_gap, layer_gap
    from_up = jnp.where(layer < layers - layer_gap, pltpu.roll(v, up, 0) - v, 0.0)
    from_down = jnp.where(layer >= layer_gap, pltpu.roll(v, down, 0) - v, 0.0)
    z_gain = (k_thick + pltpu.roll(k_thick, up, 0)) * from_up
    z_gain = z_gain + (k_thick + pltpu.roll(k_thick, down, 0)) * from_down
    return ((v + source) + (high - low)) + (z_gain + y_gain(v, k_plane, coefs_beside))


def beside(row):
    even, odd = row[:, :LANES], row[:, LANES:]
    return jnp.concatenate([pltpu.roll(odd, 1, 1), pltpu.roll(even, LANES - 1, 1)], axis=1)


def fine_y(v, k, coefs_beside):
    va, vb, ka, kb = v[:, :LANES], v[:, LANES:], k[:, :LANES], k[:, LANES:]
    lane = iota(v.shape, 1)
    inner = (ka + kb) * (vb - va)
    rate, slope = coefs_beside
    v_beside = beside(v)
    drop = jnp.where((lane > 0) & (lane < 2 * LANES - 1), v_beside - v, 0.0)
    outer = (k + (rate + slope * v_beside)) * drop
    return outer + jnp.concatenate([inner, -inner], axis=1)


def coarse_y(v, k, _):
    lane = iota(v.shape, 1)
    from_last = jnp.where(lane > 0, pltpu.roll(v, 1, 1) - v, 0.0)
    from_next = jnp.where(lane < LANES - 1, pltpu.roll(v, LANES - 1, 1) - v, 0.0)
    last = (k + pltpu.roll(k, 1, 1)) * from_last
    return last + (k + pltpu.roll(k, LANES - 1, 1)) * from_next


def outer_mask(core):
    tile, tiles = lax.axis_index("tile"), lax.axis_size("tile")
    at_edge = jnp.where(core == 1, tile == 0, tile == tiles - 1)
    return jnp.where(at_edge, 0.0, 1.0).astype(jnp.float32)


def look_up(table_ref, zone):
    zone = zone.astype(jnp.int32)
    halves_of = (zone[:, :LANES], zone[:, LANES:])
    tables = [jnp.broadcast_to(table_ref[k : k + 1, :], halves_of[0].shape) for k in range(3)]
    plane, thick, soft = (
        jnp.concatenate([pick(t, z) for z in halves_of], axis=1) for t in tables
    )
    return [plane, plane * soft, thick, thick * soft, soft]


def flux_row(head_ref, i):
    return head_ref[HALO + i // 8, i % 8 : i % 8 + 1, :]


def to_source(flux, layers):
    return jnp.where(iota((layers, flux.shape[1]), 0) == 0, flux, 0.0)


def to_coarse(coarse_ref, at, rows):
    sums = []
    for coefs, v, flux in rows:
        sums.append([halves(x) for x in (coefs[0], coefs[2], coefs[4], v, flux)])
    first, second = sums
    for k in range(4):
        coarse_ref[k, at] = 0.125 * pair_sum(first[k] + second[k])
    pair = iota(coarse_ref.shape[2:], 0) < 2
    coarse_ref[4, at] = jnp.where(pair, 0.5 * (first[4] + second[4]), 0.0)


def fine_step(rows, state, load_coef, source, mask):
    v_next = state[rows[0] - 1]
    k_next = load_coef(0, rows[0] - 1) + load_coef(1, rows[0] - 1) * v_next
    high = None
    fresh = {}
    for j in (rows[0] - 1, *rows):
        v, k_plane, low = v_next, k_next, high
        v_next = state[j + 1]
        k_next = load_coef(0, j + 1) + load_coef(1, j + 1) * v_next
        high = (k_plane + k_next) * (v_next - v)
        if j == HALO - 1:
            high = high * mask
        if j >= rows[0]:
            k_thick = load_coef(2, j) + load_coef(3, j) * v
            near = [load_coef(k, j) for k in (4, 5)]
            fresh[j] = step_row(v, low, high, k_plane, k_thick, source(j), fine_y, 1, near)
    return fresh


def interior_kernel(
    own_ref,
    own_tail,
    other_ref,
    row_hbm,
    plane_hbm,
    thick_hbm,
    soft_hbm,
    edge_ref,
    coef_out,
    coarse_ref,
    table_ref,
    v_ref,
    coef_ref,
    row_ref,
    plane_ref,
    thick_ref,
    soft_ref,
    sems,
):
    parameters = (row_ref, plane_ref, thick_ref, soft_ref)
    for copy in start_copies((row_hbm, plane_hbm, thick_hbm, soft_hbm), parameters, sems):
        copy.wait()
    fill_tables(table_ref, *parameters)
    width, layers = v_ref.shape[:2]
    core = lax.axis_index("layer")

    first = core == 0

    def gather():
        rows = []
        for i in range(width):
            a, b = own_ref[i] if i < HALO else own_tail[i - HALO], other_ref[i]
            v, zone = join_layers(jnp.where(first, a, b), jnp.where(first, b, a))
            coefs = look_up(table_ref, zone)
            v_ref[i] = v
            for k, coef in enumerate((*coefs[:4], beside(coefs[0]), beside(coefs[1]))):
                coef_ref[k, i] = coef
                if i < coef_out.shape[1]:
                    coef_out[k, i] = coef
            rows.append((coefs, v, flux_row(own_ref, i)))
            if i % 2:
                to_coarse(coarse_ref, i // 2, rows)
                rows = []

    gather()
    state = {HALO + i: v_ref[i] for i in range(width)}
    for level in range(FINE_STEPS):
        if level:
            state = fine_step(
                range(HALO + level, HALO + width - level),
                state,
                lambda k, j: coef_ref[k, j - HALO],
                lambda j: to_source(flux_row(own_ref, j - HALO), layers),
                None,
            )
        for i in range(2):
            edge_ref[level, i] = state[HALO + level + i]


def edge_kernel(
    recv_ref,
    recv_other,
    own_ref,
    table_ref,
    edge_ref,
    own_coef,
    rest_ref,
    share_ref,
    coarse_ref,
    v_ref,
    coef_ref,
    source_ref,
):
    layers = v_ref.shape[1]
    half = v_ref.shape[0] - HALO
    core = lax.axis_index("layer")
    mask = outer_mask(core)

    first = core == 0

    def gather():
        rows = []
        for j in range(HALO):
            i = HALO - 1 - j
            a, b = recv_ref[i], recv_other[i]
            v, zone = join_layers(jnp.where(first, b, a), jnp.where(first, a, b))
            coefs = look_up(table_ref, zone)
            v_ref[j] = v
            for k, coef in enumerate((*coefs[:4], beside(coefs[0]), beside(coefs[1]))):
                coef_ref[k, j] = coef
            rows.append((coefs, v, flux_row(recv_ref, i)))
            if j % 2:
                if j >= HALO - EDGE:
                    to_coarse(coarse_ref, (j - (HALO - EDGE)) // 2, rows)
                rows = []

    gather()

    for j in range(HALO + FINE_STEPS):
        flux = flux_row(own_ref, j - HALO) if j >= HALO else flux_row(recv_ref, HALO - 1 - j)
        source_ref[j] = to_source(flux, layers)
    source = lambda j: source_ref[j]

    state = {j: v_ref[j] for j in range(HALO)}
    for step in range(1, FINE_STEPS + 1):
        for i in range(2):
            state[HALO + step - 1 + i] = edge_ref[step - 1, i]
        state = fine_step(
            range(step, HALO + step),
            state,
            lambda k, j: own_coef[k, j - HALO] if j >= HALO else coef_ref[k, j],
            source,
            mask,
        )

    even = iota((layers, LANES), 0) % 2 == 0
    restricted = []
    for j in range(HALO - EDGE, HALO + half, 2):
        restricted.append(0.125 * pair_sum(halves(state[j]) + halves(state[j + 1])))
    for i in range(0, len(restricted), 2):
        rest_ref[i // 2] = jnp.where(even, restricted[i], restricted[i + 1])
    for i in range(half):
        share_ref[2 * i] = state[HALO + i][:, :LANES]
        share_ref[2 * i + 1] = state[HALO + i][:, LANES:]
    for k in range(5):
        for i in range(COARSE_STEPS):
            share_ref[2 * half + k * COARSE_STEPS + i] = coarse_ref[k, i]


def coarse_fields(coarse_ref, outer_ref, other_ref):
    own = coarse_ref.shape[1]

    def row(k, j):
        if j < COARSE_STEPS:
            return outer_ref[k, j]
        if j < COARSE_STEPS + own:
            return coarse_ref[k, j - COARSE_STEPS]
        return other_ref[2 * own + k * COARSE_STEPS + own + 2 * COARSE_STEPS - 1 - j]

    return row


def coarse_propagate(state, field, masks):
    count = len(state)
    flux = {j: field(4, j) for j in range(1, count - 1)}
    plane = [field(0, j) for j in range(count)]
    thick = [field(1, j) for j in range(count)]
    soft = [field(2, j) for j in range(count)]
    for step in range(1, COARSE_STEPS + 1):
        k_plane = {
            j: plane[j] * (1.0 + soft[j] * state[j]) for j in range(step - 1, count - step + 1)
        }
        flows = {}
        for j in range(step - 1, count - step):
            flow = (k_plane[j] + k_plane[j + 1]) * (state[j + 1] - state[j])
            flows[j] = flow * masks[j] if j in masks else flow
        fresh = list(state)
        for j in range(step, count - step):
            k_thick = thick[j] * (1.0 + soft[j] * state[j])
            fresh[j] = step_row(
                state[j], flows[j - 1], flows[j], k_plane[j], k_thick, flux[j], coarse_y, 2
            )
        state = fresh
    return state[COARSE_STEPS : count - COARSE_STEPS]


def edge_factors(rows):
    core = lax.axis_index("layer")
    return {
        COARSE_STEPS - 1: outer_mask(core),
        rows - COARSE_STEPS - 1: outer_mask(1 - core),
    }


def expand(slab):
    layers = slab.shape[0]
    even = iota(slab.shape, 0) % 2 == 0
    return [
        jnp.where(even, slab, pltpu.roll(slab, 1, 0)),
        jnp.where(even, pltpu.roll(slab, layers - 1, 0), slab),
    ]


def read_state(refs):
    if len(refs) == 1:
        return [refs[0][j] for j in range(refs[0].shape[0])]
    mine, other = (sum((expand(ref[i]) for i in range(ref.shape[0])), []) for ref in refs)
    return mine + other[::-1]


def unfold_kernel(mine_ref, other_ref, state_ref):
    for j, row in enumerate(read_state((mine_ref, other_ref))):
        state_ref[j] = row


def propagated(refs, state_refs=None):
    field = coarse_fields(*refs)
    rows = refs[0].shape[1] + 2 * COARSE_STEPS
    state = [field(3, j) for j in range(rows)]
    if state_refs:
        first = lax.axis_index("tm") == 0
        state = [jnp.where(first, a, b) for a, b in zip(state, read_state(state_refs))]
    return coarse_propagate(state, field, edge_factors(rows))


def base_kernel(coarse_ref, outer_ref, share_ref, other_ref, base_ref):
    depth, width = base_ref.shape[:2]
    core = lax.axis_index("layer")
    base = propagated((coarse_ref, outer_ref, other_ref))

    def write(mirror):
        for j in range(0, width, 2):
            slabs = []
            for i in (j, j + 1):
                ref, at = (share_ref, i) if i < width // 2 else (other_ref, width - 1 - i)
                slab = jnp.concatenate(
                    [ref[2 * at] - base[j // 2], ref[2 * at + 1] - base[j // 2]], axis=1
                )
                slabs.append(slab[:depth] if mirror else slab[depth:])
            both = join_lanes(jnp.concatenate(slabs, axis=0))
            for i in (0, 1):
                row = width - 1 - (j + i) if mirror else j + i
                base_ref[:, row, :] = both[depth * i : depth * (i + 1)]

    pl.when(core == 0)(lambda: write(True))
    pl.when(core == 1)(lambda: write(False))


def output_kernel(*refs):
    *state_refs, coarse_ref, outer_ref, other_ref, base_ref, out_ref = refs
    depth, width = base_ref.shape[:2]
    core = lax.axis_index("layer")
    moved = propagated((coarse_ref, outer_ref, other_ref), state_refs)
    half = iota(moved[0].shape, 1) // 2

    def write(mirror):
        for j, row in enumerate(moved):
            gain = jnp.concatenate([pick(row, half), pick(row, half + LANES // 2)], axis=1)
            gain = gain[:depth] if mirror else gain[depth:]
            for i in (2 * j, 2 * j + 1):
                at = width - 1 - i if mirror else i
                out_ref[0, :, at, :] = base_ref[:, at, :] + gain

    pl.when(core == 0)(lambda: write(True))
    pl.when(core == 1)(lambda: write(False))


def advance_kernel(state_ref, coarse_ref, outer_ref, share_ref, other_ref, next_ref):
    own = next_ref.shape[0]
    refs = (coarse_ref, outer_ref, other_ref)
    moved, base = propagated(refs, (state_ref,)), propagated(refs)
    for j in range(own):
        pair = []
        for i in (2 * j, 2 * j + 1):
            ref, at = (share_ref, i) if i < own else (other_ref, 2 * own - 1 - i)
            pair.append(ref[2 * at] + ref[2 * at + 1])
        next_ref[j] = moved[j] - base[j] + 0.125 * pair_sum(pair[0] + pair[1])


def layer_swap(value):
    return lax.ppermute(value, "layer", [(0, 1), (1, 0)])


def swap_pairs(pairs):
    return [edge for a, b in pairs for edge in ((a, b), (b, a))]


def tile_swap(value):
    tiles, slices = lax.axis_size("tile"), lax.axis_size("tm")
    at = lambda tile, time, core: (tile * slices + time) * 2 + core
    pairs = [
        (at(t, m, 1), at(t - 1, m, 0)) for t in range(1, tiles) for m in range(slices)
    ]
    for m in range(0, slices - 1, 2):
        pairs.append((at(0, m, 1), at(0, m + 1, 1)))
        pairs.append((at(tiles - 1, m, 0), at(tiles - 1, m + 1, 0)))
    return lax.ppermute(value, ("tile", "tm", "layer"), swap_pairs(pairs))


def time_swap(value, parity):
    slices = lax.axis_size("tm")
    at = lambda time, core: time * 2 + core
    pairs = [
        (at(m, c), at(m + 1, c)) for m in range(parity, slices - 1, 2) for c in range(2)
    ]
    used = {d for pair in pairs for d in pair}
    pairs += [(at(m, 0), at(m, 1)) for m in range(slices) if at(m, 0) not in used]
    return lax.ppermute(value, ("tm", "layer"), swap_pairs(pairs))


def cross_swap(value):
    slices = lax.axis_size("tm")
    pairs = [(m * 2 + c, m * 2 + 3 - c) for m in range(0, slices - 1, 2) for c in range(2)]
    return lax.ppermute(value, ("tm", "layer"), swap_pairs(pairs))


def on_device(u_start, flux, zone_of_cell, zone_row, plane_rate, thick_rate, soften):
    depth, width, length = zone_of_cell.shape
    layers = depth * lax.axis_size("layer")
    half = width // 2
    f32 = jnp.float32
    slabs = lambda *lead: jax.ShapeDtypeStruct((*lead, layers, LANES), f32)
    wide = lambda *lead: jax.ShapeDtypeStruct((*lead, layers, length), f32)

    def call(kernel, out_shape, *operands, name, scratch=(), in_hbm=()):
        spaces = [pltpu.HBM if k in in_hbm else pltpu.VMEM for k in range(len(operands))]
        operands = [
            pltpu.with_memory_space_constraint(x, space) if space is pltpu.HBM else x
            for x, space in zip(operands, spaces)
        ]
        return pl.pallas_call(
            kernel,
            out_shape=out_shape,
            in_specs=[pl.BlockSpec(memory_space=space) for space in spaces],
            out_specs=jax.tree.map(lambda _: VMEM, out_shape),
            scratch_shapes=scratch,
            compiler_params=pltpu.CompilerParams(vmem_limit_bytes=VMEM_BYTES),
            name=name,
        )(*operands)

    u_own = u_start[0]
    own, own_tail, turned = call(
        pack_kernel,
        (wide(HALO + width // 8), wide(width - HALO), wide(width)),
        *(u_own, zone_of_cell, flux[0]),
        name="pack",
        scratch=[
            pltpu.VMEM(u_own.shape, f32),
            pltpu.VMEM(zone_of_cell.shape, jnp.int32),
            pltpu.VMEM(flux.shape[1:], f32),
            pltpu.SemaphoreType.DMA((3,)),
        ],
        in_hbm=range(3),
    )
    other = layer_swap(turned)
    recv, recv_other = tile_swap(own), tile_swap(other[:HALO])

    levels, own_coef, coarse, tables = call(
        interior_kernel,
        (
            wide(FINE_STEPS, 2),
            wide(6, FINE_STEPS + 1),
            slabs(5, half),
            jax.ShapeDtypeStruct((3, LANES), f32),
        ),
        *(own, own_tail, other, zone_row, plane_rate, thick_rate, soften),
        name="interior",
        scratch=[
            pltpu.VMEM((width, layers, length), f32),
            pltpu.VMEM((6, width, layers, length), f32),
            pltpu.SMEM(zone_row.shape, jnp.int32),
            *[pltpu.SMEM(plane_rate.shape, f32)] * 3,
            pltpu.SemaphoreType.DMA((4,)),
        ],
        in_hbm=range(3, 7),
    )
    rest, share, outer = call(
        edge_kernel,
        (
            slabs((half + EDGE) // 4),
            slabs(2 * half + 5 * COARSE_STEPS),
            slabs(5, COARSE_STEPS),
        ),
        *(recv, recv_other, own, tables, levels, own_coef),
        name="edge",
        scratch=[
            pltpu.VMEM((HALO + half, layers, length), f32),
            pltpu.VMEM((6, HALO, layers, length), f32),
            pltpu.VMEM((HALO + FINE_STEPS, layers, length), f32),
        ],
    )

    slices = lax.axis_size("tm")
    position = lax.axis_index("tm")
    state = [rest, rest]
    if slices > 1:
        state = [time_swap(rest, 0), cross_swap(rest)]
    other_share = layer_swap(share)
    base = call(
        base_kernel,
        jax.ShapeDtypeStruct((depth, width, length), f32),
        *(coarse, outer, share, other_share),
        name="base",
    )
    if slices > 2:
        full = slabs(half + 2 * COARSE_STEPS)
        state = [call(unfold_kernel, full, *state, name="unfold")]
    for turn in range(1, slices - 1):
        ended = call(
            advance_kernel,
            slabs(half),
            *(*state, coarse, outer, share, other_share),
            name="advance",
        )
        low = tile_swap(ended[:COARSE_STEPS])
        high = layer_swap(low)
        arrived = time_swap(jnp.concatenate([low[::-1], ended, high], axis=0), turn % 2)
        state = [jnp.where(position == turn + 1, arrived, state[0])]
    return call(
        output_kernel,
        jax.ShapeDtypeStruct((1, depth, width, length), f32),
        *(*state, coarse, outer, other_share, base),
        name="output",
    )


def solution(mesh):
    return jax.shard_map(
        on_device,
        mesh=mesh,
        in_specs=(
            P(("parts", "tm"), "layer", "tile", None),
            P(("parts", "tm"), "tile", None),
            P("layer", "tile", None),
            P(),
            P(),
            P(),
            P(),
        ),
        out_specs=P(("parts", "tm"), "layer", "tile", None),
        check_vma=False,
    )
```

```python
import jax
import jax.numpy as jnp
from jax import lax
from jax.experimental import pallas as pl
from jax.experimental.pallas import tpu as pltpu
from jax.sharding import PartitionSpec as P

FINE_STEPS = 8
COARSE_STEPS = 2
LANES = 128
EDGE = 2 * COARSE_STEPS
HALO = FINE_STEPS + EDGE
VMEM_BYTES = 16 * 2**20
VMEM = pl.BlockSpec(memory_space=pltpu.VMEM)


def iota(shape, dim):
    return lax.broadcasted_iota(jnp.int32, shape, dim)


def pick(table, index):
    return jnp.take_along_axis(table, index, axis=1, mode="promise_in_bounds")


def split_lanes(row):
    rows = row.shape[0]
    lane = iota((rows, LANES), 1)
    low = lane < LANES // 2
    even = (2 * lane) % LANES
    first, second = row[:, :LANES], row[:, LANES:]
    return jnp.concatenate(
        [
            jnp.where(low, pick(first, even), pick(second, even)),
            jnp.where(low, pick(first, even + 1), pick(second, even + 1)),
        ],
        axis=1,
    )


def join_lanes(row):
    rows = row.shape[0]
    lane = iota((rows, LANES), 1)
    is_even = lane % 2 == 0
    half = lane // 2
    even, odd = row[:, :LANES], row[:, LANES:]
    return jnp.concatenate(
        [
            jnp.where(is_even, pick(even, half), pick(odd, half)),
            jnp.where(is_even, pick(even, half + LANES // 2), pick(odd, half + LANES // 2)),
        ],
        axis=1,
    )


def pack_kernel(
    u_hbm, zone_hbm, flux_hbm, head_ref, tail_ref, turned_ref, u_ref, zone_ref, flux_ref, sems
):
    copies = start_copies((u_hbm, zone_hbm, flux_hbm), (u_ref, zone_ref, flux_ref), sems)
    width = u_ref.shape[1]

    def fill(mirror):
        for i in range(width):
            row = width - 1 - i if mirror else i
            slab = jnp.concatenate(
                [u_ref[:, row, :], zone_ref[:, row, :].astype(jnp.float32)], axis=0
            )
            slab = split_lanes(slab)
            turned_ref[width - 1 - i] = slab
            if i < HALO:
                head_ref[i] = slab
            else:
                tail_ref[i - HALO] = slab
        flux = split_lanes(flux_ref[...])
        for i in range(width):
            row = width - 1 - i if mirror else i
            head_ref[HALO + i // 8, i % 8 : i % 8 + 1, :] = flux[row : row + 1]

    for copy in copies:
        copy.wait()
    core = lax.axis_index("layer")
    pl.when(core == 0)(lambda: fill(True))
    pl.when(core == 1)(lambda: fill(False))


def start_copies(sources, targets, sems):
    copies = [
        pltpu.make_async_copy(source, target, sems.at[k])
        for k, (source, target) in enumerate(zip(sources, targets))
    ]
    for copy in copies:
        copy.start()
    return copies


def fill_tables(table_ref, row_ref, plane_ref, thick_ref, soft_ref):
    lane = iota((1, LANES), 1)
    tables = [jnp.zeros((1, LANES), jnp.float32)] * 3
    for zone in range(row_ref.shape[0]):
        at = row_ref[zone]
        values = (0.5 * plane_ref[at], 0.5 * thick_ref[at], soft_ref[at])
        tables = [jnp.where(lane == zone, x, t) for x, t in zip(values, tables)]
    for k in range(3):
        table_ref[k : k + 1] = tables[k]


def join_layers(low, high):
    depth = low.shape[0] // 2
    return (
        jnp.concatenate([low[:depth], high[:depth]], axis=0),
        jnp.concatenate([low[depth:], high[depth:]], axis=0),
    )


def pair_sum(value):
    layers = value.shape[0]
    even = iota(value.shape, 0) % 2 == 0
    return value + jnp.where(even, pltpu.roll(value, layers - 1, 0), pltpu.roll(value, 1, 0))


def halves(value):
    return value[:, :LANES] + value[:, LANES:]


def step_row(v, low, high, k_plane, k_thick, source, y_gain, layer_gap, coefs_beside=None):
    layers = v.shape[0]
    layer = iota(v.shape, 0)
    up, down = layers - layer_gap, layer_gap
    flow = (k_thick + pltpu.roll(k_thick, up, 0)) * (pltpu.roll(v, up, 0) - v)
    flow = jnp.where(layer < layers - layer_gap, flow, 0.0)
    z_gain = flow - pltpu.roll(flow, down, 0)
    return ((v + source) + (high - low)) + (z_gain + y_gain(v, k_plane, coefs_beside))


def beside(row):
    even, odd = row[:, :LANES], row[:, LANES:]
    return jnp.concatenate([pltpu.roll(odd, 1, 1), pltpu.roll(even, LANES - 1, 1)], axis=1)


def fine_y(v, k, coefs_beside):
    va, vb, ka, kb = v[:, :LANES], v[:, LANES:], k[:, :LANES], k[:, LANES:]
    lane = iota(v.shape, 1)
    inner = (ka + kb) * (vb - va)
    rate, slope = coefs_beside
    v_beside = beside(v)
    drop = jnp.where((lane > 0) & (lane < 2 * LANES - 1), v_beside - v, 0.0)
    outer = (k + (rate + slope * v_beside)) * drop
    return outer + jnp.concatenate([inner, -inner], axis=1)


def coarse_y(v, k, _):
    lane = iota(v.shape, 1)
    from_last = jnp.where(lane > 0, pltpu.roll(v, 1, 1) - v, 0.0)
    from_next = jnp.where(lane < LANES - 1, pltpu.roll(v, LANES - 1, 1) - v, 0.0)
    last = (k + pltpu.roll(k, 1, 1)) * from_last
    return last + (k + pltpu.roll(k, LANES - 1, 1)) * from_next


def outer_mask(core):
    tile, tiles = lax.axis_index("tile"), lax.axis_size("tile")
    at_edge = jnp.where(core == 1, tile == 0, tile == tiles - 1)
    return jnp.where(at_edge, 0.0, 1.0).astype(jnp.float32)


def look_up(table_ref, zone):
    zone = zone.astype(jnp.int32)
    halves_of = (zone[:, :LANES], zone[:, LANES:])
    tables = [jnp.broadcast_to(table_ref[k : k + 1, :], halves_of[0].shape) for k in range(3)]
    plane, thick, soft = (
        jnp.concatenate([pick(t, z) for z in halves_of], axis=1) for t in tables
    )
    return [plane, plane * soft, thick, thick * soft, soft]


def flux_row(head_ref, i):
    return head_ref[HALO + i // 8, i % 8 : i % 8 + 1, :]


def to_source(flux, layers):
    return jnp.where(iota((layers, flux.shape[1]), 0) == 0, flux, 0.0)


def to_coarse(coarse_ref, at, rows):
    sums = []
    for coefs, v, flux in rows:
        sums.append([halves(x) for x in (coefs[0], coefs[2], coefs[4], v, flux)])
    first, second = sums
    for k in range(4):
        coarse_ref[k, at] = 0.125 * pair_sum(first[k] + second[k])
    pair = iota(coarse_ref.shape[2:], 0) < 2
    coarse_ref[4, at] = jnp.where(pair, 0.5 * (first[4] + second[4]), 0.0)


def fine_step(rows, state, load_coef, source, mask):
    v_next = state[rows[0] - 1]
    k_next = load_coef(0, rows[0] - 1) + load_coef(1, rows[0] - 1) * v_next
    high = None
    fresh = {}
    for j in (rows[0] - 1, *rows):
        v, k_plane, low = v_next, k_next, high
        v_next = state[j + 1]
        k_next = load_coef(0, j + 1) + load_coef(1, j + 1) * v_next
        high = (k_plane + k_next) * (v_next - v)
        if j == HALO - 1:
            high = high * mask
        if j >= rows[0]:
            k_thick = load_coef(2, j) + load_coef(3, j) * v
            near = [load_coef(k, j) for k in (4, 5)]
            fresh[j] = step_row(v, low, high, k_plane, k_thick, source(j), fine_y, 1, near)
    return fresh


def interior_kernel(
    own_ref,
    own_tail,
    other_ref,
    row_hbm,
    plane_hbm,
    thick_hbm,
    soft_hbm,
    edge_ref,
    coef_out,
    coarse_ref,
    table_ref,
    v_ref,
    coef_ref,
    row_ref,
    plane_ref,
    thick_ref,
    soft_ref,
    sems,
):
    parameters = (row_ref, plane_ref, thick_ref, soft_ref)
    for copy in start_copies((row_hbm, plane_hbm, thick_hbm, soft_hbm), parameters, sems):
        copy.wait()
    fill_tables(table_ref, *parameters)
    width, layers = v_ref.shape[:2]
    core = lax.axis_index("layer")

    first = core == 0

    def gather():
        rows = []
        for i in range(width):
            a, b = own_ref[i] if i < HALO else own_tail[i - HALO], other_ref[i]
            v, zone = join_layers(jnp.where(first, a, b), jnp.where(first, b, a))
            coefs = look_up(table_ref, zone)
            v_ref[i] = v
            for k, coef in enumerate((*coefs[:4], beside(coefs[0]), beside(coefs[1]))):
                coef_ref[k, i] = coef
                if i < coef_out.shape[1]:
                    coef_out[k, i] = coef
            rows.append((coefs, v, flux_row(own_ref, i)))
            if i % 2:
                to_coarse(coarse_ref, i // 2, rows)
                rows = []

    gather()
    state = {HALO + i: v_ref[i] for i in range(width)}
    for level in range(FINE_STEPS):
        if level:
            state = fine_step(
                range(HALO + level, HALO + width - level),
                state,
                lambda k, j: coef_ref[k, j - HALO],
                lambda j: to_source(flux_row(own_ref, j - HALO), layers),
                None,
            )
        for i in range(2):
            edge_ref[level, i] = state[HALO + level + i]


def edge_kernel(
    recv_ref,
    recv_other,
    own_ref,
    table_ref,
    edge_ref,
    own_coef,
    share_ref,
    coarse_ref,
    v_ref,
    coef_ref,
    source_ref,
):
    layers = v_ref.shape[1]
    half = v_ref.shape[0] - HALO
    core = lax.axis_index("layer")
    mask = outer_mask(core)

    first = core == 0

    def gather():
        rows = []
        for j in range(HALO):
            i = HALO - 1 - j
            a, b = recv_ref[i], recv_other[i]
            v, zone = join_layers(jnp.where(first, b, a), jnp.where(first, a, b))
            coefs = look_up(table_ref, zone)
            v_ref[j] = v
            for k, coef in enumerate((*coefs[:4], beside(coefs[0]), beside(coefs[1]))):
                coef_ref[k, j] = coef
            rows.append((coefs, v, flux_row(recv_ref, i)))
            if j % 2:
                if j >= HALO - EDGE:
                    to_coarse(coarse_ref, (j - (HALO - EDGE)) // 2, rows)
                rows = []

    gather()

    for j in range(HALO + FINE_STEPS):
        flux = flux_row(own_ref, j - HALO) if j >= HALO else flux_row(recv_ref, HALO - 1 - j)
        source_ref[j] = to_source(flux, layers)
    source = lambda j: source_ref[j]

    state = {j: v_ref[j] for j in range(HALO)}
    for step in range(1, FINE_STEPS + 1):
        for i in range(2):
            state[HALO + step - 1 + i] = edge_ref[step - 1, i]
        state = fine_step(
            range(step, HALO + step),
            state,
            lambda k, j: own_coef[k, j - HALO] if j >= HALO else coef_ref[k, j],
            source,
            mask,
        )

    for i in range(half):
        share_ref[2 * i] = state[HALO + i][:, :LANES]
        share_ref[2 * i + 1] = state[HALO + i][:, LANES:]
    for k in range(5):
        for i in range(COARSE_STEPS):
            share_ref[2 * half + k * COARSE_STEPS + i] = coarse_ref[k, i]
    even = iota((layers, LANES), 0) % 2 == 0
    restricted = []
    for j in range(HALO - EDGE, HALO + half, 2):
        restricted.append(0.125 * pair_sum(halves(state[j]) + halves(state[j + 1])))
    first = share_ref.shape[0] - len(restricted) // 2
    for i in range(0, len(restricted), 2):
        share_ref[first + i // 2] = jnp.where(even, restricted[i], restricted[i + 1])


def coarse_fields(coarse_ref, outer_ref, other_ref):
    own = coarse_ref.shape[1]

    def row(k, j):
        if j < COARSE_STEPS:
            return outer_ref[k, j]
        if j < COARSE_STEPS + own:
            return coarse_ref[k, j - COARSE_STEPS]
        return other_ref[2 * own + k * COARSE_STEPS + own + 2 * COARSE_STEPS - 1 - j]

    return row


def coarse_propagate(state, field, masks):
    count = len(state)
    flux = {j: field(4, j) for j in range(1, count - 1)}
    plane = [field(0, j) for j in range(count)]
    thick = [field(1, j) for j in range(count)]
    soft = [field(2, j) for j in range(count)]
    for step in range(1, COARSE_STEPS + 1):
        k_plane = {
            j: plane[j] * (1.0 + soft[j] * state[j]) for j in range(step - 1, count - step + 1)
        }
        flows = {}
        for j in range(step - 1, count - step):
            flow = (k_plane[j] + k_plane[j + 1]) * (state[j + 1] - state[j])
            flows[j] = flow * masks[j] if j in masks else flow
        fresh = list(state)
        for j in range(step, count - step):
            k_thick = thick[j] * (1.0 + soft[j] * state[j])
            fresh[j] = step_row(
                state[j], flows[j - 1], flows[j], k_plane[j], k_thick, flux[j], coarse_y, 2
            )
        state = fresh
    return state[COARSE_STEPS : count - COARSE_STEPS]


def edge_factors(rows):
    core = lax.axis_index("layer")
    return {
        COARSE_STEPS - 1: outer_mask(core),
        rows - COARSE_STEPS - 1: outer_mask(1 - core),
    }


def expand(slab):
    layers = slab.shape[0]
    even = iota(slab.shape, 0) % 2 == 0
    return [
        jnp.where(even, slab, pltpu.roll(slab, 1, 0)),
        jnp.where(even, pltpu.roll(slab, layers - 1, 0), slab),
    ]


def read_state(state_ref, rows):
    if state_ref.shape[0] == rows:
        return [state_ref[j] for j in range(rows)]
    count = state_ref.shape[0] // 2
    mine, other = (
        sum((expand(state_ref[i]) for i in range(at, at + count)), []) for at in (0, count)
    )
    return mine + other[::-1]


def unfold_kernel(halves_ref, state_ref):
    for j, row in enumerate(read_state(halves_ref, state_ref.shape[0])):
        state_ref[j] = row


def propagated(refs, state_ref=None):
    field = coarse_fields(*refs)
    rows = refs[0].shape[1] + 2 * COARSE_STEPS
    state = [field(3, j) for j in range(rows)]
    if state_ref is not None:
        first = lax.axis_index("tm") == 0
        state = [jnp.where(first, a, b) for a, b in zip(state, read_state(state_ref, rows))]
    return coarse_propagate(state, field, edge_factors(rows))


def base_kernel(coarse_ref, outer_ref, share_ref, other_ref, base_ref):
    depth, width = base_ref.shape[:2]
    core = lax.axis_index("layer")
    base = propagated((coarse_ref, outer_ref, other_ref))

    def write(mirror):
        for j in range(0, width, 2):
            slabs = []
            for i in (j, j + 1):
                ref, at = (share_ref, i) if i < width // 2 else (other_ref, width - 1 - i)
                slab = jnp.concatenate(
                    [ref[2 * at] - base[j // 2], ref[2 * at + 1] - base[j // 2]], axis=1
                )
                slabs.append(slab[:depth] if mirror else slab[depth:])
            both = join_lanes(jnp.concatenate(slabs, axis=0))
            for i in (0, 1):
                row = width - 1 - (j + i) if mirror else j + i
                base_ref[:, row, :] = both[depth * i : depth * (i + 1)]

    pl.when(core == 0)(lambda: write(True))
    pl.when(core == 1)(lambda: write(False))


def output_kernel(state_ref, coarse_ref, outer_ref, other_ref, base_ref, out_ref):
    depth, width = base_ref.shape[:2]
    core = lax.axis_index("layer")
    moved = propagated((coarse_ref, outer_ref, other_ref), state_ref)
    half = iota(moved[0].shape, 1) // 2

    def write(mirror):
        for j, row in enumerate(moved):
            gain = jnp.concatenate([pick(row, half), pick(row, half + LANES // 2)], axis=1)
            gain = gain[:depth] if mirror else gain[depth:]
            for i in (2 * j, 2 * j + 1):
                at = width - 1 - i if mirror else i
                out_ref[0, :, at, :] = base_ref[:, at, :] + gain

    pl.when(core == 0)(lambda: write(True))
    pl.when(core == 1)(lambda: write(False))


def advance_kernel(state_ref, coarse_ref, outer_ref, share_ref, other_ref, next_ref):
    own = next_ref.shape[0]
    refs = (coarse_ref, outer_ref, other_ref)
    moved, base = propagated(refs, state_ref), propagated(refs)
    for j in range(own):
        pair = []
        for i in (2 * j, 2 * j + 1):
            ref, at = (share_ref, i) if i < own else (other_ref, 2 * own - 1 - i)
            pair.append(ref[2 * at] + ref[2 * at + 1])
        next_ref[j] = moved[j] - base[j] + 0.125 * pair_sum(pair[0] + pair[1])


def layer_swap(value):
    return lax.ppermute(value, "layer", [(0, 1), (1, 0)])


def swap_pairs(pairs):
    return [edge for a, b in pairs for edge in ((a, b), (b, a))]


def tile_swap(value):
    tiles, slices = lax.axis_size("tile"), lax.axis_size("tm")
    at = lambda tile, time, core: (tile * slices + time) * 2 + core
    pairs = [
        (at(t, m, 1), at(t - 1, m, 0)) for t in range(1, tiles) for m in range(slices)
    ]
    for m in range(0, slices - 1, 2):
        pairs.append((at(0, m, 1), at(0, m + 1, 1)))
        pairs.append((at(tiles - 1, m, 0), at(tiles - 1, m + 1, 0)))
    return lax.ppermute(value, ("tile", "tm", "layer"), swap_pairs(pairs))


def time_swap(value, parity):
    slices = lax.axis_size("tm")
    at = lambda time, core: time * 2 + core
    pairs = [
        (at(m, c), at(m + 1, c)) for m in range(parity, slices - 1, 2) for c in range(2)
    ]
    used = {d for pair in pairs for d in pair}
    pairs += [(at(m, 0), at(m, 1)) for m in range(slices) if at(m, 0) not in used]
    return lax.ppermute(value, ("tm", "layer"), swap_pairs(pairs))


def cross_swap(value):
    slices = lax.axis_size("tm")
    pairs = [(m * 2 + c, m * 2 + 3 - c) for m in range(0, slices - 1, 2) for c in range(2)]
    return lax.ppermute(value, ("tm", "layer"), swap_pairs(pairs))


def on_device(u_start, flux, zone_of_cell, zone_row, plane_rate, thick_rate, soften):
    depth, width, length = zone_of_cell.shape
    layers = depth * lax.axis_size("layer")
    half = width // 2
    f32 = jnp.float32
    slabs = lambda *lead: jax.ShapeDtypeStruct((*lead, layers, LANES), f32)
    wide = lambda *lead: jax.ShapeDtypeStruct((*lead, layers, length), f32)

    def call(kernel, out_shape, *operands, name, scratch=(), in_hbm=()):
        spaces = [pltpu.HBM if k in in_hbm else pltpu.VMEM for k in range(len(operands))]
        operands = [
            pltpu.with_memory_space_constraint(x, space) if space is pltpu.HBM else x
            for x, space in zip(operands, spaces)
        ]
        return pl.pallas_call(
            kernel,
            out_shape=out_shape,
            in_specs=[pl.BlockSpec(memory_space=space) for space in spaces],
            out_specs=jax.tree.map(lambda _: VMEM, out_shape),
            scratch_shapes=scratch,
            compiler_params=pltpu.CompilerParams(vmem_limit_bytes=VMEM_BYTES),
            name=name,
        )(*operands)

    u_own = u_start[0]
    own, own_tail, turned = call(
        pack_kernel,
        (wide(HALO + width // 8), wide(width - HALO), wide(width)),
        *(u_own, zone_of_cell, flux[0]),
        name="pack",
        scratch=[
            pltpu.VMEM(u_own.shape, f32),
            pltpu.VMEM(zone_of_cell.shape, jnp.int32),
            pltpu.VMEM(flux.shape[1:], f32),
            pltpu.SemaphoreType.DMA((3,)),
        ],
        in_hbm=range(3),
    )
    other = layer_swap(turned)
    recv, recv_other = tile_swap(own), tile_swap(other[:HALO])

    levels, own_coef, coarse, tables = call(
        interior_kernel,
        (
            wide(FINE_STEPS, 2),
            wide(6, FINE_STEPS + 1),
            slabs(5, half),
            jax.ShapeDtypeStruct((3, LANES), f32),
        ),
        *(own, own_tail, other, zone_row, plane_rate, thick_rate, soften),
        name="interior",
        scratch=[
            pltpu.VMEM((width, layers, length), f32),
            pltpu.VMEM((6, width, layers, length), f32),
            pltpu.SMEM(zone_row.shape, jnp.int32),
            *[pltpu.SMEM(plane_rate.shape, f32)] * 3,
            pltpu.SemaphoreType.DMA((4,)),
        ],
        in_hbm=range(3, 7),
    )
    count = (half + EDGE) // 4
    share, outer = call(
        edge_kernel,
        (slabs(2 * half + 5 * COARSE_STEPS + count), slabs(5, COARSE_STEPS)),
        *(recv, recv_other, own, tables, levels, own_coef),
        name="edge",
        scratch=[
            pltpu.VMEM((HALO + half, layers, length), f32),
            pltpu.VMEM((6, HALO, layers, length), f32),
            pltpu.VMEM((HALO + FINE_STEPS, layers, length), f32),
        ],
    )

    slices = lax.axis_size("tm")
    position = lax.axis_index("tm")
    other_share = layer_swap(share)
    state = cross_swap(jnp.concatenate([other_share[-count:], share[-count:]], axis=0))
    base = call(
        base_kernel,
        jax.ShapeDtypeStruct((depth, width, length), f32),
        *(coarse, outer, share, other_share),
        name="base",
    )
    if slices > 2:
        full = slabs(half + 2 * COARSE_STEPS)
        state = call(unfold_kernel, full, state, name="unfold")
    for turn in range(1, slices - 1):
        ended = call(
            advance_kernel,
            slabs(half),
            *(state, coarse, outer, share, other_share),
            name="advance",
        )
        low = tile_swap(ended[:COARSE_STEPS])
        high = layer_swap(low)
        arrived = time_swap(jnp.concatenate([low[::-1], ended, high], axis=0), turn % 2)
        state = jnp.where(position == turn + 1, arrived, state)
    return call(
        output_kernel,
        jax.ShapeDtypeStruct((1, depth, width, length), f32),
        *(state, coarse, outer, other_share, base),
        name="output",
    )


def solution(mesh):
    return jax.shard_map(
        on_device,
        mesh=mesh,
        in_specs=(
            P(("parts", "tm"), "layer", "tile", None),
            P(("parts", "tm"), "tile", None),
            P("layer", "tile", None),
            P(),
            P(),
            P(),
            P(),
        ),
        out_specs=P(("parts", "tm"), "layer", "tile", None),
        check_vma=False,
    )
```

```python
import jax
import jax.numpy as jnp
from jax import lax
from jax.experimental import pallas as pl
from jax.experimental.pallas import tpu as pltpu
from jax.sharding import PartitionSpec as P

FINE_STEPS = 8
COARSE_STEPS = 2
LANES = 128
EDGE = 2 * COARSE_STEPS
HALO = FINE_STEPS + EDGE
VMEM_BYTES = 16 * 2**20
VMEM = pl.BlockSpec(memory_space=pltpu.VMEM)


def iota(shape, dim):
    return lax.broadcasted_iota(jnp.int32, shape, dim)


def pick(table, index):
    return jnp.take_along_axis(table, index, axis=1, mode="promise_in_bounds")


def split_lanes(row):
    rows = row.shape[0]
    lane = iota((rows, LANES), 1)
    low = lane < LANES // 2
    even = (2 * lane) % LANES
    first, second = row[:, :LANES], row[:, LANES:]
    return jnp.concatenate(
        [
            jnp.where(low, pick(first, even), pick(second, even)),
            jnp.where(low, pick(first, even + 1), pick(second, even + 1)),
        ],
        axis=1,
    )


def join_lanes(row):
    rows = row.shape[0]
    lane = iota((rows, LANES), 1)
    is_even = lane % 2 == 0
    half = lane // 2
    even, odd = row[:, :LANES], row[:, LANES:]
    return jnp.concatenate(
        [
            jnp.where(is_even, pick(even, half), pick(odd, half)),
            jnp.where(is_even, pick(even, half + LANES // 2), pick(odd, half + LANES // 2)),
        ],
        axis=1,
    )


def pack_kernel(
    u_hbm, zone_hbm, flux_hbm, head_ref, tail_ref, turned_ref, u_ref, zone_ref, flux_ref, sems
):
    width = u_ref.shape[1]
    parts = [
        (source.at[:, pl.ds(row, 8)], target.at[:, pl.ds(row, 8)])
        for row in range(0, width, 8)
        for source, target in ((u_hbm, u_ref), (zone_hbm, zone_ref))
    ]
    copies = start_copies(*zip(*parts, (flux_hbm, flux_ref)), sems)

    def fill(mirror):
        for i in range(width):
            row = width - 1 - i if mirror else i
            slab = jnp.concatenate(
                [u_ref[:, row, :], zone_ref[:, row, :].astype(jnp.float32)], axis=0
            )
            slab = split_lanes(slab)
            turned_ref[width - 1 - i] = slab
            if i < HALO:
                head_ref[i] = slab
            else:
                tail_ref[i - HALO] = slab
        flux = split_lanes(flux_ref[...])
        for i in range(width):
            row = width - 1 - i if mirror else i
            head_ref[HALO + i // 8, i % 8 : i % 8 + 1, :] = flux[row : row + 1]

    for copy in copies:
        copy.wait()
    core = lax.axis_index("layer")
    pl.when(core == 0)(lambda: fill(True))
    pl.when(core == 1)(lambda: fill(False))


def start_copies(sources, targets, sems):
    copies = [
        pltpu.make_async_copy(source, target, sems.at[k])
        for k, (source, target) in enumerate(zip(sources, targets))
    ]
    for copy in copies:
        copy.start()
    return copies


def fill_tables(table_ref, row_ref, plane_ref, thick_ref, soft_ref):
    lane = iota((1, LANES), 1)
    tables = [jnp.zeros((1, LANES), jnp.float32)] * 3
    for zone in range(row_ref.shape[0]):
        at = row_ref[zone]
        values = (0.5 * plane_ref[at], 0.5 * thick_ref[at], soft_ref[at])
        tables = [jnp.where(lane == zone, x, t) for x, t in zip(values, tables)]
    for k in range(3):
        table_ref[k : k + 1] = tables[k]


def join_layers(low, high):
    depth = low.shape[0] // 2
    return (
        jnp.concatenate([low[:depth], high[:depth]], axis=0),
        jnp.concatenate([low[depth:], high[depth:]], axis=0),
    )


def pair_sum(value):
    layers = value.shape[0]
    even = iota(value.shape, 0) % 2 == 0
    return value + jnp.where(even, pltpu.roll(value, layers - 1, 0), pltpu.roll(value, 1, 0))


def halves(value):
    return value[:, :LANES] + value[:, LANES:]


def step_row(v, low, high, k_plane, k_thick, source, y_gain, layer_gap, coefs_beside=None):
    layers = v.shape[0]
    layer = iota(v.shape, 0)
    up, down = layers - layer_gap, layer_gap
    flow = (k_thick + pltpu.roll(k_thick, up, 0)) * (pltpu.roll(v, up, 0) - v)
    flow = jnp.where(layer < layers - layer_gap, flow, 0.0)
    z_gain = flow - pltpu.roll(flow, down, 0)
    return ((v + source) + (high - low)) + (z_gain + y_gain(v, k_plane, coefs_beside))


def beside(row):
    even, odd = row[:, :LANES], row[:, LANES:]
    return jnp.concatenate([pltpu.roll(odd, 1, 1), pltpu.roll(even, LANES - 1, 1)], axis=1)


def fine_y(v, k, coefs_beside):
    va, vb, ka, kb = v[:, :LANES], v[:, LANES:], k[:, :LANES], k[:, LANES:]
    lane = iota(v.shape, 1)
    inner = (ka + kb) * (vb - va)
    rate, slope = coefs_beside
    v_beside = beside(v)
    drop = jnp.where((lane > 0) & (lane < 2 * LANES - 1), v_beside - v, 0.0)
    outer = (k + (rate + slope * v_beside)) * drop
    return outer + jnp.concatenate([inner, -inner], axis=1)


def coarse_y(v, k, _):
    lane = iota(v.shape, 1)
    from_last = jnp.where(lane > 0, pltpu.roll(v, 1, 1) - v, 0.0)
    from_next = jnp.where(lane < LANES - 1, pltpu.roll(v, LANES - 1, 1) - v, 0.0)
    last = (k + pltpu.roll(k, 1, 1)) * from_last
    return last + (k + pltpu.roll(k, LANES - 1, 1)) * from_next


def outer_mask(core):
    tile, tiles = lax.axis_index("tile"), lax.axis_size("tile")
    at_edge = jnp.where(core == 1, tile == 0, tile == tiles - 1)
    return jnp.where(at_edge, 0.0, 1.0).astype(jnp.float32)


def look_up(table_ref, zone):
    zone = zone.astype(jnp.int32)
    halves_of = (zone[:, :LANES], zone[:, LANES:])
    tables = [jnp.broadcast_to(table_ref[k : k + 1, :], halves_of[0].shape) for k in range(3)]
    plane, thick, soft = (
        jnp.concatenate([pick(t, z) for z in halves_of], axis=1) for t in tables
    )
    return [plane, plane * soft, thick, thick * soft, soft]


def flux_row(head_ref, i):
    return head_ref[HALO + i // 8, i % 8 : i % 8 + 1, :]


def to_source(flux, layers):
    return jnp.where(iota((layers, flux.shape[1]), 0) == 0, flux, 0.0)


def to_coarse(coarse_ref, at, rows):
    sums = []
    for coefs, v, flux in rows:
        sums.append([halves(x) for x in (coefs[0], coefs[2], coefs[4], v, flux)])
    first, second = sums
    for k in range(4):
        coarse_ref[k, at] = 0.125 * pair_sum(first[k] + second[k])
    pair = iota(coarse_ref.shape[2:], 0) < 2
    coarse_ref[4, at] = jnp.where(pair, 0.5 * (first[4] + second[4]), 0.0)


def fine_step(rows, state, load_coef, source, mask):
    v_next = state[rows[0] - 1]
    k_next = load_coef(0, rows[0] - 1) + load_coef(1, rows[0] - 1) * v_next
    high = None
    fresh = {}
    for j in (rows[0] - 1, *rows):
        v, k_plane, low = v_next, k_next, high
        v_next = state[j + 1]
        k_next = load_coef(0, j + 1) + load_coef(1, j + 1) * v_next
        high = (k_plane + k_next) * (v_next - v)
        if j == HALO - 1:
            high = high * mask
        if j >= rows[0]:
            k_thick = load_coef(2, j) + load_coef(3, j) * v
            near = [load_coef(k, j) for k in (4, 5)]
            fresh[j] = step_row(v, low, high, k_plane, k_thick, source(j), fine_y, 1, near)
    return fresh


def interior_kernel(
    own_ref,
    own_tail,
    other_ref,
    row_hbm,
    plane_hbm,
    thick_hbm,
    soft_hbm,
    edge_ref,
    coef_out,
    coarse_ref,
    table_ref,
    v_ref,
    coef_ref,
    row_ref,
    plane_ref,
    thick_ref,
    soft_ref,
    sems,
):
    parameters = (row_ref, plane_ref, thick_ref, soft_ref)
    for copy in start_copies((row_hbm, plane_hbm, thick_hbm, soft_hbm), parameters, sems):
        copy.wait()
    fill_tables(table_ref, *parameters)
    width, layers = v_ref.shape[:2]
    core = lax.axis_index("layer")

    first = core == 0

    def gather():
        rows = []
        for i in range(width):
            a, b = own_ref[i] if i < HALO else own_tail[i - HALO], other_ref[i]
            v, zone = join_layers(jnp.where(first, a, b), jnp.where(first, b, a))
            coefs = look_up(table_ref, zone)
            v_ref[i] = v
            for k, coef in enumerate((*coefs[:4], beside(coefs[0]), beside(coefs[1]))):
                coef_ref[k, i] = coef
                if i < coef_out.shape[1]:
                    coef_out[k, i] = coef
            rows.append((coefs, v, flux_row(own_ref, i)))
            if i % 2:
                to_coarse(coarse_ref, i // 2, rows)
                rows = []

    gather()
    state = {HALO + i: v_ref[i] for i in range(width)}
    for level in range(FINE_STEPS):
        if level:
            state = fine_step(
                range(HALO + level, HALO + width - level),
                state,
                lambda k, j: coef_ref[k, j - HALO],
                lambda j: to_source(flux_row(own_ref, j - HALO), layers),
                None,
            )
        for i in range(2):
            edge_ref[level, i] = state[HALO + level + i]


def edge_kernel(
    recv_ref,
    recv_other,
    own_ref,
    table_ref,
    edge_ref,
    own_coef,
    rest_ref,
    share_ref,
    coarse_ref,
    v_ref,
    coef_ref,
    source_ref,
):
    layers = v_ref.shape[1]
    half = v_ref.shape[0] - HALO
    core = lax.axis_index("layer")
    mask = outer_mask(core)

    first = core == 0

    def gather():
        rows = []
        for j in range(HALO):
            i = HALO - 1 - j
            a, b = recv_ref[i], recv_other[i]
            v, zone = join_layers(jnp.where(first, b, a), jnp.where(first, a, b))
            coefs = look_up(table_ref, zone)
            v_ref[j] = v
            for k, coef in enumerate((*coefs[:4], beside(coefs[0]), beside(coefs[1]))):
                coef_ref[k, j] = coef
            rows.append((coefs, v, flux_row(recv_ref, i)))
            if j % 2:
                if j >= HALO - EDGE:
                    to_coarse(coarse_ref, (j - (HALO - EDGE)) // 2, rows)
                rows = []

    gather()

    for j in range(HALO + FINE_STEPS):
        flux = flux_row(own_ref, j - HALO) if j >= HALO else flux_row(recv_ref, HALO - 1 - j)
        source_ref[j] = to_source(flux, layers)
    source = lambda j: source_ref[j]

    state = {j: v_ref[j] for j in range(HALO)}
    for step in range(1, FINE_STEPS + 1):
        for i in range(2):
            state[HALO + step - 1 + i] = edge_ref[step - 1, i]
        state = fine_step(
            range(step, HALO + step),
            state,
            lambda k, j: own_coef[k, j - HALO] if j >= HALO else coef_ref[k, j],
            source,
            mask,
        )

    for i in range(half):
        share_ref[2 * i] = state[HALO + i][:, :LANES]
        share_ref[2 * i + 1] = state[HALO + i][:, LANES:]
    for k in range(5):
        for i in range(COARSE_STEPS):
            share_ref[2 * half + k * COARSE_STEPS + i] = coarse_ref[k, i]
    even = iota((layers, LANES), 0) % 2 == 0
    restricted = []
    for j in range(HALO - EDGE, HALO + half, 2):
        restricted.append(0.125 * pair_sum(halves(state[j]) + halves(state[j + 1])))
    for i in range(0, len(restricted), 2):
        rest_ref[i // 2] = jnp.where(even, restricted[i], restricted[i + 1])


def coarse_fields(coarse_ref, outer_ref, other_ref):
    own = coarse_ref.shape[1]

    def row(k, j):
        if j < COARSE_STEPS:
            return outer_ref[k, j]
        if j < COARSE_STEPS + own:
            return coarse_ref[k, j - COARSE_STEPS]
        return other_ref[2 * own + k * COARSE_STEPS + own + 2 * COARSE_STEPS - 1 - j]

    return row


def coarse_propagate(state, field, masks):
    count = len(state)
    flux = {j: field(4, j) for j in range(1, count - 1)}
    plane = [field(0, j) for j in range(count)]
    thick = [field(1, j) for j in range(count)]
    soft = [field(2, j) for j in range(count)]
    for step in range(1, COARSE_STEPS + 1):
        k_plane = {
            j: plane[j] * (1.0 + soft[j] * state[j]) for j in range(step - 1, count - step + 1)
        }
        flows = {}
        for j in range(step - 1, count - step):
            flow = (k_plane[j] + k_plane[j + 1]) * (state[j + 1] - state[j])
            flows[j] = flow * masks[j] if j in masks else flow
        fresh = list(state)
        for j in range(step, count - step):
            k_thick = thick[j] * (1.0 + soft[j] * state[j])
            fresh[j] = step_row(
                state[j], flows[j - 1], flows[j], k_plane[j], k_thick, flux[j], coarse_y, 2
            )
        state = fresh
    return state[COARSE_STEPS : count - COARSE_STEPS]


def edge_factors(rows):
    core = lax.axis_index("layer")
    return {
        COARSE_STEPS - 1: outer_mask(core),
        rows - COARSE_STEPS - 1: outer_mask(1 - core),
    }


def expand(slab):
    layers = slab.shape[0]
    even = iota(slab.shape, 0) % 2 == 0
    return [
        jnp.where(even, slab, pltpu.roll(slab, 1, 0)),
        jnp.where(even, pltpu.roll(slab, layers - 1, 0), slab),
    ]


def read_state(state_ref, rows):
    if state_ref.shape[0] == rows:
        return [state_ref[j] for j in range(rows)]
    count = state_ref.shape[0] // 2
    mine, other = (
        sum((expand(state_ref[i]) for i in range(at, at + count)), []) for at in (0, count)
    )
    return mine + other[::-1]


def unfold_kernel(halves_ref, state_ref):
    for j, row in enumerate(read_state(halves_ref, state_ref.shape[0])):
        state_ref[j] = row


def propagated(refs, state_ref=None):
    field = coarse_fields(*refs)
    rows = refs[0].shape[1] + 2 * COARSE_STEPS
    state = [field(3, j) for j in range(rows)]
    if state_ref is not None:
        first = lax.axis_index("tm") == 0
        state = [jnp.where(first, a, b) for a, b in zip(state, read_state(state_ref, rows))]
    return coarse_propagate(state, field, edge_factors(rows))


def base_kernel(coarse_ref, outer_ref, share_ref, other_ref, base_ref):
    depth, width = base_ref.shape[:2]
    core = lax.axis_index("layer")
    base = propagated((coarse_ref, outer_ref, other_ref))

    def write(mirror):
        for j in range(0, width, 2):
            slabs = []
            for i in (j, j + 1):
                ref, at = (share_ref, i) if i < width // 2 else (other_ref, width - 1 - i)
                slab = jnp.concatenate(
                    [ref[2 * at] - base[j // 2], ref[2 * at + 1] - base[j // 2]], axis=1
                )
                slabs.append(slab[:depth] if mirror else slab[depth:])
            both = join_lanes(jnp.concatenate(slabs, axis=0))
            for i in (0, 1):
                row = width - 1 - (j + i) if mirror else j + i
                base_ref[:, row, :] = both[depth * i : depth * (i + 1)]

    pl.when(core == 0)(lambda: write(True))
    pl.when(core == 1)(lambda: write(False))


def output_kernel(state_ref, coarse_ref, outer_ref, other_ref, base_ref, out_ref):
    depth, width = base_ref.shape[:2]
    core = lax.axis_index("layer")
    moved = propagated((coarse_ref, outer_ref, other_ref), state_ref)
    half = iota(moved[0].shape, 1) // 2

    def write(mirror):
        for j, row in enumerate(moved):
            gain = jnp.concatenate([pick(row, half), pick(row, half + LANES // 2)], axis=1)
            gain = gain[:depth] if mirror else gain[depth:]
            for i in (2 * j, 2 * j + 1):
                at = width - 1 - i if mirror else i
                out_ref[0, :, at, :] = base_ref[:, at, :] + gain

    pl.when(core == 0)(lambda: write(True))
    pl.when(core == 1)(lambda: write(False))


def advance_kernel(state_ref, coarse_ref, outer_ref, share_ref, other_ref, next_ref):
    own = next_ref.shape[0]
    refs = (coarse_ref, outer_ref, other_ref)
    moved, base = propagated(refs, state_ref), propagated(refs)
    for j in range(own):
        pair = []
        for i in (2 * j, 2 * j + 1):
            ref, at = (share_ref, i) if i < own else (other_ref, 2 * own - 1 - i)
            pair.append(ref[2 * at] + ref[2 * at + 1])
        next_ref[j] = moved[j] - base[j] + 0.125 * pair_sum(pair[0] + pair[1])


def layer_swap(value):
    return lax.ppermute(value, "layer", [(0, 1), (1, 0)])


def swap_pairs(pairs):
    return [edge for a, b in pairs for edge in ((a, b), (b, a))]


def tile_swap(value):
    tiles, slices = lax.axis_size("tile"), lax.axis_size("tm")
    at = lambda tile, time, core: (tile * slices + time) * 2 + core
    pairs = [
        (at(t, m, 1), at(t - 1, m, 0)) for t in range(1, tiles) for m in range(slices)
    ]
    for m in range(0, slices - 1, 2):
        pairs.append((at(0, m, 1), at(0, m + 1, 1)))
        pairs.append((at(tiles - 1, m, 0), at(tiles - 1, m + 1, 0)))
    return lax.ppermute(value, ("tile", "tm", "layer"), swap_pairs(pairs))


def time_swap(value, parity):
    slices = lax.axis_size("tm")
    at = lambda time, core: time * 2 + core
    pairs = [
        (at(m, c), at(m + 1, c)) for m in range(parity, slices - 1, 2) for c in range(2)
    ]
    used = {d for pair in pairs for d in pair}
    pairs += [(at(m, 0), at(m, 1)) for m in range(slices) if at(m, 0) not in used]
    return lax.ppermute(value, ("tm", "layer"), swap_pairs(pairs))


def cross_swap(value):
    slices = lax.axis_size("tm")
    pairs = [(m * 2 + c, m * 2 + 3 - c) for m in range(0, slices - 1, 2) for c in range(2)]
    return lax.ppermute(value, ("tm", "layer"), swap_pairs(pairs))


def on_device(u_start, flux, zone_of_cell, zone_row, plane_rate, thick_rate, soften):
    depth, width, length = zone_of_cell.shape
    layers = depth * lax.axis_size("layer")
    half = width // 2
    f32 = jnp.float32
    slabs = lambda *lead: jax.ShapeDtypeStruct((*lead, layers, LANES), f32)
    wide = lambda *lead: jax.ShapeDtypeStruct((*lead, layers, length), f32)

    def call(kernel, out_shape, *operands, name, scratch=(), in_hbm=()):
        spaces = [pltpu.HBM if k in in_hbm else pltpu.VMEM for k in range(len(operands))]
        operands = [
            pltpu.with_memory_space_constraint(x, space) if space is pltpu.HBM else x
            for x, space in zip(operands, spaces)
        ]
        return pl.pallas_call(
            kernel,
            out_shape=out_shape,
            in_specs=[pl.BlockSpec(memory_space=space) for space in spaces],
            out_specs=jax.tree.map(lambda _: VMEM, out_shape),
            scratch_shapes=scratch,
            compiler_params=pltpu.CompilerParams(vmem_limit_bytes=VMEM_BYTES),
            name=name,
        )(*operands)

    u_own = u_start[0]
    own, own_tail, turned = call(
        pack_kernel,
        (wide(HALO + width // 8), wide(width - HALO), wide(width)),
        *(u_own, zone_of_cell, flux[0]),
        name="pack",
        scratch=[
            pltpu.VMEM(u_own.shape, f32),
            pltpu.VMEM(zone_of_cell.shape, jnp.int32),
            pltpu.VMEM(flux.shape[1:], f32),
            pltpu.SemaphoreType.DMA((2 * (width // 8) + 1,)),
        ],
        in_hbm=range(3),
    )
    other = layer_swap(turned)
    recv, recv_other = tile_swap(own), tile_swap(other[:HALO])

    levels, own_coef, coarse, tables = call(
        interior_kernel,
        (
            wide(FINE_STEPS, 2),
            wide(6, FINE_STEPS + 1),
            slabs(5, half),
            jax.ShapeDtypeStruct((3, LANES), f32),
        ),
        *(own, own_tail, other, zone_row, plane_rate, thick_rate, soften),
        name="interior",
        scratch=[
            pltpu.VMEM((width, layers, length), f32),
            pltpu.VMEM((6, width, layers, length), f32),
            pltpu.SMEM(zone_row.shape, jnp.int32),
            *[pltpu.SMEM(plane_rate.shape, f32)] * 3,
            pltpu.SemaphoreType.DMA((4,)),
        ],
        in_hbm=range(3, 7),
    )
    rest, share, outer = call(
        edge_kernel,
        (
            slabs((half + EDGE) // 4),
            slabs(2 * half + 5 * COARSE_STEPS),
            slabs(5, COARSE_STEPS),
        ),
        *(recv, recv_other, own, tables, levels, own_coef),
        name="edge",
        scratch=[
            pltpu.VMEM((HALO + half, layers, length), f32),
            pltpu.VMEM((6, HALO, layers, length), f32),
            pltpu.VMEM((HALO + FINE_STEPS, layers, length), f32),
        ],
    )

    slices = lax.axis_size("tm")
    position = lax.axis_index("tm")
    other_rest, other_share = layer_swap(rest), layer_swap(share)
    state = cross_swap(jnp.concatenate([other_rest, rest], axis=0))
    base = call(
        base_kernel,
        jax.ShapeDtypeStruct((depth, width, length), f32),
        *(coarse, outer, share, other_share),
        name="base",
    )
    if slices > 2:
        full = slabs(half + 2 * COARSE_STEPS)
        state = call(unfold_kernel, full, state, name="unfold")
    for turn in range(1, slices - 1):
        ended = call(
            advance_kernel,
            slabs(half),
            *(state, coarse, outer, share, other_share),
            name="advance",
        )
        low = tile_swap(ended[:COARSE_STEPS])
        high = layer_swap(low)
        arrived = time_swap(jnp.concatenate([low[::-1], ended, high], axis=0), turn % 2)
        state = jnp.where(position == turn + 1, arrived, state)
    return call(
        output_kernel,
        jax.ShapeDtypeStruct((1, depth, width, length), f32),
        *(state, coarse, outer, other_share, base),
        name="output",
    )


def solution(mesh):
    return jax.shard_map(
        on_device,
        mesh=mesh,
        in_specs=(
            P(("parts", "tm"), "layer", "tile", None),
            P(("parts", "tm"), "tile", None),
            P("layer", "tile", None),
            P(),
            P(),
            P(),
            P(),
        ),
        out_specs=P(("parts", "tm"), "layer", "tile", None),
        check_vma=False,
    )
```

```python
import jax
import jax.numpy as jnp
from jax import lax
from jax.experimental import pallas as pl
from jax.experimental.pallas import tpu as pltpu
from jax.sharding import PartitionSpec as P

FINE_STEPS = 8
COARSE_STEPS = 2
LANES = 128
EDGE = 2 * COARSE_STEPS
HALO = FINE_STEPS + EDGE
VMEM_BYTES = 16 * 2**20
VMEM = pl.BlockSpec(memory_space=pltpu.VMEM)


def iota(shape, dim):
    return lax.broadcasted_iota(jnp.int32, shape, dim)


def pick(table, index):
    return jnp.take_along_axis(table, index, axis=1, mode="promise_in_bounds")


def split_lanes(row):
    rows = row.shape[0]
    lane = iota((rows, LANES), 1)
    low = lane < LANES // 2
    even = (2 * lane) % LANES
    first, second = row[:, :LANES], row[:, LANES:]
    return jnp.concatenate(
        [
            jnp.where(low, pick(first, even), pick(second, even)),
            jnp.where(low, pick(first, even + 1), pick(second, even + 1)),
        ],
        axis=1,
    )


def join_lanes(row):
    rows = row.shape[0]
    lane = iota((rows, LANES), 1)
    is_even = lane % 2 == 0
    half = lane // 2
    even, odd = row[:, :LANES], row[:, LANES:]
    return jnp.concatenate(
        [
            jnp.where(is_even, pick(even, half), pick(odd, half)),
            jnp.where(is_even, pick(even, half + LANES // 2), pick(odd, half + LANES // 2)),
        ],
        axis=1,
    )


def pack_kernel(
    u_hbm, zone_hbm, flux_hbm, head_ref, tail_ref, turned_ref, u_ref, zone_ref, flux_ref, sems
):
    width = u_ref.shape[1]
    parts = [
        (source.at[:, pl.ds(row, 8)], target.at[:, pl.ds(row, 8)])
        for row in range(0, width, 8)
        for source, target in ((u_hbm, u_ref), (zone_hbm, zone_ref))
    ]
    copies = start_copies(*zip(*parts, (flux_hbm, flux_ref)), sems)

    def fill(mirror):
        for i in range(width):
            row = width - 1 - i if mirror else i
            slab = jnp.concatenate(
                [u_ref[:, row, :], zone_ref[:, row, :].astype(jnp.float32)], axis=0
            )
            slab = split_lanes(slab)
            turned_ref[width - 1 - i] = slab
            if i < HALO:
                head_ref[i] = slab
            else:
                tail_ref[i - HALO] = slab
        flux = split_lanes(flux_ref[...])
        for i in range(width):
            row = width - 1 - i if mirror else i
            head_ref[HALO + i // 8, i % 8 : i % 8 + 1, :] = flux[row : row + 1]

    for copy in copies:
        copy.wait()
    core = lax.axis_index("layer")
    pl.when(core == 0)(lambda: fill(True))
    pl.when(core == 1)(lambda: fill(False))


def start_copies(sources, targets, sems):
    copies = [
        pltpu.make_async_copy(source, target, sems.at[k])
        for k, (source, target) in enumerate(zip(sources, targets))
    ]
    for copy in copies:
        copy.start()
    return copies


def fill_tables(table_ref, row_ref, plane_ref, thick_ref, soft_ref):
    lane = iota((1, LANES), 1)
    tables = [jnp.zeros((1, LANES), jnp.float32)] * 3
    for zone in range(row_ref.shape[0]):
        at = row_ref[zone]
        values = (0.5 * plane_ref[at], 0.5 * thick_ref[at], soft_ref[at])
        tables = [jnp.where(lane == zone, x, t) for x, t in zip(values, tables)]
    for k in range(3):
        table_ref[k : k + 1] = tables[k]


def join_layers(low, high):
    depth = low.shape[0] // 2
    return (
        jnp.concatenate([low[:depth], high[:depth]], axis=0),
        jnp.concatenate([low[depth:], high[depth:]], axis=0),
    )


def pair_sum(value):
    layers = value.shape[0]
    even = iota(value.shape, 0) % 2 == 0
    return value + jnp.where(even, pltpu.roll(value, layers - 1, 0), pltpu.roll(value, 1, 0))


def halves(value):
    return value[:, :LANES] + value[:, LANES:]


def step_row(v, low, high, k_plane, k_thick, source, y_gain, layer_gap, coefs_beside=None):
    layers = v.shape[0]
    layer = iota(v.shape, 0)
    up, down = layers - layer_gap, layer_gap
    flow = (k_thick + pltpu.roll(k_thick, up, 0)) * (pltpu.roll(v, up, 0) - v)
    flow = jnp.where(layer < layers - layer_gap, flow, 0.0)
    z_gain = flow - pltpu.roll(flow, down, 0)
    return ((v + source) + (high - low)) + (z_gain + y_gain(v, k_plane, coefs_beside))


def beside(row):
    even, odd = row[:, :LANES], row[:, LANES:]
    return jnp.concatenate([pltpu.roll(odd, 1, 1), pltpu.roll(even, LANES - 1, 1)], axis=1)


def fine_y(v, k, coefs_beside):
    va, vb, ka, kb = v[:, :LANES], v[:, LANES:], k[:, :LANES], k[:, LANES:]
    lane = iota(v.shape, 1)
    inner = (ka + kb) * (vb - va)
    rate, slope = coefs_beside
    v_beside = beside(v)
    drop = jnp.where((lane > 0) & (lane < 2 * LANES - 1), v_beside - v, 0.0)
    outer = (k + (rate + slope * v_beside)) * drop
    return outer + jnp.concatenate([inner, -inner], axis=1)


def coarse_y(v, k, _):
    lane = iota(v.shape, 1)
    from_last = jnp.where(lane > 0, pltpu.roll(v, 1, 1) - v, 0.0)
    from_next = jnp.where(lane < LANES - 1, pltpu.roll(v, LANES - 1, 1) - v, 0.0)
    last = (k + pltpu.roll(k, 1, 1)) * from_last
    return last + (k + pltpu.roll(k, LANES - 1, 1)) * from_next


def outer_mask(core):
    tile, tiles = lax.axis_index("tile"), lax.axis_size("tile")
    at_edge = jnp.where(core == 1, tile == 0, tile == tiles - 1)
    return jnp.where(at_edge, 0.0, 1.0).astype(jnp.float32)


def look_up(table_ref, zone):
    zone = zone.astype(jnp.int32)
    halves_of = (zone[:, :LANES], zone[:, LANES:])
    tables = [jnp.broadcast_to(table_ref[k : k + 1, :], halves_of[0].shape) for k in range(3)]
    plane, thick, soft = (
        jnp.concatenate([pick(t, z) for z in halves_of], axis=1) for t in tables
    )
    return [plane, plane * soft, thick, thick * soft, soft]


def flux_row(head_ref, i):
    return head_ref[HALO + i // 8, i % 8 : i % 8 + 1, :]


def to_source(flux, layers):
    return jnp.where(iota((layers, flux.shape[1]), 0) == 0, flux, 0.0)


def to_coarse(coarse_ref, at, rows):
    sums = []
    for coefs, v, flux in rows:
        sums.append([halves(x) for x in (coefs[0], coefs[2], coefs[4], v, flux)])
    first, second = sums
    for k in range(4):
        coarse_ref[k, at] = 0.125 * pair_sum(first[k] + second[k])
    pair = iota(coarse_ref.shape[2:], 0) < 2
    coarse_ref[4, at] = jnp.where(pair, 0.5 * (first[4] + second[4]), 0.0)


def fine_step(rows, state, load_coef, source, mask):
    v_next = state[rows[0] - 1]
    k_next = load_coef(0, rows[0] - 1) + load_coef(1, rows[0] - 1) * v_next
    high = None
    fresh = {}
    for j in (rows[0] - 1, *rows):
        v, k_plane, low = v_next, k_next, high
        v_next = state[j + 1]
        k_next = load_coef(0, j + 1) + load_coef(1, j + 1) * v_next
        high = (k_plane + k_next) * (v_next - v)
        if j == HALO - 1:
            high = high * mask
        if j >= rows[0]:
            k_thick = load_coef(2, j) + load_coef(3, j) * v
            near = [load_coef(k, j) for k in (4, 5)]
            fresh[j] = step_row(v, low, high, k_plane, k_thick, source(j), fine_y, 1, near)
    return fresh


def interior_kernel(
    own_ref,
    own_tail,
    other_ref,
    row_hbm,
    plane_hbm,
    thick_hbm,
    soft_hbm,
    edge_ref,
    coef_out,
    coarse_ref,
    table_ref,
    v_ref,
    coef_ref,
    row_ref,
    plane_ref,
    thick_ref,
    soft_ref,
    sems,
):
    parameters = (row_ref, plane_ref, thick_ref, soft_ref)
    for copy in start_copies((row_hbm, plane_hbm, thick_hbm, soft_hbm), parameters, sems):
        copy.wait()
    fill_tables(table_ref, *parameters)
    width, layers = v_ref.shape[:2]
    core = lax.axis_index("layer")

    first = core == 0

    def gather():
        rows = []
        for i in range(width):
            a, b = own_ref[i] if i < HALO else own_tail[i - HALO], other_ref[i]
            v, zone = join_layers(jnp.where(first, a, b), jnp.where(first, b, a))
            coefs = look_up(table_ref, zone)
            v_ref[i] = v
            for k, coef in enumerate((*coefs[:4], beside(coefs[0]), beside(coefs[1]))):
                coef_ref[k, i] = coef
                if i < coef_out.shape[1]:
                    coef_out[k, i] = coef
            rows.append((coefs, v, flux_row(own_ref, i)))
            if i % 2:
                to_coarse(coarse_ref, i // 2, rows)
                rows = []

    gather()
    state = {HALO + i: v_ref[i] for i in range(width)}
    for level in range(FINE_STEPS):
        if level:
            state = fine_step(
                range(HALO + level, HALO + width - level),
                state,
                lambda k, j: coef_ref[k, j - HALO],
                lambda j: to_source(flux_row(own_ref, j - HALO), layers),
                None,
            )
        for i in range(2):
            edge_ref[level, i] = state[HALO + level + i]


def edge_kernel(
    recv_ref,
    recv_other,
    own_ref,
    table_ref,
    edge_ref,
    own_coef,
    rest_ref,
    share_ref,
    coarse_ref,
    v_ref,
    coef_ref,
    source_ref,
):
    layers = v_ref.shape[1]
    half = v_ref.shape[0] - HALO
    core = lax.axis_index("layer")
    mask = outer_mask(core)

    first = core == 0

    def gather():
        rows = []
        for j in range(HALO):
            i = HALO - 1 - j
            a, b = recv_ref[i], recv_other[i]
            v, zone = join_layers(jnp.where(first, b, a), jnp.where(first, a, b))
            coefs = look_up(table_ref, zone)
            v_ref[j] = v
            for k, coef in enumerate((*coefs[:4], beside(coefs[0]), beside(coefs[1]))):
                coef_ref[k, j] = coef
            rows.append((coefs, v, flux_row(recv_ref, i)))
            if j % 2:
                if j >= HALO - EDGE:
                    to_coarse(coarse_ref, (j - (HALO - EDGE)) // 2, rows)
                rows = []

    gather()

    for j in range(HALO + FINE_STEPS):
        flux = flux_row(own_ref, j - HALO) if j >= HALO else flux_row(recv_ref, HALO - 1 - j)
        source_ref[j] = to_source(flux, layers)
    source = lambda j: source_ref[j]

    state = {j: v_ref[j] for j in range(HALO)}
    for step in range(1, FINE_STEPS + 1):
        for i in range(2):
            state[HALO + step - 1 + i] = edge_ref[step - 1, i]
        state = fine_step(
            range(step, HALO + step),
            state,
            lambda k, j: own_coef[k, j - HALO] if j >= HALO else coef_ref[k, j],
            source,
            mask,
        )

    for i in range(half):
        share_ref[2 * i] = state[HALO + i][:, :LANES]
        share_ref[2 * i + 1] = state[HALO + i][:, LANES:]
    for k in range(5):
        for i in range(COARSE_STEPS):
            share_ref[2 * half + k * COARSE_STEPS + i] = coarse_ref[k, i]
    even = iota((layers, LANES), 0) % 2 == 0
    restricted = []
    for j in range(HALO - EDGE, HALO + half, 2):
        restricted.append(0.125 * pair_sum(halves(state[j]) + halves(state[j + 1])))
    for i in range(0, len(restricted), 2):
        rest_ref[i // 2] = jnp.where(even, restricted[i], restricted[i + 1])


def coarse_fields(coarse_ref, outer_ref, other_ref):
    own = coarse_ref.shape[1]

    def row(k, j):
        if j < COARSE_STEPS:
            return outer_ref[k, j]
        if j < COARSE_STEPS + own:
            return coarse_ref[k, j - COARSE_STEPS]
        return other_ref[2 * own + k * COARSE_STEPS + own + 2 * COARSE_STEPS - 1 - j]

    return row


def coarse_propagate(state, field, masks):
    count = len(state)
    flux = {j: field(4, j) for j in range(1, count - 1)}
    plane = [field(0, j) for j in range(count)]
    thick = [field(1, j) for j in range(count)]
    plane_slope = [field(2, j) * plane[j] for j in range(count)]
    thick_slope = [field(2, j) * thick[j] for j in range(count)]
    for step in range(1, COARSE_STEPS + 1):
        k_plane = {
            j: plane[j] + plane_slope[j] * state[j] for j in range(step - 1, count - step + 1)
        }
        flows = {}
        for j in range(step - 1, count - step):
            flow = (k_plane[j] + k_plane[j + 1]) * (state[j + 1] - state[j])
            flows[j] = flow * masks[j] if j in masks else flow
        fresh = list(state)
        for j in range(step, count - step):
            k_thick = thick[j] + thick_slope[j] * state[j]
            fresh[j] = step_row(
                state[j], flows[j - 1], flows[j], k_plane[j], k_thick, flux[j], coarse_y, 2
            )
        state = fresh
    return state[COARSE_STEPS : count - COARSE_STEPS]


def edge_factors(rows):
    core = lax.axis_index("layer")
    return {
        COARSE_STEPS - 1: outer_mask(core),
        rows - COARSE_STEPS - 1: outer_mask(1 - core),
    }


def expand(slab):
    layers = slab.shape[0]
    even = iota(slab.shape, 0) % 2 == 0
    return [
        jnp.where(even, slab, pltpu.roll(slab, 1, 0)),
        jnp.where(even, pltpu.roll(slab, layers - 1, 0), slab),
    ]


def read_state(state_ref, rows):
    if state_ref.shape[0] == rows:
        return [state_ref[j] for j in range(rows)]
    count = state_ref.shape[0] // 2
    mine, other = (
        sum((expand(state_ref[i]) for i in range(at, at + count)), []) for at in (0, count)
    )
    return mine + other[::-1]


def unfold_kernel(halves_ref, state_ref):
    for j, row in enumerate(read_state(halves_ref, state_ref.shape[0])):
        state_ref[j] = row


def propagated(refs, state_ref=None):
    field = coarse_fields(*refs)
    rows = refs[0].shape[1] + 2 * COARSE_STEPS
    state = [field(3, j) for j in range(rows)]
    if state_ref is not None:
        first = lax.axis_index("tm") == 0
        state = [jnp.where(first, a, b) for a, b in zip(state, read_state(state_ref, rows))]
    return coarse_propagate(state, field, edge_factors(rows))


def base_kernel(coarse_ref, outer_ref, share_ref, other_ref, base_ref):
    depth, width = base_ref.shape[:2]
    core = lax.axis_index("layer")
    base = propagated((coarse_ref, outer_ref, other_ref))

    def write(mirror):
        for j in range(0, width, 2):
            slabs = []
            for i in (j, j + 1):
                ref, at = (share_ref, i) if i < width // 2 else (other_ref, width - 1 - i)
                slab = jnp.concatenate(
                    [ref[2 * at] - base[j // 2], ref[2 * at + 1] - base[j // 2]], axis=1
                )
                slabs.append(slab[:depth] if mirror else slab[depth:])
            both = join_lanes(jnp.concatenate(slabs, axis=0))
            for i in (0, 1):
                row = width - 1 - (j + i) if mirror else j + i
                base_ref[:, row, :] = both[depth * i : depth * (i + 1)]

    pl.when(core == 0)(lambda: write(True))
    pl.when(core == 1)(lambda: write(False))


def output_kernel(state_ref, coarse_ref, outer_ref, other_ref, base_ref, out_ref):
    depth, width = base_ref.shape[:2]
    core = lax.axis_index("layer")
    moved = propagated((coarse_ref, outer_ref, other_ref), state_ref)
    half = iota(moved[0].shape, 1) // 2

    def write(mirror):
        for j, row in enumerate(moved):
            gain = jnp.concatenate([pick(row, half), pick(row, half + LANES // 2)], axis=1)
            gain = gain[:depth] if mirror else gain[depth:]
            for i in (2 * j, 2 * j + 1):
                at = width - 1 - i if mirror else i
                out_ref[0, :, at, :] = base_ref[:, at, :] + gain

    pl.when(core == 0)(lambda: write(True))
    pl.when(core == 1)(lambda: write(False))


def advance_kernel(state_ref, coarse_ref, outer_ref, share_ref, other_ref, next_ref):
    own = next_ref.shape[0]
    refs = (coarse_ref, outer_ref, other_ref)
    moved, base = propagated(refs, state_ref), propagated(refs)
    for j in range(own):
        pair = []
        for i in (2 * j, 2 * j + 1):
            ref, at = (share_ref, i) if i < own else (other_ref, 2 * own - 1 - i)
            pair.append(ref[2 * at] + ref[2 * at + 1])
        next_ref[j] = moved[j] - base[j] + 0.125 * pair_sum(pair[0] + pair[1])


def layer_swap(value):
    return lax.ppermute(value, "layer", [(0, 1), (1, 0)])


def swap_pairs(pairs):
    return [edge for a, b in pairs for edge in ((a, b), (b, a))]


def tile_swap(value):
    tiles, slices = lax.axis_size("tile"), lax.axis_size("tm")
    at = lambda tile, time, core: (tile * slices + time) * 2 + core
    pairs = [
        (at(t, m, 1), at(t - 1, m, 0)) for t in range(1, tiles) for m in range(slices)
    ]
    for m in range(0, slices - 1, 2):
        pairs.append((at(0, m, 1), at(0, m + 1, 1)))
        pairs.append((at(tiles - 1, m, 0), at(tiles - 1, m + 1, 0)))
    return lax.ppermute(value, ("tile", "tm", "layer"), swap_pairs(pairs))


def time_swap(value, parity):
    slices = lax.axis_size("tm")
    at = lambda time, core: time * 2 + core
    pairs = [
        (at(m, c), at(m + 1, c)) for m in range(parity, slices - 1, 2) for c in range(2)
    ]
    used = {d for pair in pairs for d in pair}
    pairs += [(at(m, 0), at(m, 1)) for m in range(slices) if at(m, 0) not in used]
    return lax.ppermute(value, ("tm", "layer"), swap_pairs(pairs))


def cross_swap(value):
    slices = lax.axis_size("tm")
    pairs = [(m * 2 + c, m * 2 + 3 - c) for m in range(0, slices - 1, 2) for c in range(2)]
    return lax.ppermute(value, ("tm", "layer"), swap_pairs(pairs))


def on_device(u_start, flux, zone_of_cell, zone_row, plane_rate, thick_rate, soften):
    depth, width, length = zone_of_cell.shape
    layers = depth * lax.axis_size("layer")
    half = width // 2
    f32 = jnp.float32
    slabs = lambda *lead: jax.ShapeDtypeStruct((*lead, layers, LANES), f32)
    wide = lambda *lead: jax.ShapeDtypeStruct((*lead, layers, length), f32)

    def call(kernel, out_shape, *operands, name, scratch=(), in_hbm=()):
        spaces = [pltpu.HBM if k in in_hbm else pltpu.VMEM for k in range(len(operands))]
        operands = [
            pltpu.with_memory_space_constraint(x, space) if space is pltpu.HBM else x
            for x, space in zip(operands, spaces)
        ]
        return pl.pallas_call(
            kernel,
            out_shape=out_shape,
            in_specs=[pl.BlockSpec(memory_space=space) for space in spaces],
            out_specs=jax.tree.map(lambda _: VMEM, out_shape),
            scratch_shapes=scratch,
            compiler_params=pltpu.CompilerParams(vmem_limit_bytes=VMEM_BYTES),
            name=name,
        )(*operands)

    u_own = u_start[0]
    own, own_tail, turned = call(
        pack_kernel,
        (wide(HALO + width // 8), wide(width - HALO), wide(width)),
        *(u_own, zone_of_cell, flux[0]),
        name="pack",
        scratch=[
            pltpu.VMEM(u_own.shape, f32),
            pltpu.VMEM(zone_of_cell.shape, jnp.int32),
            pltpu.VMEM(flux.shape[1:], f32),
            pltpu.SemaphoreType.DMA((2 * (width // 8) + 1,)),
        ],
        in_hbm=range(3),
    )
    other = layer_swap(turned)
    recv, recv_other = tile_swap(own), tile_swap(other[:HALO])

    levels, own_coef, coarse, tables = call(
        interior_kernel,
        (
            wide(FINE_STEPS, 2),
            wide(6, FINE_STEPS + 1),
            slabs(5, half),
            jax.ShapeDtypeStruct((3, LANES), f32),
        ),
        *(own, own_tail, other, zone_row, plane_rate, thick_rate, soften),
        name="interior",
        scratch=[
            pltpu.VMEM((width, layers, length), f32),
            pltpu.VMEM((6, width, layers, length), f32),
            pltpu.SMEM(zone_row.shape, jnp.int32),
            *[pltpu.SMEM(plane_rate.shape, f32)] * 3,
            pltpu.SemaphoreType.DMA((4,)),
        ],
        in_hbm=range(3, 7),
    )
    rest, share, outer = call(
        edge_kernel,
        (
            slabs((half + EDGE) // 4),
            slabs(2 * half + 5 * COARSE_STEPS),
            slabs(5, COARSE_STEPS),
        ),
        *(recv, recv_other, own, tables, levels, own_coef),
        name="edge",
        scratch=[
            pltpu.VMEM((HALO + half, layers, length), f32),
            pltpu.VMEM((6, HALO, layers, length), f32),
            pltpu.VMEM((HALO + FINE_STEPS, layers, length), f32),
        ],
    )

    slices = lax.axis_size("tm")
    position = lax.axis_index("tm")
    other_rest, other_share = layer_swap(rest), layer_swap(share)
    state = cross_swap(jnp.concatenate([other_rest, rest], axis=0))
    base = call(
        base_kernel,
        jax.ShapeDtypeStruct((depth, width, length), f32),
        *(coarse, outer, share, other_share),
        name="base",
    )
    if slices > 2:
        full = slabs(half + 2 * COARSE_STEPS)
        state = call(unfold_kernel, full, state, name="unfold")
    for turn in range(1, slices - 1):
        ended = call(
            advance_kernel,
            slabs(half),
            *(state, coarse, outer, share, other_share),
            name="advance",
        )
        low = tile_swap(ended[:COARSE_STEPS])
        high = layer_swap(low)
        arrived = time_swap(jnp.concatenate([low[::-1], ended, high], axis=0), turn % 2)
        state = jnp.where(position == turn + 1, arrived, state)
    return call(
        output_kernel,
        jax.ShapeDtypeStruct((1, depth, width, length), f32),
        *(state, coarse, outer, other_share, base),
        name="output",
    )


def solution(mesh):
    return jax.shard_map(
        on_device,
        mesh=mesh,
        in_specs=(
            P(("parts", "tm"), "layer", "tile", None),
            P(("parts", "tm"), "tile", None),
            P("layer", "tile", None),
            P(),
            P(),
            P(),
            P(),
        ),
        out_specs=P(("parts", "tm"), "layer", "tile", None),
        check_vma=False,
    )
```

```python
import jax
import jax.numpy as jnp
from jax import lax
from jax.experimental import pallas as pl
from jax.experimental.pallas import tpu as pltpu
from jax.sharding import PartitionSpec as P

FINE_STEPS = 8
COARSE_STEPS = 2
LANES = 128
EDGE = 2 * COARSE_STEPS
HALO = FINE_STEPS + EDGE
VMEM_BYTES = 16 * 2**20
VMEM = pl.BlockSpec(memory_space=pltpu.VMEM)


def iota(shape, dim):
    return lax.broadcasted_iota(jnp.int32, shape, dim)


def pick(table, index):
    return jnp.take_along_axis(table, index, axis=1, mode="promise_in_bounds")


def split_lanes(row):
    rows = row.shape[0]
    lane = iota((rows, LANES), 1)
    low = lane < LANES // 2
    even = (2 * lane) % LANES
    first, second = row[:, :LANES], row[:, LANES:]
    return jnp.concatenate(
        [
            jnp.where(low, pick(first, even), pick(second, even)),
            jnp.where(low, pick(first, even + 1), pick(second, even + 1)),
        ],
        axis=1,
    )


def join_lanes(row):
    rows = row.shape[0]
    lane = iota((rows, LANES), 1)
    is_even = lane % 2 == 0
    half = lane // 2
    even, odd = row[:, :LANES], row[:, LANES:]
    return jnp.concatenate(
        [
            jnp.where(is_even, pick(even, half), pick(odd, half)),
            jnp.where(is_even, pick(even, half + LANES // 2), pick(odd, half + LANES // 2)),
        ],
        axis=1,
    )


def pack_kernel(
    u_hbm, zone_hbm, flux_hbm, head_ref, tail_ref, turned_head, turned_tail, u_ref, zone_ref, flux_ref, sems
):
    width = u_ref.shape[1]
    parts = [
        (source.at[:, pl.ds(row, 8)], target.at[:, pl.ds(row, 8)])
        for row in range(0, width, 8)
        for source, target in ((u_hbm, u_ref), (zone_hbm, zone_ref))
    ]
    copies = start_copies(*zip(*parts, (flux_hbm, flux_ref)), sems)

    def fill(mirror):
        for i in range(width):
            row = width - 1 - i if mirror else i
            slab = jnp.concatenate(
                [u_ref[:, row, :], zone_ref[:, row, :].astype(jnp.float32)], axis=0
            )
            slab = split_lanes(slab)
            at = width - 1 - i
            if at < HALO:
                turned_head[at] = slab
            else:
                turned_tail[at - HALO] = slab
            if i < HALO:
                head_ref[i] = slab
            else:
                tail_ref[i - HALO] = slab
        flux = split_lanes(flux_ref[...])
        for i in range(width):
            row = width - 1 - i if mirror else i
            head_ref[HALO + i // 8, i % 8 : i % 8 + 1, :] = flux[row : row + 1]

    for copy in copies:
        copy.wait()
    core = lax.axis_index("layer")
    pl.when(core == 0)(lambda: fill(True))
    pl.when(core == 1)(lambda: fill(False))


def start_copies(sources, targets, sems):
    copies = [
        pltpu.make_async_copy(source, target, sems.at[k])
        for k, (source, target) in enumerate(zip(sources, targets))
    ]
    for copy in copies:
        copy.start()
    return copies


def fill_tables(table_ref, row_ref, plane_ref, thick_ref, soft_ref):
    lane = iota((1, LANES), 1)
    tables = [jnp.zeros((1, LANES), jnp.float32)] * 3
    for zone in range(row_ref.shape[0]):
        at = row_ref[zone]
        values = (0.5 * plane_ref[at], 0.5 * thick_ref[at], soft_ref[at])
        tables = [jnp.where(lane == zone, x, t) for x, t in zip(values, tables)]
    for k in range(3):
        table_ref[k : k + 1] = tables[k]


def join_layers(low, high):
    depth = low.shape[0] // 2
    return (
        jnp.concatenate([low[:depth], high[:depth]], axis=0),
        jnp.concatenate([low[depth:], high[depth:]], axis=0),
    )


def pair_sum(value):
    layers = value.shape[0]
    even = iota(value.shape, 0) % 2 == 0
    return value + jnp.where(even, pltpu.roll(value, layers - 1, 0), pltpu.roll(value, 1, 0))


def halves(value):
    return value[:, :LANES] + value[:, LANES:]


def step_row(v, low, high, k_plane, k_thick, source, y_gain, layer_gap, coefs_beside=None):
    layers = v.shape[0]
    layer = iota(v.shape, 0)
    up, down = layers - layer_gap, layer_gap
    flow = (k_thick + pltpu.roll(k_thick, up, 0)) * (pltpu.roll(v, up, 0) - v)
    flow = jnp.where(layer < layers - layer_gap, flow, 0.0)
    z_gain = flow - pltpu.roll(flow, down, 0)
    return ((v + source) + (high - low)) + (z_gain + y_gain(v, k_plane, coefs_beside))


def beside(row):
    even, odd = row[:, :LANES], row[:, LANES:]
    return jnp.concatenate([pltpu.roll(odd, 1, 1), pltpu.roll(even, LANES - 1, 1)], axis=1)


def fine_y(v, k, coefs_beside):
    va, vb, ka, kb = v[:, :LANES], v[:, LANES:], k[:, :LANES], k[:, LANES:]
    lane = iota(v.shape, 1)
    inner = (ka + kb) * (vb - va)
    rate, slope = coefs_beside
    v_beside = beside(v)
    drop = jnp.where((lane > 0) & (lane < 2 * LANES - 1), v_beside - v, 0.0)
    outer = (k + (rate + slope * v_beside)) * drop
    return outer + jnp.concatenate([inner, -inner], axis=1)


def coarse_y(v, k, _):
    lane = iota(v.shape, 1)
    from_last = jnp.where(lane > 0, pltpu.roll(v, 1, 1) - v, 0.0)
    from_next = jnp.where(lane < LANES - 1, pltpu.roll(v, LANES - 1, 1) - v, 0.0)
    last = (k + pltpu.roll(k, 1, 1)) * from_last
    return last + (k + pltpu.roll(k, LANES - 1, 1)) * from_next


def outer_mask(core):
    tile, tiles = lax.axis_index("tile"), lax.axis_size("tile")
    at_edge = jnp.where(core == 1, tile == 0, tile == tiles - 1)
    return jnp.where(at_edge, 0.0, 1.0).astype(jnp.float32)


def look_up(table_ref, zone):
    zone = zone.astype(jnp.int32)
    halves_of = (zone[:, :LANES], zone[:, LANES:])
    tables = [jnp.broadcast_to(table_ref[k : k + 1, :], halves_of[0].shape) for k in range(3)]
    plane, thick, soft = (
        jnp.concatenate([pick(t, z) for z in halves_of], axis=1) for t in tables
    )
    return [plane, plane * soft, thick, thick * soft, soft]


def flux_row(head_ref, i):
    return head_ref[HALO + i // 8, i % 8 : i % 8 + 1, :]


def to_source(flux, layers):
    return jnp.where(iota((layers, flux.shape[1]), 0) == 0, flux, 0.0)


def to_coarse(coarse_ref, at, rows):
    sums = []
    for coefs, v, flux in rows:
        sums.append([halves(x) for x in (coefs[0], coefs[2], coefs[4], v, flux)])
    first, second = sums
    for k in range(4):
        coarse_ref[k, at] = 0.125 * pair_sum(first[k] + second[k])
    pair = iota(coarse_ref.shape[2:], 0) < 2
    coarse_ref[4, at] = jnp.where(pair, 0.5 * (first[4] + second[4]), 0.0)


def fine_step(rows, state, load_coef, source, mask):
    v_next = state[rows[0] - 1]
    k_next = load_coef(0, rows[0] - 1) + load_coef(1, rows[0] - 1) * v_next
    high = None
    fresh = {}
    for j in (rows[0] - 1, *rows):
        v, k_plane, low = v_next, k_next, high
        v_next = state[j + 1]
        k_next = load_coef(0, j + 1) + load_coef(1, j + 1) * v_next
        high = (k_plane + k_next) * (v_next - v)
        if j == HALO - 1:
            high = high * mask
        if j >= rows[0]:
            k_thick = load_coef(2, j) + load_coef(3, j) * v
            near = [load_coef(k, j) for k in (4, 5)]
            fresh[j] = step_row(v, low, high, k_plane, k_thick, source(j), fine_y, 1, near)
    return fresh


def interior_kernel(
    own_ref,
    own_tail,
    other_ref,
    other_tail,
    row_hbm,
    plane_hbm,
    thick_hbm,
    soft_hbm,
    edge_ref,
    coef_out,
    coarse_ref,
    table_ref,
    v_ref,
    coef_ref,
    row_ref,
    plane_ref,
    thick_ref,
    soft_ref,
    sems,
):
    parameters = (row_ref, plane_ref, thick_ref, soft_ref)
    for copy in start_copies((row_hbm, plane_hbm, thick_hbm, soft_hbm), parameters, sems):
        copy.wait()
    fill_tables(table_ref, *parameters)
    width, layers = v_ref.shape[:2]
    core = lax.axis_index("layer")

    first = core == 0

    def gather():
        rows = []
        for i in range(width):
            a, b = (
                head[i] if i < HALO else tail[i - HALO]
                for head, tail in ((own_ref, own_tail), (other_ref, other_tail))
            )
            v, zone = join_layers(jnp.where(first, a, b), jnp.where(first, b, a))
            coefs = look_up(table_ref, zone)
            v_ref[i] = v
            for k, coef in enumerate((*coefs[:4], beside(coefs[0]), beside(coefs[1]))):
                coef_ref[k, i] = coef
                if i < coef_out.shape[1]:
                    coef_out[k, i] = coef
            rows.append((coefs, v, flux_row(own_ref, i)))
            if i % 2:
                to_coarse(coarse_ref, i // 2, rows)
                rows = []

    gather()
    state = {HALO + i: v_ref[i] for i in range(width)}
    for level in range(FINE_STEPS):
        if level:
            state = fine_step(
                range(HALO + level, HALO + width - level),
                state,
                lambda k, j: coef_ref[k, j - HALO],
                lambda j: to_source(flux_row(own_ref, j - HALO), layers),
                None,
            )
        for i in range(2):
            edge_ref[level, i] = state[HALO + level + i]


def edge_kernel(
    recv_ref,
    recv_other,
    own_ref,
    table_ref,
    edge_ref,
    own_coef,
    rest_ref,
    share_ref,
    coarse_ref,
    v_ref,
    coef_ref,
    source_ref,
):
    layers = v_ref.shape[1]
    half = v_ref.shape[0] - HALO
    core = lax.axis_index("layer")
    mask = outer_mask(core)

    first = core == 0

    def gather():
        rows = []
        for j in range(HALO):
            i = HALO - 1 - j
            a, b = recv_ref[i], recv_other[i]
            v, zone = join_layers(jnp.where(first, b, a), jnp.where(first, a, b))
            coefs = look_up(table_ref, zone)
            v_ref[j] = v
            for k, coef in enumerate((*coefs[:4], beside(coefs[0]), beside(coefs[1]))):
                coef_ref[k, j] = coef
            rows.append((coefs, v, flux_row(recv_ref, i)))
            if j % 2:
                if j >= HALO - EDGE:
                    to_coarse(coarse_ref, (j - (HALO - EDGE)) // 2, rows)
                rows = []

    gather()

    for j in range(HALO + FINE_STEPS):
        flux = flux_row(own_ref, j - HALO) if j >= HALO else flux_row(recv_ref, HALO - 1 - j)
        source_ref[j] = to_source(flux, layers)
    source = lambda j: source_ref[j]

    state = {j: v_ref[j] for j in range(HALO)}
    for step in range(1, FINE_STEPS + 1):
        for i in range(2):
            state[HALO + step - 1 + i] = edge_ref[step - 1, i]
        state = fine_step(
            range(step, HALO + step),
            state,
            lambda k, j: own_coef[k, j - HALO] if j >= HALO else coef_ref[k, j],
            source,
            mask,
        )

    for i in range(half):
        share_ref[2 * i] = state[HALO + i][:, :LANES]
        share_ref[2 * i + 1] = state[HALO + i][:, LANES:]
    for k in range(5):
        for i in range(COARSE_STEPS):
            share_ref[2 * half + k * COARSE_STEPS + i] = coarse_ref[k, i]
    even = iota((layers, LANES), 0) % 2 == 0
    restricted = []
    for j in range(HALO - EDGE, HALO + half, 2):
        restricted.append(0.125 * pair_sum(halves(state[j]) + halves(state[j + 1])))
    for i in range(0, len(restricted), 2):
        rest_ref[i // 2] = jnp.where(even, restricted[i], restricted[i + 1])


def coarse_fields(coarse_ref, outer_ref, other_ref):
    own = coarse_ref.shape[1]

    def row(k, j):
        if j < COARSE_STEPS:
            return outer_ref[k, j]
        if j < COARSE_STEPS + own:
            return coarse_ref[k, j - COARSE_STEPS]
        return other_ref[2 * own + k * COARSE_STEPS + own + 2 * COARSE_STEPS - 1 - j]

    return row


def coarse_propagate(state, field, masks):
    count = len(state)
    flux = {j: field(4, j) for j in range(1, count - 1)}
    plane = [field(0, j) for j in range(count)]
    thick = [field(1, j) for j in range(count)]
    plane_slope = [field(2, j) * plane[j] for j in range(count)]
    thick_slope = [field(2, j) * thick[j] for j in range(count)]
    for step in range(1, COARSE_STEPS + 1):
        k_plane = {
            j: plane[j] + plane_slope[j] * state[j] for j in range(step - 1, count - step + 1)
        }
        flows = {}
        for j in range(step - 1, count - step):
            flow = (k_plane[j] + k_plane[j + 1]) * (state[j + 1] - state[j])
            flows[j] = flow * masks[j] if j in masks else flow
        fresh = list(state)
        for j in range(step, count - step):
            k_thick = thick[j] + thick_slope[j] * state[j]
            fresh[j] = step_row(
                state[j], flows[j - 1], flows[j], k_plane[j], k_thick, flux[j], coarse_y, 2
            )
        state = fresh
    return state[COARSE_STEPS : count - COARSE_STEPS]


def edge_factors(rows):
    core = lax.axis_index("layer")
    return {
        COARSE_STEPS - 1: outer_mask(core),
        rows - COARSE_STEPS - 1: outer_mask(1 - core),
    }


def expand(slab):
    layers = slab.shape[0]
    even = iota(slab.shape, 0) % 2 == 0
    return [
        jnp.where(even, slab, pltpu.roll(slab, 1, 0)),
        jnp.where(even, pltpu.roll(slab, layers - 1, 0), slab),
    ]


def read_state(state_ref, rows):
    if state_ref.shape[0] == rows:
        return [state_ref[j] for j in range(rows)]
    count = state_ref.shape[0] // 2
    mine, other = (
        sum((expand(state_ref[i]) for i in range(at, at + count)), []) for at in (0, count)
    )
    return mine + other[::-1]


def unfold_kernel(halves_ref, state_ref):
    for j, row in enumerate(read_state(halves_ref, state_ref.shape[0])):
        state_ref[j] = row


def propagated(refs, state_ref=None):
    field = coarse_fields(*refs)
    rows = refs[0].shape[1] + 2 * COARSE_STEPS
    state = [field(3, j) for j in range(rows)]
    if state_ref is not None:
        first = lax.axis_index("tm") == 0
        state = [jnp.where(first, a, b) for a, b in zip(state, read_state(state_ref, rows))]
    return coarse_propagate(state, field, edge_factors(rows))


def base_kernel(coarse_ref, outer_ref, share_ref, other_ref, base_ref):
    depth, width = base_ref.shape[:2]
    core = lax.axis_index("layer")
    base = propagated((coarse_ref, outer_ref, other_ref))

    def write(mirror):
        for j in range(0, width, 2):
            slabs = []
            for i in (j, j + 1):
                ref, at = (share_ref, i) if i < width // 2 else (other_ref, width - 1 - i)
                slab = jnp.concatenate(
                    [ref[2 * at] - base[j // 2], ref[2 * at + 1] - base[j // 2]], axis=1
                )
                slabs.append(slab[:depth] if mirror else slab[depth:])
            both = join_lanes(jnp.concatenate(slabs, axis=0))
            for i in (0, 1):
                row = width - 1 - (j + i) if mirror else j + i
                base_ref[:, row, :] = both[depth * i : depth * (i + 1)]

    pl.when(core == 0)(lambda: write(True))
    pl.when(core == 1)(lambda: write(False))


def output_kernel(state_ref, coarse_ref, outer_ref, other_ref, base_ref, out_ref):
    depth, width = base_ref.shape[:2]
    core = lax.axis_index("layer")
    moved = propagated((coarse_ref, outer_ref, other_ref), state_ref)
    half = iota(moved[0].shape, 1) // 2

    def write(mirror):
        for j, row in enumerate(moved):
            gain = jnp.concatenate([pick(row, half), pick(row, half + LANES // 2)], axis=1)
            gain = gain[:depth] if mirror else gain[depth:]
            for i in (2 * j, 2 * j + 1):
                at = width - 1 - i if mirror else i
                out_ref[0, :, at, :] = base_ref[:, at, :] + gain

    pl.when(core == 0)(lambda: write(True))
    pl.when(core == 1)(lambda: write(False))


def advance_kernel(state_ref, coarse_ref, outer_ref, share_ref, other_ref, next_ref):
    own = next_ref.shape[0]
    refs = (coarse_ref, outer_ref, other_ref)
    moved, base = propagated(refs, state_ref), propagated(refs)
    for j in range(own):
        pair = []
        for i in (2 * j, 2 * j + 1):
            ref, at = (share_ref, i) if i < own else (other_ref, 2 * own - 1 - i)
            pair.append(ref[2 * at] + ref[2 * at + 1])
        next_ref[j] = moved[j] - base[j] + 0.125 * pair_sum(pair[0] + pair[1])


def layer_swap(value):
    return lax.ppermute(value, "layer", [(0, 1), (1, 0)])


def swap_pairs(pairs):
    return [edge for a, b in pairs for edge in ((a, b), (b, a))]


def tile_swap(value):
    tiles, slices = lax.axis_size("tile"), lax.axis_size("tm")
    at = lambda tile, time, core: (tile * slices + time) * 2 + core
    pairs = [
        (at(t, m, 1), at(t - 1, m, 0)) for t in range(1, tiles) for m in range(slices)
    ]
    for m in range(0, slices - 1, 2):
        pairs.append((at(0, m, 1), at(0, m + 1, 1)))
        pairs.append((at(tiles - 1, m, 0), at(tiles - 1, m + 1, 0)))
    return lax.ppermute(value, ("tile", "tm", "layer"), swap_pairs(pairs))


def time_swap(value, parity):
    slices = lax.axis_size("tm")
    at = lambda time, core: time * 2 + core
    pairs = [
        (at(m, c), at(m + 1, c)) for m in range(parity, slices - 1, 2) for c in range(2)
    ]
    used = {d for pair in pairs for d in pair}
    pairs += [(at(m, 0), at(m, 1)) for m in range(slices) if at(m, 0) not in used]
    return lax.ppermute(value, ("tm", "layer"), swap_pairs(pairs))


def cross_swap(value):
    slices = lax.axis_size("tm")
    pairs = [(m * 2 + c, m * 2 + 3 - c) for m in range(0, slices - 1, 2) for c in range(2)]
    return lax.ppermute(value, ("tm", "layer"), swap_pairs(pairs))


def on_device(u_start, flux, zone_of_cell, zone_row, plane_rate, thick_rate, soften):
    depth, width, length = zone_of_cell.shape
    layers = depth * lax.axis_size("layer")
    half = width // 2
    f32 = jnp.float32
    slabs = lambda *lead: jax.ShapeDtypeStruct((*lead, layers, LANES), f32)
    wide = lambda *lead: jax.ShapeDtypeStruct((*lead, layers, length), f32)

    def call(kernel, out_shape, *operands, name, scratch=(), in_hbm=()):
        spaces = [pltpu.HBM if k in in_hbm else pltpu.VMEM for k in range(len(operands))]
        operands = [
            pltpu.with_memory_space_constraint(x, space) if space is pltpu.HBM else x
            for x, space in zip(operands, spaces)
        ]
        return pl.pallas_call(
            kernel,
            out_shape=out_shape,
            in_specs=[pl.BlockSpec(memory_space=space) for space in spaces],
            out_specs=jax.tree.map(lambda _: VMEM, out_shape),
            scratch_shapes=scratch,
            compiler_params=pltpu.CompilerParams(vmem_limit_bytes=VMEM_BYTES),
            name=name,
        )(*operands)

    u_own = u_start[0]
    own, own_tail, turned, turned_tail = call(
        pack_kernel,
        (wide(HALO + width // 8), wide(width - HALO), wide(HALO), wide(width - HALO)),
        *(u_own, zone_of_cell, flux[0]),
        name="pack",
        scratch=[
            pltpu.VMEM(u_own.shape, f32),
            pltpu.VMEM(zone_of_cell.shape, jnp.int32),
            pltpu.VMEM(flux.shape[1:], f32),
            pltpu.SemaphoreType.DMA((2 * (width // 8) + 1,)),
        ],
        in_hbm=range(3),
    )
    other, other_tail = layer_swap(turned), layer_swap(turned_tail)
    recv, recv_other = tile_swap(own), tile_swap(other)

    levels, own_coef, coarse, tables = call(
        interior_kernel,
        (
            wide(FINE_STEPS, 2),
            wide(6, FINE_STEPS + 1),
            slabs(5, half),
            jax.ShapeDtypeStruct((3, LANES), f32),
        ),
        *(own, own_tail, other, other_tail, zone_row, plane_rate, thick_rate, soften),
        name="interior",
        scratch=[
            pltpu.VMEM((width, layers, length), f32),
            pltpu.VMEM((6, width, layers, length), f32),
            pltpu.SMEM(zone_row.shape, jnp.int32),
            *[pltpu.SMEM(plane_rate.shape, f32)] * 3,
            pltpu.SemaphoreType.DMA((4,)),
        ],
        in_hbm=range(4, 8),
    )
    rest, share, outer = call(
        edge_kernel,
        (
            slabs((half + EDGE) // 4),
            slabs(2 * half + 5 * COARSE_STEPS),
            slabs(5, COARSE_STEPS),
        ),
        *(recv, recv_other, own, tables, levels, own_coef),
        name="edge",
        scratch=[
            pltpu.VMEM((HALO + half, layers, length), f32),
            pltpu.VMEM((6, HALO, layers, length), f32),
            pltpu.VMEM((HALO + FINE_STEPS, layers, length), f32),
        ],
    )

    slices = lax.axis_size("tm")
    position = lax.axis_index("tm")
    other_rest, other_share = layer_swap(rest), layer_swap(share)
    state = cross_swap(jnp.concatenate([other_rest, rest], axis=0))
    base = call(
        base_kernel,
        jax.ShapeDtypeStruct((depth, width, length), f32),
        *(coarse, outer, share, other_share),
        name="base",
    )
    if slices > 2:
        full = slabs(half + 2 * COARSE_STEPS)
        state = call(unfold_kernel, full, state, name="unfold")
    for turn in range(1, slices - 1):
        ended = call(
            advance_kernel,
            slabs(half),
            *(state, coarse, outer, share, other_share),
            name="advance",
        )
        low = tile_swap(ended[:COARSE_STEPS])
        high = layer_swap(low)
        arrived = time_swap(jnp.concatenate([low[::-1], ended, high], axis=0), turn % 2)
        state = jnp.where(position == turn + 1, arrived, state)
    return call(
        output_kernel,
        jax.ShapeDtypeStruct((1, depth, width, length), f32),
        *(state, coarse, outer, other_share, base),
        name="output",
    )


def solution(mesh):
    return jax.shard_map(
        on_device,
        mesh=mesh,
        in_specs=(
            P(("parts", "tm"), "layer", "tile", None),
            P(("parts", "tm"), "tile", None),
            P("layer", "tile", None),
            P(),
            P(),
            P(),
            P(),
        ),
        out_specs=P(("parts", "tm"), "layer", "tile", None),
        check_vma=False,
    )
```

```python
import jax
import jax.numpy as jnp
from jax import lax
from jax.experimental import pallas as pl
from jax.experimental.pallas import tpu as pltpu
from jax.sharding import PartitionSpec as P

FINE_STEPS = 8
COARSE_STEPS = 2
LANES = 128
EDGE = 2 * COARSE_STEPS
HALO = FINE_STEPS + EDGE
VMEM_BYTES = 16 * 2**20
VMEM = pl.BlockSpec(memory_space=pltpu.VMEM)


def iota(shape, dim):
    return lax.broadcasted_iota(jnp.int32, shape, dim)


def pick(table, index):
    return jnp.take_along_axis(table, index, axis=1, mode="promise_in_bounds")


def split_lanes(row):
    rows = row.shape[0]
    lane = iota((rows, LANES), 1)
    low = lane < LANES // 2
    even = (2 * lane) % LANES
    first, second = row[:, :LANES], row[:, LANES:]
    return jnp.concatenate(
        [
            jnp.where(low, pick(first, even), pick(second, even)),
            jnp.where(low, pick(first, even + 1), pick(second, even + 1)),
        ],
        axis=1,
    )


def join_lanes(row):
    rows = row.shape[0]
    lane = iota((rows, LANES), 1)
    is_even = lane % 2 == 0
    half = lane // 2
    even, odd = row[:, :LANES], row[:, LANES:]
    return jnp.concatenate(
        [
            jnp.where(is_even, pick(even, half), pick(odd, half)),
            jnp.where(is_even, pick(even, half + LANES // 2), pick(odd, half + LANES // 2)),
        ],
        axis=1,
    )


def pack_kernel(
    u_hbm, zone_hbm, flux_hbm, head_ref, tail_ref, turned_head, turned_tail, u_ref, zone_ref, flux_ref, sems
):
    width = u_ref.shape[1]
    parts = [
        (source.at[:, pl.ds(row, 8)], target.at[:, pl.ds(row, 8)])
        for row in range(0, width, 8)
        for source, target in ((u_hbm, u_ref), (zone_hbm, zone_ref))
    ]
    copies = start_copies(*zip(*parts, (flux_hbm, flux_ref)), sems)

    def fill(mirror):
        for i in range(width):
            row = width - 1 - i if mirror else i
            if i % 8 == 0:
                for copy in copies[row // 8 * 2 : row // 8 * 2 + 2]:
                    copy.wait()
            slab = jnp.concatenate(
                [u_ref[:, row, :], zone_ref[:, row, :].astype(jnp.float32)], axis=0
            )
            slab = split_lanes(slab)
            at = width - 1 - i
            if at < HALO:
                turned_head[at] = slab
            else:
                turned_tail[at - HALO] = slab
            if i < HALO:
                head_ref[i] = slab
            else:
                tail_ref[i - HALO] = slab
        copies[-1].wait()
        flux = split_lanes(flux_ref[...])
        for i in range(width):
            row = width - 1 - i if mirror else i
            head_ref[HALO + i // 8, i % 8 : i % 8 + 1, :] = flux[row : row + 1]

    core = lax.axis_index("layer")
    pl.when(core == 0)(lambda: fill(True))
    pl.when(core == 1)(lambda: fill(False))


def start_copies(sources, targets, sems):
    copies = [
        pltpu.make_async_copy(source, target, sems.at[k])
        for k, (source, target) in enumerate(zip(sources, targets))
    ]
    for copy in copies:
        copy.start()
    return copies


def fill_tables(table_ref, row_ref, plane_ref, thick_ref, soft_ref):
    lane = iota((1, LANES), 1)
    tables = [jnp.zeros((1, LANES), jnp.float32)] * 3
    for zone in range(row_ref.shape[0]):
        at = row_ref[zone]
        values = (0.5 * plane_ref[at], 0.5 * thick_ref[at], soft_ref[at])
        tables = [jnp.where(lane == zone, x, t) for x, t in zip(values, tables)]
    for k in range(3):
        table_ref[k : k + 1] = tables[k]


def join_layers(low, high):
    depth = low.shape[0] // 2
    return (
        jnp.concatenate([low[:depth], high[:depth]], axis=0),
        jnp.concatenate([low[depth:], high[depth:]], axis=0),
    )


def pair_sum(value):
    layers = value.shape[0]
    even = iota(value.shape, 0) % 2 == 0
    return value + jnp.where(even, pltpu.roll(value, layers - 1, 0), pltpu.roll(value, 1, 0))


def halves(value):
    return value[:, :LANES] + value[:, LANES:]


def step_row(v, low, high, k_plane, k_thick, source, y_gain, layer_gap, coefs_beside=None):
    layers = v.shape[0]
    layer = iota(v.shape, 0)
    up, down = layers - layer_gap, layer_gap
    flow = (k_thick + pltpu.roll(k_thick, up, 0)) * (pltpu.roll(v, up, 0) - v)
    flow = jnp.where(layer < layers - layer_gap, flow, 0.0)
    z_gain = flow - pltpu.roll(flow, down, 0)
    return ((v + source) + (high - low)) + (z_gain + y_gain(v, k_plane, coefs_beside))


def beside(row):
    even, odd = row[:, :LANES], row[:, LANES:]
    return jnp.concatenate([pltpu.roll(odd, 1, 1), pltpu.roll(even, LANES - 1, 1)], axis=1)


def fine_y(v, k, coefs_beside):
    va, vb, ka, kb = v[:, :LANES], v[:, LANES:], k[:, :LANES], k[:, LANES:]
    lane = iota(v.shape, 1)
    inner = (ka + kb) * (vb - va)
    rate, slope = coefs_beside
    v_beside = beside(v)
    drop = jnp.where((lane > 0) & (lane < 2 * LANES - 1), v_beside - v, 0.0)
    outer = (k + (rate + slope * v_beside)) * drop
    return outer + jnp.concatenate([inner, -inner], axis=1)


def coarse_y(v, k, _):
    lane = iota(v.shape, 1)
    from_last = jnp.where(lane > 0, pltpu.roll(v, 1, 1) - v, 0.0)
    from_next = jnp.where(lane < LANES - 1, pltpu.roll(v, LANES - 1, 1) - v, 0.0)
    last = (k + pltpu.roll(k, 1, 1)) * from_last
    return last + (k + pltpu.roll(k, LANES - 1, 1)) * from_next


def outer_mask(core):
    tile, tiles = lax.axis_index("tile"), lax.axis_size("tile")
    at_edge = jnp.where(core == 1, tile == 0, tile == tiles - 1)
    return jnp.where(at_edge, 0.0, 1.0).astype(jnp.float32)


def look_up(table_ref, zone):
    zone = zone.astype(jnp.int32)
    halves_of = (zone[:, :LANES], zone[:, LANES:])
    tables = [jnp.broadcast_to(table_ref[k : k + 1, :], halves_of[0].shape) for k in range(3)]
    plane, thick, soft = (
        jnp.concatenate([pick(t, z) for z in halves_of], axis=1) for t in tables
    )
    return [plane, plane * soft, thick, thick * soft, soft]


def flux_row(head_ref, i):
    return head_ref[HALO + i // 8, i % 8 : i % 8 + 1, :]


def to_source(flux, layers):
    return jnp.where(iota((layers, flux.shape[1]), 0) == 0, flux, 0.0)


def to_coarse(coarse_ref, at, rows):
    sums = []
    for coefs, v, flux in rows:
        sums.append([halves(x) for x in (coefs[0], coefs[2], coefs[4], v, flux)])
    first, second = sums
    for k in range(4):
        coarse_ref[k, at] = 0.125 * pair_sum(first[k] + second[k])
    pair = iota(coarse_ref.shape[2:], 0) < 2
    coarse_ref[4, at] = jnp.where(pair, 0.5 * (first[4] + second[4]), 0.0)


def fine_step(rows, state, load_coef, source, mask):
    v_next = state[rows[0] - 1]
    k_next = load_coef(0, rows[0] - 1) + load_coef(1, rows[0] - 1) * v_next
    high = None
    fresh = {}
    for j in (rows[0] - 1, *rows):
        v, k_plane, low = v_next, k_next, high
        v_next = state[j + 1]
        k_next = load_coef(0, j + 1) + load_coef(1, j + 1) * v_next
        high = (k_plane + k_next) * (v_next - v)
        if j == HALO - 1:
            high = high * mask
        if j >= rows[0]:
            k_thick = load_coef(2, j) + load_coef(3, j) * v
            near = [load_coef(k, j) for k in (4, 5)]
            fresh[j] = step_row(v, low, high, k_plane, k_thick, source(j), fine_y, 1, near)
    return fresh


def interior_kernel(
    own_ref,
    own_tail,
    other_ref,
    other_tail,
    row_hbm,
    plane_hbm,
    thick_hbm,
    soft_hbm,
    edge_ref,
    coef_out,
    coarse_ref,
    table_ref,
    v_ref,
    coef_ref,
    row_ref,
    plane_ref,
    thick_ref,
    soft_ref,
    sems,
):
    parameters = (row_ref, plane_ref, thick_ref, soft_ref)
    for copy in start_copies((row_hbm, plane_hbm, thick_hbm, soft_hbm), parameters, sems):
        copy.wait()
    fill_tables(table_ref, *parameters)
    width, layers = v_ref.shape[:2]
    core = lax.axis_index("layer")

    first = core == 0

    def gather():
        rows = []
        for i in range(width):
            a, b = (
                head[i] if i < HALO else tail[i - HALO]
                for head, tail in ((own_ref, own_tail), (other_ref, other_tail))
            )
            v, zone = join_layers(jnp.where(first, a, b), jnp.where(first, b, a))
            coefs = look_up(table_ref, zone)
            v_ref[i] = v
            for k, coef in enumerate((*coefs[:4], beside(coefs[0]), beside(coefs[1]))):
                coef_ref[k, i] = coef
                if i < coef_out.shape[1]:
                    coef_out[k, i] = coef
            rows.append((coefs, v, flux_row(own_ref, i)))
            if i % 2:
                to_coarse(coarse_ref, i // 2, rows)
                rows = []

    gather()
    state = {HALO + i: v_ref[i] for i in range(width)}
    for level in range(FINE_STEPS):
        if level:
            state = fine_step(
                range(HALO + level, HALO + width - level),
                state,
                lambda k, j: coef_ref[k, j - HALO],
                lambda j: to_source(flux_row(own_ref, j - HALO), layers),
                None,
            )
        for i in range(2):
            edge_ref[level, i] = state[HALO + level + i]


def edge_kernel(
    recv_ref,
    recv_other,
    own_ref,
    table_ref,
    edge_ref,
    own_coef,
    rest_ref,
    share_ref,
    coarse_ref,
    v_ref,
    coef_ref,
    source_ref,
):
    layers = v_ref.shape[1]
    half = v_ref.shape[0] - HALO
    core = lax.axis_index("layer")
    mask = outer_mask(core)

    first = core == 0

    def gather():
        rows = []
        for j in range(HALO):
            i = HALO - 1 - j
            a, b = recv_ref[i], recv_other[i]
            v, zone = join_layers(jnp.where(first, b, a), jnp.where(first, a, b))
            coefs = look_up(table_ref, zone)
            v_ref[j] = v
            for k, coef in enumerate((*coefs[:4], beside(coefs[0]), beside(coefs[1]))):
                coef_ref[k, j] = coef
            rows.append((coefs, v, flux_row(recv_ref, i)))
            if j % 2:
                if j >= HALO - EDGE:
                    to_coarse(coarse_ref, (j - (HALO - EDGE)) // 2, rows)
                rows = []

    gather()

    for j in range(HALO + FINE_STEPS):
        flux = flux_row(own_ref, j - HALO) if j >= HALO else flux_row(recv_ref, HALO - 1 - j)
        source_ref[j] = to_source(flux, layers)
    source = lambda j: source_ref[j]

    state = {j: v_ref[j] for j in range(HALO)}
    for step in range(1, FINE_STEPS + 1):
        for i in range(2):
            state[HALO + step - 1 + i] = edge_ref[step - 1, i]
        state = fine_step(
            range(step, HALO + step),
            state,
            lambda k, j: own_coef[k, j - HALO] if j >= HALO else coef_ref[k, j],
            source,
            mask,
        )

    for i in range(half):
        share_ref[2 * i] = state[HALO + i][:, :LANES]
        share_ref[2 * i + 1] = state[HALO + i][:, LANES:]
    for k in range(5):
        for i in range(COARSE_STEPS):
            share_ref[2 * half + k * COARSE_STEPS + i] = coarse_ref[k, i]
    even = iota((layers, LANES), 0) % 2 == 0
    restricted = []
    for j in range(HALO - EDGE, HALO + half, 2):
        restricted.append(0.125 * pair_sum(halves(state[j]) + halves(state[j + 1])))
    for i in range(0, len(restricted), 2):
        rest_ref[i // 2] = jnp.where(even, restricted[i], restricted[i + 1])


def coarse_fields(coarse_ref, outer_ref, other_ref):
    own = coarse_ref.shape[1]

    def row(k, j):
        if j < COARSE_STEPS:
            return outer_ref[k, j]
        if j < COARSE_STEPS + own:
            return coarse_ref[k, j - COARSE_STEPS]
        return other_ref[2 * own + k * COARSE_STEPS + own + 2 * COARSE_STEPS - 1 - j]

    return row


def coarse_propagate(state, field, masks):
    count = len(state)
    flux = {j: field(4, j) for j in range(1, count - 1)}
    plane = [field(0, j) for j in range(count)]
    thick = [field(1, j) for j in range(count)]
    plane_slope = [field(2, j) * plane[j] for j in range(count)]
    thick_slope = [field(2, j) * thick[j] for j in range(count)]
    for step in range(1, COARSE_STEPS + 1):
        k_plane = {
            j: plane[j] + plane_slope[j] * state[j] for j in range(step - 1, count - step + 1)
        }
        flows = {}
        for j in range(step - 1, count - step):
            flow = (k_plane[j] + k_plane[j + 1]) * (state[j + 1] - state[j])
            flows[j] = flow * masks[j] if j in masks else flow
        fresh = list(state)
        for j in range(step, count - step):
            k_thick = thick[j] + thick_slope[j] * state[j]
            fresh[j] = step_row(
                state[j], flows[j - 1], flows[j], k_plane[j], k_thick, flux[j], coarse_y, 2
            )
        state = fresh
    return state[COARSE_STEPS : count - COARSE_STEPS]


def edge_factors(rows):
    core = lax.axis_index("layer")
    return {
        COARSE_STEPS - 1: outer_mask(core),
        rows - COARSE_STEPS - 1: outer_mask(1 - core),
    }


def expand(slab):
    layers = slab.shape[0]
    even = iota(slab.shape, 0) % 2 == 0
    return [
        jnp.where(even, slab, pltpu.roll(slab, 1, 0)),
        jnp.where(even, pltpu.roll(slab, layers - 1, 0), slab),
    ]


def read_state(state_ref, rows):
    if state_ref.shape[0] == rows:
        return [state_ref[j] for j in range(rows)]
    count = state_ref.shape[0] // 2
    mine, other = (
        sum((expand(state_ref[i]) for i in range(at, at + count)), []) for at in (0, count)
    )
    return mine + other[::-1]


def unfold_kernel(halves_ref, state_ref):
    for j, row in enumerate(read_state(halves_ref, state_ref.shape[0])):
        state_ref[j] = row


def propagated(refs, state_ref=None):
    field = coarse_fields(*refs)
    rows = refs[0].shape[1] + 2 * COARSE_STEPS
    state = [field(3, j) for j in range(rows)]
    if state_ref is not None:
        first = lax.axis_index("tm") == 0
        state = [jnp.where(first, a, b) for a, b in zip(state, read_state(state_ref, rows))]
    return coarse_propagate(state, field, edge_factors(rows))


def base_kernel(coarse_ref, outer_ref, share_ref, other_ref, base_ref):
    depth, width = base_ref.shape[:2]
    core = lax.axis_index("layer")
    base = propagated((coarse_ref, outer_ref, other_ref))

    def write(mirror):
        for j in range(0, width, 2):
            slabs = []
            for i in (j, j + 1):
                ref, at = (share_ref, i) if i < width // 2 else (other_ref, width - 1 - i)
                slab = jnp.concatenate(
                    [ref[2 * at] - base[j // 2], ref[2 * at + 1] - base[j // 2]], axis=1
                )
                slabs.append(slab[:depth] if mirror else slab[depth:])
            both = join_lanes(jnp.concatenate(slabs, axis=0))
            for i in (0, 1):
                row = width - 1 - (j + i) if mirror else j + i
                base_ref[:, row, :] = both[depth * i : depth * (i + 1)]

    pl.when(core == 0)(lambda: write(True))
    pl.when(core == 1)(lambda: write(False))


def output_kernel(state_ref, coarse_ref, outer_ref, other_ref, base_ref, out_ref):
    depth, width = base_ref.shape[:2]
    core = lax.axis_index("layer")
    moved = propagated((coarse_ref, outer_ref, other_ref), state_ref)
    half = iota(moved[0].shape, 1) // 2

    def write(mirror):
        for j, row in enumerate(moved):
            gain = jnp.concatenate([pick(row, half), pick(row, half + LANES // 2)], axis=1)
            gain = gain[:depth] if mirror else gain[depth:]
            for i in (2 * j, 2 * j + 1):
                at = width - 1 - i if mirror else i
                out_ref[0, :, at, :] = base_ref[:, at, :] + gain

    pl.when(core == 0)(lambda: write(True))
    pl.when(core == 1)(lambda: write(False))


def advance_kernel(state_ref, coarse_ref, outer_ref, share_ref, other_ref, next_ref):
    own = next_ref.shape[0]
    refs = (coarse_ref, outer_ref, other_ref)
    moved, base = propagated(refs, state_ref), propagated(refs)
    for j in range(own):
        pair = []
        for i in (2 * j, 2 * j + 1):
            ref, at = (share_ref, i) if i < own else (other_ref, 2 * own - 1 - i)
            pair.append(ref[2 * at] + ref[2 * at + 1])
        next_ref[j] = moved[j] - base[j] + 0.125 * pair_sum(pair[0] + pair[1])


def layer_swap(value):
    return lax.ppermute(value, "layer", [(0, 1), (1, 0)])


def swap_pairs(pairs):
    return [edge for a, b in pairs for edge in ((a, b), (b, a))]


def tile_swap(value):
    tiles, slices = lax.axis_size("tile"), lax.axis_size("tm")
    at = lambda tile, time, core: (tile * slices + time) * 2 + core
    pairs = [
        (at(t, m, 1), at(t - 1, m, 0)) for t in range(1, tiles) for m in range(slices)
    ]
    for m in range(0, slices - 1, 2):
        pairs.append((at(0, m, 1), at(0, m + 1, 1)))
        pairs.append((at(tiles - 1, m, 0), at(tiles - 1, m + 1, 0)))
    return lax.ppermute(value, ("tile", "tm", "layer"), swap_pairs(pairs))


def time_swap(value, parity):
    slices = lax.axis_size("tm")
    at = lambda time, core: time * 2 + core
    pairs = [
        (at(m, c), at(m + 1, c)) for m in range(parity, slices - 1, 2) for c in range(2)
    ]
    used = {d for pair in pairs for d in pair}
    pairs += [(at(m, 0), at(m, 1)) for m in range(slices) if at(m, 0) not in used]
    return lax.ppermute(value, ("tm", "layer"), swap_pairs(pairs))


def cross_swap(value):
    slices = lax.axis_size("tm")
    pairs = [(m * 2 + c, m * 2 + 3 - c) for m in range(0, slices - 1, 2) for c in range(2)]
    return lax.ppermute(value, ("tm", "layer"), swap_pairs(pairs))


def on_device(u_start, flux, zone_of_cell, zone_row, plane_rate, thick_rate, soften):
    depth, width, length = zone_of_cell.shape
    layers = depth * lax.axis_size("layer")
    half = width // 2
    f32 = jnp.float32
    slabs = lambda *lead: jax.ShapeDtypeStruct((*lead, layers, LANES), f32)
    wide = lambda *lead: jax.ShapeDtypeStruct((*lead, layers, length), f32)

    def call(kernel, out_shape, *operands, name, scratch=(), in_hbm=()):
        spaces = [pltpu.HBM if k in in_hbm else pltpu.VMEM for k in range(len(operands))]
        operands = [
            pltpu.with_memory_space_constraint(x, space) if space is pltpu.HBM else x
            for x, space in zip(operands, spaces)
        ]
        return pl.pallas_call(
            kernel,
            out_shape=out_shape,
            in_specs=[pl.BlockSpec(memory_space=space) for space in spaces],
            out_specs=jax.tree.map(lambda _: VMEM, out_shape),
            scratch_shapes=scratch,
            compiler_params=pltpu.CompilerParams(vmem_limit_bytes=VMEM_BYTES),
            name=name,
        )(*operands)

    u_own = u_start[0]
    own, own_tail, turned, turned_tail = call(
        pack_kernel,
        (wide(HALO + width // 8), wide(width - HALO), wide(HALO), wide(width - HALO)),
        *(u_own, zone_of_cell, flux[0]),
        name="pack",
        scratch=[
            pltpu.VMEM(u_own.shape, f32),
            pltpu.VMEM(zone_of_cell.shape, jnp.int32),
            pltpu.VMEM(flux.shape[1:], f32),
            pltpu.SemaphoreType.DMA((2 * (width // 8) + 1,)),
        ],
        in_hbm=range(3),
    )
    other, other_tail = layer_swap(turned), layer_swap(turned_tail)
    recv, recv_other = tile_swap(own), tile_swap(other)

    levels, own_coef, coarse, tables = call(
        interior_kernel,
        (
            wide(FINE_STEPS, 2),
            wide(6, FINE_STEPS + 1),
            slabs(5, half),
            jax.ShapeDtypeStruct((3, LANES), f32),
        ),
        *(own, own_tail, other, other_tail, zone_row, plane_rate, thick_rate, soften),
        name="interior",
        scratch=[
            pltpu.VMEM((width, layers, length), f32),
            pltpu.VMEM((6, width, layers, length), f32),
            pltpu.SMEM(zone_row.shape, jnp.int32),
            *[pltpu.SMEM(plane_rate.shape, f32)] * 3,
            pltpu.SemaphoreType.DMA((4,)),
        ],
        in_hbm=range(4, 8),
    )
    rest, share, outer = call(
        edge_kernel,
        (
            slabs((half + EDGE) // 4),
            slabs(2 * half + 5 * COARSE_STEPS),
            slabs(5, COARSE_STEPS),
        ),
        *(recv, recv_other, own, tables, levels, own_coef),
        name="edge",
        scratch=[
            pltpu.VMEM((HALO + half, layers, length), f32),
            pltpu.VMEM((6, HALO, layers, length), f32),
            pltpu.VMEM((HALO + FINE_STEPS, layers, length), f32),
        ],
    )

    slices = lax.axis_size("tm")
    position = lax.axis_index("tm")
    other_rest, other_share = layer_swap(rest), layer_swap(share)
    state = cross_swap(jnp.concatenate([other_rest, rest], axis=0))
    base = call(
        base_kernel,
        jax.ShapeDtypeStruct((depth, width, length), f32),
        *(coarse, outer, share, other_share),
        name="base",
    )
    if slices > 2:
        full = slabs(half + 2 * COARSE_STEPS)
        state = call(unfold_kernel, full, state, name="unfold")
    for turn in range(1, slices - 1):
        ended = call(
            advance_kernel,
            slabs(half),
            *(state, coarse, outer, share, other_share),
            name="advance",
        )
        low = tile_swap(ended[:COARSE_STEPS])
        high = layer_swap(low)
        arrived = time_swap(jnp.concatenate([low[::-1], ended, high], axis=0), turn % 2)
        state = jnp.where(position == turn + 1, arrived, state)
    return call(
        output_kernel,
        jax.ShapeDtypeStruct((1, depth, width, length), f32),
        *(state, coarse, outer, other_share, base),
        name="output",
    )


def solution(mesh):
    return jax.shard_map(
        on_device,
        mesh=mesh,
        in_specs=(
            P(("parts", "tm"), "layer", "tile", None),
            P(("parts", "tm"), "tile", None),
            P("layer", "tile", None),
            P(),
            P(),
            P(),
            P(),
        ),
        out_specs=P(("parts", "tm"), "layer", "tile", None),
        check_vma=False,
    )
```
